128 devices in a mesh: clip: 8 (over x, y_lo), fsdp: 16 (over y_hi, z, core).
Axes of the slice: x: 4, y: 4 (y_hi: 2, y_lo: 2; y = y_hi * 2 + y_lo), z: 4, core: 2. Of those that a mesh axis runs over, the one named last changes fastest.
Arguments:
- sample: bfloat16 [16384, 5120], P('clip', 'fsdp'), may hold values from -150 to 150
- noise: bfloat16 [16384, 5120], P('clip', 'fsdp'), may hold values from -6 to 6
- gen_branch: bfloat16 [16384, 5120], P('clip', 'fsdp'), may hold values from -6 to 6
- step: int32 [8], P('clip'), may hold values from 20 to 979
- teacher_mod: float32 [8, 2, 5120], P('clip'), may hold values from -3 to 3
- fake_mod: float32 [8, 2, 5120], P('clip'), may hold values from -3 to 3
- teacher_weight: bfloat16 [5120, 5120], P('clip', 'fsdp'), may hold values from -0.078125 to 0.078125
- fake_weight: bfloat16 [5120, 5120], P('clip', 'fsdp'), may hold values from -0.078125 to 0.078125
- gen_gate: float32 [8, 5120], P('clip', 'fsdp'), may hold values from -4 to 4
Outputs:
- branch_cot: bfloat16 [16384, 5120], P('clip', 'fsdp')
- gate_grad: float32 [8, 5120], P('clip', 'fsdp')
- fake_grad: float32 [5120, 5120], P('clip', 'fsdp')
The draws below stay inside these ranges and needn't reach their ends.
All inputs are finite; a program needn't handle non-finite values. Where the reference program divides by a largest or mean magnitude, that divisor is 1e-20 or more.
Results may differ from the reference program's by a relative error of at most 0.017.
Values may be sent and summed in bfloat16 or wider, within the bound.
A program may use at most 128 MiB of HBM per device.

```python
import math
import jax
import jax.numpy as jnp
from jax import lax

D = 5120
CLIP_TOK = 2048
CLIPS = 8
TOKENS = 16384


def draw_sample(key, part):
    key = jax.random.fold_in(key, 11)
    first, second, third = jax.random.split(key, 3)
    row_scale = jnp.exp(jax.random.uniform(first, (TOKENS, 1), jnp.float32, math.log(0.5), math.log(5.0)))
    ramp = jnp.arange(D, dtype=jnp.float32) / D
    rough = jnp.exp(jax.random.uniform(second, (1, D), jnp.float32, -0.35, 0.35))
    col_scale = 0.5 * jnp.exp(math.log(10.0) * ramp)[None, :] * rough
    base = jnp.clip(jax.random.normal(third, (TOKENS, D), jnp.float32), -4.0, 4.0)
    values = base * row_scale * col_scale
    return values.astype(jnp.bfloat16)


def set_ends(entries, own_key, least, top_value):
    shape = entries.shape
    spot = [jax.random.randint(jax.random.fold_in(own_key, axis), (), 0, shape[axis]) for axis in range(len(shape))]
    entries = entries.at[tuple(spot)].set(least)
    longest = shape.index(max(shape))
    spot[longest] = (spot[longest] + 1) % shape[longest]
    return entries.at[tuple(spot)].set(top_value)


def block_levels(key, extent, pieces, low, largest):
    def one(dim, blocks):
        heights = jax.random.uniform(jax.random.fold_in(jax.random.fold_in(key, 6), dim), (blocks,), jnp.float32, low / len(pieces), largest / len(pieces))
        return jnp.repeat(jnp.exp(heights), extent[dim] // blocks).reshape((-1,) + (1,) * (len(extent) - dim - 1))

    level = one(*pieces[0])
    for cut in pieces[1:]:
        level = level * one(*cut)
    return level


def gaussian(key, extent, scale, most, cuts=(), kind=jnp.bfloat16):
    values = scale * jax.random.normal(key, extent, jnp.float32)
    if cuts:
        values = values * block_levels(key, extent, cuts, -0.22, 0.18)
    return jnp.clip(values, -most, most).astype(kind)


def setup_inputs(seed: int = 0) -> dict:
    streams_of = jax.random.split(jax.random.key(seed), 10)
    return {
        "sample": draw_sample(jax.random.fold_in(streams_of[9], 71), 0),
        "noise": gaussian(streams_of[1], (TOKENS, D), 1.0, 6.0, ((0, 8), (1, 16))),
        "gen_branch": gaussian(streams_of[2], (TOKENS, D), 1.0, 6.0, ((0, 8), (1, 16))),
        "step": set_ends(jax.random.randint(streams_of[3], (CLIPS,), 20, 980), jax.random.fold_in(streams_of[3], 1), 20, 979).astype(jnp.int32),
        "teacher_mod": gaussian(streams_of[4], (CLIPS, 2, D), 0.5, 3.0, ((0, 8),), jnp.float32),
        "fake_mod": gaussian(streams_of[5], (CLIPS, 2, D), 0.5, 3.0, ((0, 8),), jnp.float32),
        "teacher_weight": gaussian(streams_of[6], (D, D), D ** -0.5, 0.078125, ((0, 8), (1, 16))),
        "fake_weight": gaussian(streams_of[7], (D, D), D ** -0.5, 0.078125, ((0, 8), (1, 16))),
        "gen_gate": gaussian(streams_of[8], (CLIPS, D), 1.0, 4.0, ((0, 8), (1, 16)), jnp.float32),
    }


EPS = 1e-06

def reference(sample, noise, gen_branch, step, teacher_mod, fake_mod, teacher_weight, fake_weight, gen_gate):
    shaped = (CLIPS, CLIP_TOK, D)
    items = (sample.reshape(shaped), noise.reshape(shaped), gen_branch.reshape(shaped), step, teacher_mod, fake_mod, gen_gate)

    def one_clip(total, item):
        smp, nse, brn, stp, tmod, fmod, gate = item
        frac = stp.astype(jnp.float32) / 1000.0
        sigma = 5.0 * frac / (1.0 + 4.0 * frac)
        smp32 = smp.astype(jnp.float32)
        nse32 = nse.astype(jnp.float32)
        noised = ((1.0 - sigma) * smp32 + sigma * nse32).astype(jnp.bfloat16)
        noised32 = noised.astype(jnp.float32)
        center = lax.optimization_barrier(jnp.mean(noised32, axis=1, keepdims=True))
        spread = noised32 - center
        power = lax.optimization_barrier(jnp.mean(spread * spread, axis=1, keepdims=True))
        normed = (spread * lax.rsqrt(power + EPS)).astype(jnp.bfloat16)
        normed32 = normed.astype(jnp.float32)
        teacher_in = (normed32 * (1.0 + tmod[1]) + tmod[0]).astype(jnp.bfloat16)
        fake_in = (normed32 * (1.0 + fmod[1]) + fmod[0]).astype(jnp.bfloat16)
        teacher_velocity = jnp.dot(teacher_in, teacher_weight, preferred_element_type=jnp.float32)
        fake_velocity = jnp.dot(fake_in, fake_weight, preferred_element_type=jnp.float32)
        target = nse32 - smp32
        teacher_estimate = noised32 - sigma * teacher_velocity
        fake_estimate = noised32 - sigma * fake_velocity
        gap = jnp.mean(jnp.abs(smp32 - teacher_estimate))
        push = (fake_estimate - teacher_estimate) / (gap + EPS)
        branch_cot = (gate * push).astype(jnp.bfloat16)
        gate_grad = lax.optimization_barrier(jnp.sum(push * brn.astype(jnp.float32), axis=0)) / math.sqrt(CLIP_TOK)
        velocity_error = ((fake_velocity - target) / math.sqrt(TOKENS)).astype(jnp.bfloat16)
        term = jnp.dot(fake_in.T, velocity_error, preferred_element_type=jnp.float32)
        return (total + term, (branch_cot, gate_grad))
    fake_grad, outputs = lax.scan(one_clip, jnp.zeros((D, D), jnp.float32), items)
    branch_cot, gate_grad = outputs
    return (branch_cot.reshape(TOKENS, D), gate_grad, fake_grad)
```

```python
import functools
import math

import jax
import jax.numpy as jnp
from jax import lax
from jax.experimental import pallas as pl
from jax.experimental.pallas import tpu as pltpu
from jax.sharding import PartitionSpec as P

EPS = 1e-06
F32 = jnp.float32
BF16 = jnp.bfloat16
NT = (((1,), (1,)), ((), ()))

TOK = 2048
FB = 320
CB = 640
CLIPS = 8
COPIES = 64


def eye(n, dtype):
    same = lax.broadcasted_iota(jnp.int32, (n, n), 0) == lax.broadcasted_iota(jnp.int32, (n, n), 1)
    return same.astype(F32).astype(dtype)


def transposed(x):
    return lax.dot_general(eye(x.shape[1], BF16), x, NT, preferred_element_type=F32)


def kernel(
    sample, noise, gen, step, tmod, fmod, tw, fw, gate,
    bc_out, gg_out, fg_out,
    at, wt, acc, xs, ws, sT, nT, gT, vv, st1, st2, piv, mr, cs, bw, sv, sb, col,
    gopp, gnb, gy, gown, ropp, rnb, ry, fg, gap_s, gap_r,
    send_sems, recv_sems, loc_sems,
):
    clip = lax.axis_index("clip")
    fs = lax.axis_index("fsdp")
    x, l = clip // 2, clip % 2
    p, z, yh = fs % 2, (fs // 2) % 4, fs // 8
    s = 1 - 2 * p
    zu, zd, zo = (z + s + 4) % 4, (z - s + 4) % 4, (z + 2) % 4
    yo = 1 - yh
    xr, xl, xo = (x + 1) % 4, (x + 3) % 4, (x + 2) % 4

    def q(y, zz):
        return y * 4 + zz

    def on_f(y, zz, pp):
        return {"fsdp": (y * 4 + zz) * 2 + pp}

    def on_c(xx, ll):
        return {"clip": xx * 2 + ll}

    up, dn, across, sib = on_f(yh, zu, p), on_f(yh, zd, p), on_f(yo, z, p), on_f(yh, z, 1 - p)
    right, left, pair = on_c(xr, l), on_c(xl, l), on_c(x, 1 - l)
    me, u, d, o = q(yh, z), q(yh, zu), q(yh, zd), q(yh, zo)
    y_me, y_u, y_d, y_o = q(yo, z), q(yo, zu), q(yo, zd), q(yo, zo)

    table = {}

    def copy(name, src, dst, to):
        i = len(table)
        assert i < COPIES
        c = pltpu.make_async_remote_copy(
            src_ref=src, dst_ref=dst, send_sem=send_sems.at[i], recv_sem=recv_sems.at[i],
            device_id=to, device_id_type=pl.DeviceIdType.MESH,
        )
        table[name] = [c, False]
        c.start()

    def got(*names):
        for name in names:
            table[name][0].wait_recv()

    def sent(*names):
        for name in names:
            if not table[name][1]:
                table[name][1] = True
                table[name][0].wait_send()

    part = {
        "a": (pl.multiple_of(p * 512, 128), 128),
        "b": (pl.multiple_of(128 + p * 256, 128), 128),
        "c": (pl.multiple_of(256 + p * 64, 64), 64),
        "ab": (pl.multiple_of(p * 384, 128), 256),
        "all": (pl.multiple_of(p * 320, 64), 320),
    }

    def send(name, block, which, to):
        ref = at.at[block, pl.ds(*part[which]), :]
        copy(name, ref, ref, to)

    def send_w(name, block, half, to):
        ref = wt.at[block, pl.ds(half * FB, FB), :]
        copy(name, ref, ref, to)

    loads = []
    for i, (src, dst) in enumerate(
        [(sample, xs.at[0]), (noise, xs.at[1]), (fw, ws.at[0]), (tw, ws.at[1]), (gen, xs.at[2])]
    ):
        loads.append(pltpu.make_async_copy(src, dst, loc_sems.at[i]))
        loads[-1].start()
    barrier = pltpu.get_barrier_semaphore()
    for to in (up, dn, across, sib, right, left, pair):
        pl.semaphore_signal(barrier, inc=1, device_id=to, device_id_type=pl.DeviceIdType.MESH)

    frac = jnp.full((8, 128), step[0], jnp.int32).astype(F32) / 1000.0
    sigma = (5.0 * frac / (1.0 + 4.0 * frac))[0:1, 0:1]

    loads[0].wait()
    loads[1].wait()

    @pl.loop(0, 8)
    def _(i):
        rows = pl.ds(pl.multiple_of(i * 256, 256), 256)
        s32 = xs[0, rows, :].astype(F32)
        n32 = xs[1, rows, :].astype(F32)
        noised = ((1.0 - sigma) * s32 + sigma * n32).astype(BF16)
        at[me, pl.ds(*part["all"]), rows] = transposed(noised).astype(BF16)

    pl.semaphore_wait(barrier, 7)
    send("up_a", me, "a", up)
    send("dn_b", me, "b", dn)
    send("up_c", me, "c", up)
    send("dn_a", me, "a", dn)
    send("y_own", me, "all", across)
    send("s_own", me, "all", sib)

    loads[2].wait()
    wt[clip, 0:FB, :] = transposed_w(ws, 0)
    send_w("xr_f", clip, 0, right)
    send_w("pair_f", clip, 0, pair)
    loads[3].wait()
    wt[clip, FB:CB, :] = transposed_w(ws, 1)
    send_w("xl_t", clip, 1, left)
    send_w("xr_t", clip, 1, right)
    send_w("xl_f", clip, 0, left)
    send_w("pair_t", clip, 1, pair)

    w_l, w_r, w_o = xl * 2 + l, xr * 2 + l, xo * 2 + l
    v_me, v_l, v_r, v_o = x * 2 + 1 - l, xl * 2 + 1 - l, xr * 2 + 1 - l, xo * 2 + 1 - l

    loads[4].wait()

    @pl.loop(0, 8)
    def _(i):
        rows = pl.ds(pl.multiple_of(i * 256, 256), 256)
        sT[:, rows] = transposed(xs[0, rows, :]).astype(BF16)
        nT[:, rows] = transposed(xs[1, rows, :]).astype(BF16)
        gT[:, rows] = transposed(xs[2, rows, :]).astype(BF16)
        own = at[me, pl.ds(*part["all"]), rows].astype(F32)
        piv[:, rows] = jnp.sum(own, axis=0, keepdims=True) * (1.0 / FB)
        st1[:, rows] = jnp.zeros((8, 256), F32)
        st2[:, rows] = jnp.zeros((8, 256), F32)
        acc[:, rows] = jnp.zeros((CB, 256), F32)

    cs[...] = jnp.zeros_like(cs)
    bw[...] = jnp.zeros_like(bw)
    sv[...] = jnp.zeros_like(sv)
    sb[...] = jnp.zeros_like(sb)

    def stats(block, first, rows):
        @pl.loop(0, 8)
        def _(i):
            cols = pl.ds(pl.multiple_of(i * 256, 256), 256)
            v = at[block, first : first + rows, cols].astype(F32) - piv[:, cols]
            v = v.reshape(rows // 8, 8, 256)
            st1[:, cols] += jnp.sum(v, axis=0)
            st2[:, cols] += jnp.sum(v * v, axis=0)

    def scale(block):
        for h, mod in ((0, fmod), (1, tmod)):
            lanes = pl.ds(pl.multiple_of(block * CB, 128), CB)
            factor = 1.0 + mod[1:2, lanes]
            shift = mod[0:1, lanes]

            @pl.loop(0, 5)
            def _(i):
                rows = pl.ds(pl.multiple_of(h * FB + i * 64, 64), 64)
                w = wt[block, rows, :].astype(F32)
                scaled = (w * factor).astype(BF16)
                wt[block, rows, :] = scaled
                back, moved = scaled.astype(F32), w * shift
                cs[rows, :] += sum(back[:, k : k + 128] for k in range(0, CB, 128))
                bw[rows, :] += sum(moved[:, k : k + 128] for k in range(0, CB, 128))

    def forward(block, first, rows, top=0, n=CB):
        @pl.loop(0, 4)
        def _(i):
            cols = pl.ds(pl.multiple_of(i * 512, 512), 512)
            acc[top : top + n, cols] += jnp.dot(
                wt[block, top : top + n, first : first + rows],
                at[block, first : first + rows, cols],
                preferred_element_type=F32,
            )

    got("xr_f")
    send_w("xr_of", w_l, 0, right)
    got("xl_t")
    send_w("xl_ot", w_r, 1, left)
    got("up_a")
    send("up_oa", d, "a", up)
    got("dn_b")
    send("dn_ob", u, "b", dn)
    send("dn_c", me, "c", dn)
    got("up_c")
    send("up_oc", d, "c", up)
    send("up_b", me, "b", up)
    got("pair_f")
    send_w("xr_vf", v_me, 0, right)
    got("pair_t")
    send_w("xl_vt", v_me, 1, left)
    send_w("xr_vt", v_me, 1, right)
    send_w("xl_vf", v_me, 0, left)
    got("s_own")
    stats(me, 0, CB)
    got("up_oa")
    send("y_oa", o, "a", across)
    got("y_own")
    send("up_yab", y_me, "ab", up)
    send("dn_yab", y_me, "ab", dn)
    send("up_yc", y_me, "c", up)
    send("dn_yc", y_me, "c", dn)
    send("s_y", y_me, "all", sib)
    got("dn_ob")
    send("y_ob", o, "b", across)
    got("up_oc")
    send("y_oc", o, "c", across)
    send("s_o", o, "all", sib)
    got("xr_t", "xl_f", "xr_of", "xl_ot")
    sent("xr_f", "xr_t", "xl_f", "xl_t", "pair_f", "pair_t", "xr_of", "xl_ot")
    for block in (clip, w_l, w_r, w_o):
        scale(block)
    got("xr_vf")
    send_w("xr_vof", v_l, 0, right)
    got("xl_vt")
    send_w("xl_vot", v_r, 1, left)
    got("s_y")
    stats(y_me, 0, CB)
    got("s_o")
    stats(o, 0, CB)
    got("dn_a", "dn_c")
    send("s_u", u, "all", sib)
    got("up_b")
    send("s_d", d, "all", sib)
    got("s_d")
    stats(u, 0, CB)
    got("s_u")
    stats(d, 0, CB)
    got("xr_vt", "xl_vf", "xr_vof", "xl_vot")
    sent("xr_vf", "xr_vt", "xl_vf", "xl_vt", "xr_vof", "xl_vot")
    for block in (v_me, v_l, v_r, v_o):
        scale(block)
    cs[...] = jnp.broadcast_to(jnp.sum(cs[...], axis=1, keepdims=True), cs.shape)
    bw[...] = jnp.broadcast_to(jnp.sum(bw[...], axis=1, keepdims=True), bw.shape)
    for block in (me, u, d, o, y_me):
        forward(block, 0, CB)
    got("y_oa", "y_ob", "y_oc")
    send("s_yo", y_o, "all", sib)
    got("dn_yab")
    send("s_yu", y_u, "ab", sib)
    got("up_yab")
    send("s_yd", y_d, "ab", sib)
    got("s_yo")
    stats(y_o, 0, CB)
    forward(y_o, 0, CB)
    got("s_yd", "s_yu")
    for block in (y_u, y_d):
        for first in (0, 384):
            stats(block, first, 256)
            forward(block, first, 256)
    got("dn_yc")
    send("s_yuc", y_u, "c", sib)
    got("up_yc")
    send("s_ydc", y_d, "c", sib)
    got("s_yuc", "s_ydc")
    for block in (y_u, y_d):
        stats(block, 256, 128)
        forward(block, 256, 128, 0, FB)

    shift = jnp.sum(st1[...], axis=0, keepdims=True) * (1.0 / (CLIPS * CB))
    power = jnp.sum(st2[...], axis=0, keepdims=True) * (1.0 / (CLIPS * CB))
    mr[0:1, :] = piv[...] + shift
    mr[1:2, :] = lax.rsqrt(jnp.maximum(power - shift * shift, 0.0) + EPS)

    @pl.loop(0, 40)
    def _(i):
        rows = pl.ds(pl.multiple_of((i // 8) * 64, 64), 64)
        cols = pl.ds(pl.multiple_of((i % 8) * 256, 256), 256)
        m, r = mr[0:1, cols], mr[1:2, cols]
        fv = r * (acc[rows, cols] - cs[rows, 0:1] * m) + bw[rows, 0:1]
        acc[rows, cols] = fv
        target = nT[rows, cols].astype(F32) - sT[rows, cols].astype(F32)
        err = (fv - target) * (1.0 / math.sqrt(CLIPS * TOK))
        v = (r * err).astype(BF16)
        vv[rows, cols] = v
        mv = m * v.astype(F32)
        sv[rows, :] += mv[:, :128] + mv[:, 128:]
        sb[rows, :] += err[:, :128] + err[:, 128:]

    sv[...] = jnp.broadcast_to(jnp.sum(sv[...], axis=1, keepdims=True), sv.shape)
    sb[...] = jnp.broadcast_to(jnp.sum(sb[...], axis=1, keepdims=True), sb.shape)

    def grad(block, dst):
        for first, n in ((0, 256), (256, 256), (512, 128)):
            lanes = pl.ds(pl.multiple_of(block * CB + first, 128), n)
            part_sum = lax.dot_general(
                vv[...], at[block, first : first + n, :], NT, preferred_element_type=F32
            )
            g = (part_sum - sv[:, 0:1]) * (1.0 + fmod[1:2, lanes]) + sb[:, 0:1] * fmod[0:1, lanes]
            dst[:, first : first + n] = g.astype(dst.dtype)

    HALF = FB // 2
    lo, hi = slice(0, HALF), slice(HALF, FB)
    ls = (1 - l, l)
    for j in (0, 1):
        grad(xo * 2 + ls[j], gopp.at[j])
        copy(f"or{j}", gopp.at[j, lo], ropp.at[0, j], right)
        copy(f"ol{j}", gopp.at[j, hi], ropp.at[1, j], left)
    for j in (0, 1):
        grad(xr * 2 + ls[j], gnb.at[0, j])
        copy(f"rr{j}", gnb.at[0, j, hi], rnb.at[0, j, hi], right)
        grad(xl * 2 + ls[j], gnb.at[1, j])
        copy(f"rl{j}", gnb.at[1, j, lo], rnb.at[1, j, lo], left)
        got(f"or{j}")
        gnb[0, j, lo] = (gnb[0, j, lo].astype(F32) + ropp[0, j].astype(F32)).astype(BF16)
        copy(f"sr{j}", gnb.at[0, j, lo], rnb.at[0, j, lo], right)
        got(f"ol{j}")
        gnb[1, j, hi] = (gnb[1, j, hi].astype(F32) + ropp[1, j].astype(F32)).astype(BF16)
        copy(f"sl{j}", gnb.at[1, j, hi], rnb.at[1, j, hi], left)
    for j in (0, 1):
        grad(x * 2 + ls[j], gown.at[j])

    for block in (y_u, y_d):
        forward(block, 256, 128, FB, FB)

    col[...] = jnp.zeros_like(col)

    @pl.loop(0, 40)
    def _(i):
        rows = pl.ds(pl.multiple_of((i // 8) * 64, 64), 64)
        more = pl.ds(pl.multiple_of(FB + (i // 8) * 64, 64), 64)
        own = pl.ds(pl.multiple_of(p * FB + (i // 8) * 64, 64), 64)
        cols = pl.ds(pl.multiple_of((i % 8) * 256, 256), 256)
        m, r = mr[0:1, cols], mr[1:2, cols]
        tv = r * (acc[more, cols] - cs[more, 0:1] * m) + bw[more, 0:1]
        diff = sigma * (tv - acc[rows, cols])
        acc[more, cols] = diff
        away = jnp.abs(
            sT[rows, cols].astype(F32) - (at[me, own, cols].astype(F32) - sigma * tv)
        )
        pushed = diff * gT[rows, cols].astype(F32)
        col[0, rows, :] += away[:, :128] + away[:, 128:]
        col[1, rows, :] += pushed[:, :128] + pushed[:, 128:]

    total = jnp.sum(jnp.sum(col[0], axis=0, keepdims=True), axis=1, keepdims=True)
    total = jnp.broadcast_to(total, (8, 128))
    for k, to in enumerate(
        (sib, on_f(yh, z + 1 - 2 * (z % 2), p), on_f(yh, 3 - z, p), across)
    ):
        gap_s[k] = total
        copy(f"gap{k}", gap_s.at[k], gap_r.at[k], to)
        got(f"gap{k}")
        total = total + gap_r[k]
    weight = 1.0 / (total[0:1, 0:1] * (1.0 / (TOK * CLIPS * CB)) + EPS)

    same = eye(FB, F32)
    gate_col = jnp.sum(same * gate[...], axis=1, keepdims=True) * weight
    col[0] = jnp.broadcast_to(gate_col, (FB, 128))
    gg_col = jnp.sum(col[1], axis=1, keepdims=True) * weight * (1.0 / math.sqrt(TOK))
    gg_out[...] = jnp.sum(same * gg_col, axis=0, keepdims=True)

    @pl.loop(0, 8)
    def _(i):
        rows = pl.ds(pl.multiple_of(i * 256, 256), 256)
        cot = (col[0, :, 0:1] * acc[FB:CB, rows]).astype(BF16)
        xs[0, rows, :] = lax.dot_general(
            eye(256, BF16), cot, NT, preferred_element_type=F32
        ).astype(BF16)

    out_bc = pltpu.make_async_copy(xs.at[0], bc_out, loc_sems.at[5])
    out_bc.start()

    got("rr0", "sr0", "rl0", "sl0")
    for k, rows in enumerate((lo, hi)):
        gy[rows] = (
            gown[0, rows] + rnb[0, 0, rows].astype(F32) + rnb[1, 0, rows].astype(F32)
        ).astype(BF16)
        copy(f"y{k}", gy.at[rows], ry.at[rows], pair)
    got("rr1", "sr1", "rl1", "sl1")
    gown[1] = gown[1] + rnb[0, 1].astype(F32) + rnb[1, 1].astype(F32)
    got("y0", "y1")
    for k in range(0, CB, 128):
        lanes = slice(k, k + 128)
        whole = gown[1, :, lanes] + ry[:, lanes].astype(F32)
        high = whole.astype(BF16)
        low = (whole - high.astype(F32)).astype(BF16)
        fg[lanes, :] = transposed(high) + transposed(low)
    out_fg = pltpu.make_async_copy(fg, fg_out, loc_sems.at[6])
    out_fg.start()
    sent(*table)
    out_bc.wait()
    out_fg.wait()


def transposed_w(ws, i):
    return transposed(ws[i]).astype(BF16)


def per_device(
    sample, noise, gen_branch, step, teacher_mod, fake_mod, teacher_weight, fake_weight, gen_gate
):
    hbm = pl.BlockSpec(memory_space=pl.ANY)
    vmem = pl.BlockSpec(memory_space=pltpu.VMEM)
    return pl.pallas_call(
        kernel,
        out_shape=(
            jax.ShapeDtypeStruct((TOK, FB), BF16),
            jax.ShapeDtypeStruct((1, FB), F32),
            jax.ShapeDtypeStruct((CB, FB), F32),
        ),
        in_specs=[
            hbm, hbm, hbm, pl.BlockSpec(memory_space=pltpu.SMEM), vmem, vmem, hbm, hbm, vmem,
        ],
        out_specs=(hbm, vmem, hbm),
        scratch_shapes=[
            pltpu.VMEM((CLIPS, CB, TOK), BF16),
            pltpu.VMEM((CLIPS, CB, CB), BF16),
            pltpu.VMEM((CB, TOK), F32),
            pltpu.VMEM((3, TOK, FB), BF16),
            pltpu.VMEM((2, CB, FB), BF16),
            pltpu.VMEM((FB, TOK), BF16),
            pltpu.VMEM((FB, TOK), BF16),
            pltpu.VMEM((FB, TOK), BF16),
            pltpu.VMEM((FB, TOK), BF16),
            pltpu.VMEM((8, TOK), F32),
            pltpu.VMEM((8, TOK), F32),
            pltpu.VMEM((1, TOK), F32),
            pltpu.VMEM((2, TOK), F32),
            pltpu.VMEM((CB, 128), F32),
            pltpu.VMEM((CB, 128), F32),
            pltpu.VMEM((FB, 128), F32),
            pltpu.VMEM((FB, 128), F32),
            pltpu.VMEM((2, FB, 128), F32),
            pltpu.VMEM((2, FB, CB), BF16),
            pltpu.VMEM((2, 2, FB, CB), BF16),
            pltpu.VMEM((FB, CB), BF16),
            pltpu.VMEM((2, FB, CB), F32),
            pltpu.VMEM((2, 2, FB // 2, CB), BF16),
            pltpu.VMEM((2, 2, FB, CB), BF16),
            pltpu.VMEM((FB, CB), BF16),
            pltpu.VMEM((CB, FB), F32),
            pltpu.VMEM((4, 8, 128), F32),
            pltpu.VMEM((4, 8, 128), F32),
            pltpu.SemaphoreType.DMA((COPIES,)),
            pltpu.SemaphoreType.DMA((COPIES,)),
            pltpu.SemaphoreType.DMA((8,)),
        ],
        compiler_params=pltpu.CompilerParams(
            collective_id=0, has_side_effects=True, vmem_limit_bytes=62 << 20
        ),
        name="step",
    )(
        sample, noise, gen_branch, step,
        teacher_mod.reshape(2, CLIPS * CB), fake_mod.reshape(2, CLIPS * CB),
        teacher_weight, fake_weight, gen_gate,
    )


def solution(mesh):
    placed = (
        P("clip", "fsdp"),
        P("clip", "fsdp"),
        P("clip", "fsdp"),
        P("clip"),
        P("clip", None, None),
        P("clip", None, None),
        P("clip", "fsdp"),
        P("clip", "fsdp"),
        P("clip", "fsdp"),
    )
    return jax.shard_map(
        per_device,
        mesh=mesh,
        in_specs=placed,
        out_specs=(P("clip", "fsdp"), P("clip", "fsdp"), P("clip", "fsdp")),
        check_vma=False,
    )
```

```python
import functools
import math

import jax
import jax.numpy as jnp
from jax import lax
from jax.experimental import pallas as pl
from jax.experimental.pallas import tpu as pltpu
from jax.sharding import PartitionSpec as P

EPS = 1e-06
F32 = jnp.float32
BF16 = jnp.bfloat16
NT = (((1,), (1,)), ((), ()))

TOK = 2048
FB = 320
CB = 640
CLIPS = 8
COPIES = 64


def eye(n):
    same = lax.broadcasted_iota(jnp.int32, (n, n), 0) == lax.broadcasted_iota(jnp.int32, (n, n), 1)
    return same.astype(F32)


def kernel(
    sample, noise, gen, step, tmod, fmod, tw, fw, gate,
    bc_out, gg_out, fg_out,
    at, wt, acc, sT, nT, gT, vv, bt, st1, st2, piv, mr, cs, bw, sv, sb, col,
    gopp, gnb, gy, gown, ropp, rnb, ry, gap_s, gap_r,
    send_sems, recv_sems, loc_sems,
):
    clip = lax.axis_index("clip")
    fs = lax.axis_index("fsdp")
    x, l = clip // 2, clip % 2
    p, z, yh = fs % 2, (fs // 2) % 4, fs // 8
    s = 1 - 2 * p
    zu, zd, zo = (z + s + 4) % 4, (z - s + 4) % 4, (z + 2) % 4
    yo = 1 - yh
    xr, xl, xo = (x + 1) % 4, (x + 3) % 4, (x + 2) % 4

    def on_f(y, zz, pp):
        return {"fsdp": (y * 4 + zz) * 2 + pp}

    def on_c(xx, ll):
        return {"clip": xx * 2 + ll}

    up, dn, across, sib = on_f(yh, zu, p), on_f(yh, zd, p), on_f(yo, z, p), on_f(yh, z, 1 - p)
    right, left, pair = on_c(xr, l), on_c(xl, l), on_c(x, 1 - l)
    me, y_me, o, u, d, y_o, y_u, y_d = range(8)

    def slot(block):
        rel = ((block % 4 - z) * s + 8) % 4
        r1, r2 = rel % 2, rel // 2
        yd = (block // 4 + yh) % 2
        return (1 - r1) * (yd + (2 + 2 * yd) * r2) + r1 * (3 + 3 * yd + r2)

    table = {}

    def copy(name, src, dst, to):
        i = len(table)
        assert i < COPIES
        c = pltpu.make_async_remote_copy(
            src_ref=src, dst_ref=dst, send_sem=send_sems.at[i], recv_sem=recv_sems.at[i],
            device_id=to, device_id_type=pl.DeviceIdType.MESH,
        )
        table[name] = [c, False]
        c.start()

    def got(*names):
        for name in names:
            table[name][0].wait_recv()

    def sent(*names):
        for name in names:
            if not table[name][1]:
                table[name][1] = True
                table[name][0].wait_send()

    part = {
        "a": (pl.multiple_of(p * 512, 128), 128),
        "b": (pl.multiple_of(128 + p * 256, 128), 128),
        "c": (pl.multiple_of(256 + p * 64, 64), 64),
        "ab": (pl.multiple_of(p * 384, 128), 256),
        "all": (pl.multiple_of(p * 320, 64), 320),
    }

    def span(block, which):
        first, n = part[which]
        return pl.ds(pl.multiple_of(block * CB + first, 64), n)

    def send(name, here, there, which, to):
        copy(name, at.at[span(here, which), :], at.at[span(there, which), :], to)

    def w_ref(block, half):
        lanes = pl.ds(pl.multiple_of(slot(block) * CB, 128), CB)
        return wt.at[pl.ds(half * FB, FB), lanes]

    def send_w(name, block, half, to):
        copy(name, w_ref(block, half), w_ref(block, half), to)

    loads = {}

    def load(name, src, dst):
        loads[name] = pltpu.make_async_copy(src, dst, loc_sems.at[len(loads)])
        loads[name].start()

    def local(which):
        first, n = part[which]
        return pl.ds(pl.multiple_of(first - p * FB, 64), n)

    for which in ("a", "b", "c"):
        load("s" + which, sample.at[local(which), :], sT.at[local(which), :])
        load("n" + which, noise.at[local(which), :], nT.at[local(which), :])
    load("fw", fw, w_ref(clip, 0))
    load("tw", tw, w_ref(clip, 1))
    load("gen", gen, gT)
    barrier = pltpu.get_barrier_semaphore()
    for to in (up, dn, across, sib, right, left, pair):
        pl.semaphore_signal(barrier, inc=1, device_id=to, device_id_type=pl.DeviceIdType.MESH)

    frac = jnp.full((8, 128), step[0], jnp.int32).astype(F32) / 1000.0
    sigma = (5.0 * frac / (1.0 + 4.0 * frac))[0:1, 0:1]

    def noised(which):
        loads["s" + which].wait()
        loads["n" + which].wait()
        first, n = part[which]
        own = pl.multiple_of(first - p * FB, 64)

        @pl.loop(0, n // 32)
        def _(i):
            rows = pl.ds(pl.multiple_of(own + i * 32, 32), 32)
            mixed = (1.0 - sigma) * sT[rows, :].astype(F32) + sigma * nT[rows, :].astype(F32)
            at[pl.ds(pl.multiple_of(first + i * 32, 32), 32), :] = mixed.astype(BF16)

    noised("a")
    pl.semaphore_wait(barrier, 7)
    send("up_a", me, d, "a", up)
    noised("b")
    send("dn_b", me, u, "b", dn)
    loads["fw"].wait()
    send_w("pair_f", clip, 0, pair)
    send("y_ab", me, y_me, "ab", across)
    send_w("xr_f", clip, 0, right)
    send_w("xl_f", clip, 0, left)
    noised("c")
    send("up_c", me, d, "c", up)
    send("dn_a", me, u, "a", dn)
    send("y_c", me, y_me, "c", across)
    send("s_own", me, me, "all", sib)
    loads["tw"].wait()
    send_w("xr_t", clip, 1, right)
    send_w("xl_t", clip, 1, left)
    send_w("pair_t", clip, 1, pair)

    w_l, w_r, w_o = xl * 2 + l, xr * 2 + l, xo * 2 + l
    v_me, v_l, v_r, v_o = x * 2 + 1 - l, xl * 2 + 1 - l, xr * 2 + 1 - l, xo * 2 + 1 - l
    everyone = (clip, w_l, w_r, w_o, v_me, v_l, v_r, v_o)

    @pl.loop(0, 8)
    def _(i):
        cols = pl.ds(pl.multiple_of(i * 256, 256), 256)
        own = at[pl.ds(*part["all"]), cols].astype(F32)
        piv[:, cols] = jnp.sum(own, axis=0, keepdims=True) * (1.0 / FB)
        st1[:, cols] = jnp.zeros((8, 256), F32)
        st2[:, cols] = jnp.zeros((8, 256), F32)

    cs[...] = jnp.zeros_like(cs)
    bw[...] = jnp.zeros_like(bw)
    sv[...] = jnp.zeros_like(sv)
    sb[...] = jnp.zeros_like(sb)
    col[...] = jnp.zeros_like(col)

    def add_stats(first, n, cols):
        v = at[first : first + n, cols].astype(F32) - piv[:, cols]
        v = v.reshape(n // 8, 8, 256)
        st1[:, cols] += jnp.sum(v, axis=0)
        st2[:, cols] += jnp.sum(v * v, axis=0)

    def stats(block, first, n):
        @pl.loop(0, 8)
        def _(i):
            add_stats(block * CB + first, n, pl.ds(pl.multiple_of(i * 256, 256), 256))

    def scale(block, h, mod):
        lanes = pl.ds(pl.multiple_of(block * CB, 128), CB)
        factor = 1.0 + mod[1:2, lanes]
        shift = mod[0:1, lanes]
        held = pl.ds(pl.multiple_of(slot(block) * CB, 128), CB)

        @pl.loop(0, 5)
        def _(i):
            rows = pl.ds(pl.multiple_of(h * FB + i * 64, 64), 64)
            w = wt[rows, held].astype(F32)
            scaled = (w * factor).astype(BF16)
            wt[rows, held] = scaled
            back, moved = scaled.astype(F32), w * shift
            cs[rows, :] += sum(back[:, k : k + 128] for k in range(0, CB, 128))
            bw[rows, :] += sum(moved[:, k : k + 128] for k in range(0, CB, 128))

    def scale_all(h, mod):
        for block in everyone:
            scale(block, h, mod)
        rows = slice(h * FB, h * FB + FB)
        for ref in (cs, bw):
            ref[rows] = jnp.broadcast_to(jnp.sum(ref[rows], axis=1, keepdims=True), (FB, 128))

    def product(top, spans, cols):
        left_side = [wt[top : top + FB, i : i + n] for i, n in spans]
        right_side = [at[i : i + n, cols] for i, n in spans]
        return jnp.dot(
            jnp.concatenate(left_side, axis=1) if len(spans) > 1 else left_side[0],
            jnp.concatenate(right_side, axis=0) if len(spans) > 1 else right_side[0],
            preferred_element_type=F32,
        )

    def forward(spans, fresh=False):
        @pl.loop(0, 8)
        def _(i):
            cols = pl.ds(pl.multiple_of(i * 256, 256), 256)
            if fresh:
                acc[0:FB, cols] = product(0, spans, cols)
            else:
                acc[0:FB, cols] += product(0, spans, cols)

    got("xr_f")
    send_w("xr_of", w_l, 0, right)
    got("pair_f")
    send_w("xr_vf", v_me, 0, right)
    send_w("xl_vf", v_me, 0, left)
    got("up_a")
    send("up_oa", d, o, "a", up)
    got("dn_b")
    send("dn_ob", u, o, "b", dn)
    send("dn_c", me, u, "c", dn)
    got("up_c")
    send("up_oc", d, o, "c", up)
    send("up_b", me, d, "b", up)
    got("s_own")
    stats(me, 0, CB)
    got("xl_vf")
    send_w("xl_vof", v_r, 0, left)
    got("xl_t")
    send_w("xl_ot", w_r, 1, left)
    got("y_ab")
    send("up_yab", y_me, y_d, "ab", up)
    send("dn_yab", y_me, y_u, "ab", dn)
    got("up_oa")
    send("y_oa", o, y_o, "a", across)
    got("dn_ob")
    send("y_ob", o, y_o, "b", across)
    got("up_oc")
    send("y_oc", o, y_o, "c", across)
    send("s_o", o, o, "all", sib)
    got("y_c")
    send("up_yc", y_me, y_d, "c", up)
    send("dn_yc", y_me, y_u, "c", dn)
    send("s_y", y_me, y_me, "all", sib)
    got("pair_t")
    send_w("xr_vt", v_me, 1, right)
    send_w("xl_vt", v_me, 1, left)
    got("xl_f", "xr_of", "xr_vf", "xl_vof")
    sent("xr_f", "xl_f", "pair_f", "xr_of", "xr_vf", "xl_vf", "xl_vof")
    scale_all(0, fmod)

    @pl.loop(0, 8)
    def _(i):
        cols = pl.ds(pl.multiple_of(i * 256, 256), 256)
        for k in range(0, FB, 64):
            rows = slice(k, k + 64)
            base = jnp.concatenate([bw[rows], bw[rows]], axis=1)
            target = nT[rows, cols].astype(F32) - sT[rows, cols].astype(F32)
            bt[rows, cols] = (base - target) * (1.0 / math.sqrt(CLIPS * TOK))

    got("s_o")
    stats(o, 0, CB)
    got("s_y")
    stats(y_me, 0, CB)
    forward([(0, 3 * CB)], fresh=True)
    got("xr_vt")
    send_w("xr_vot", v_l, 1, right)
    got("dn_a", "dn_c")
    send("s_u", u, d, "all", sib)
    got("up_b")
    send("s_d", d, u, "all", sib)
    got("s_d")
    stats(u, 0, CB)
    got("s_u")
    stats(d, 0, CB)
    forward([(3 * CB, 2 * CB)])
    got("y_oa", "y_ob")
    send("s_yo", y_o, y_o, "ab", sib)
    got("xr_t", "xl_ot", "xl_vt", "xr_vot")
    sent("xr_t", "xl_t", "pair_t", "xl_ot", "xr_vt", "xl_vt", "xr_vot")
    scale_all(1, tmod)
    got("dn_yab")
    send("s_yu", y_u, y_d, "ab", sib)
    got("up_yab")
    send("s_yd", y_d, y_u, "ab", sib)
    got("s_yo", "s_yd", "s_yu")
    spans = [(b * CB + k, 256) for b in (y_o, y_u, y_d) for k in (0, 384)]
    for first, n in spans:
        stats(0, first, n)
    forward(spans)
    got("dn_yc")
    send("s_yuc", y_u, y_d, "c", sib)
    got("up_yc")
    send("s_ydc", y_d, y_u, "c", sib)
    got("y_oc")
    send("s_yoc", y_o, y_o, "c", sib)
    got("s_yuc", "s_ydc", "s_yoc")

    last = [(b * CB + 256, 128) for b in (y_o, y_u, y_d)]

    @pl.loop(0, 8)
    def _(i):
        cols = pl.ds(pl.multiple_of(i * 256, 256), 256)
        acc[0:FB, cols] += product(0, last, cols)
        for first, n in last:
            add_stats(first, n, cols)
        shift = jnp.sum(st1[:, cols], axis=0, keepdims=True) * (1.0 / (CLIPS * CB))
        power = jnp.sum(st2[:, cols], axis=0, keepdims=True) * (1.0 / (CLIPS * CB))
        mr[0:1, cols] = piv[:, cols] + shift
        mr[1:2, cols] = lax.rsqrt(jnp.maximum(power - shift * shift, 0.0) + EPS)
        m, r = mr[0:1, cols], mr[1:2, cols]
        small = r * (1.0 / math.sqrt(CLIPS * TOK))
        for k in range(0, FB, 64):
            rows = slice(k, k + 64)
            sums = jnp.concatenate([cs[rows], cs[rows]], axis=1)
            err = small * (acc[rows, cols] - sums * m) + bt[rows, cols]
            v = (r * err).astype(BF16)
            vv[rows, cols] = v
            mv = m * v.astype(F32)
            sv[rows, :] += mv[:, :128] + mv[:, 128:]
            sb[rows, :] += err[:, :128] + err[:, 128:]

    sv[...] = jnp.broadcast_to(jnp.sum(sv[...], axis=1, keepdims=True), sv.shape)
    sb[...] = jnp.broadcast_to(jnp.sum(sb[...], axis=1, keepdims=True), sb.shape)

    def grad(block, dst):
        held = slot(block) * CB
        for first, n in ((0, 256), (256, 256), (512, 128)):
            lanes = pl.ds(pl.multiple_of(block * CB + first, 128), n)
            rows = pl.ds(pl.multiple_of(held + first, 128), n)
            part_sum = lax.dot_general(vv[...], at[rows, :], NT, preferred_element_type=F32)
            g = (part_sum - sv[:, 0:1]) * (1.0 + fmod[1:2, lanes]) + sb[:, 0:1] * fmod[0:1, lanes]
            dst[:, first : first + n] = g.astype(dst.dtype)

    HALF = FB // 2
    lo, hi = slice(0, HALF), slice(HALF, FB)
    ls = (1 - l, l)
    for j in (0, 1):
        grad(xo * 2 + ls[j], gopp.at[j])
        copy(f"or{j}", gopp.at[j, lo], ropp.at[0, j], right)
        copy(f"ol{j}", gopp.at[j, hi], ropp.at[1, j], left)
    for j in (0, 1):
        grad(xr * 2 + ls[j], gnb.at[0, j])
        copy(f"rr{j}", gnb.at[0, j, hi], rnb.at[0, j, hi], right)
        grad(xl * 2 + ls[j], gnb.at[1, j])
        copy(f"rl{j}", gnb.at[1, j, lo], rnb.at[1, j, lo], left)
        got(f"or{j}")
        gnb[0, j, lo] = (gnb[0, j, lo].astype(F32) + ropp[0, j].astype(F32)).astype(BF16)
        copy(f"sr{j}", gnb.at[0, j, lo], rnb.at[0, j, lo], right)
        got(f"ol{j}")
        gnb[1, j, hi] = (gnb[1, j, hi].astype(F32) + ropp[1, j].astype(F32)).astype(BF16)
        copy(f"sl{j}", gnb.at[1, j, hi], rnb.at[1, j, hi], left)
    for j in (0, 1):
        grad(x * 2 + ls[j], gown.at[j])

    loads["gen"].wait()

    @pl.loop(0, 8)
    def _(i):
        cols = pl.ds(pl.multiple_of(i * 256, 256), 256)
        acc[FB:CB, cols] = product(FB, [(0, CLIPS * CB)], cols)
        m, r = mr[0:1, cols], mr[1:2, cols]
        for k in range(0, FB, 64):
            rows, more = slice(k, k + 64), slice(FB + k, FB + k + 64)
            own = pl.ds(pl.multiple_of(p * FB + k, 64), 64)

            def twice(ref, where):
                return jnp.concatenate([ref[where], ref[where]], axis=1)

            fv = r * (acc[rows, cols] - twice(cs, rows) * m) + twice(bw, rows)
            tv = r * (acc[more, cols] - twice(cs, more) * m) + twice(bw, more)
            diff = sigma * (tv - fv)
            acc[more, cols] = diff
            away = jnp.abs(
                sT[rows, cols].astype(F32) - (at[own, cols].astype(F32) - sigma * tv)
            )
            pushed = diff * gT[rows, cols].astype(F32)
            col[0, rows, :] += away[:, :128] + away[:, 128:]
            col[1, rows, :] += pushed[:, :128] + pushed[:, 128:]

    total = jnp.sum(jnp.sum(col[0], axis=0, keepdims=True), axis=1, keepdims=True)
    total = jnp.broadcast_to(total, (8, 128))
    for k, to in enumerate(
        (sib, on_f(yh, z + 1 - 2 * (z % 2), p), on_f(yh, 3 - z, p), across)
    ):
        gap_s[k] = total
        copy(f"gap{k}", gap_s.at[k], gap_r.at[k], to)
        got(f"gap{k}")
        total = total + gap_r[k]
    weight = 1.0 / (total[0:1, 0:1] * (1.0 / (TOK * CLIPS * CB)) + EPS)

    same = eye(FB)
    gate_col = jnp.sum(same * gate[...], axis=1, keepdims=True) * weight
    col[0] = jnp.broadcast_to(gate_col, (FB, 128))
    gg_col = jnp.sum(col[1], axis=1, keepdims=True) * weight * (1.0 / math.sqrt(TOK))
    gg_out[...] = jnp.sum(same * gg_col, axis=0, keepdims=True)

    @pl.loop(0, 8)
    def _(i):
        rows = pl.ds(pl.multiple_of(i * 256, 256), 256)
        vv[:, rows] = (col[0, :, 0:1] * acc[FB:CB, rows]).astype(BF16)

    out_bc = pltpu.make_async_copy(vv, bc_out, loc_sems.at[10])
    out_bc.start()

    got("rr0", "sr0", "rl0", "sl0")
    for k, rows in enumerate((lo, hi)):
        gy[rows] = (
            gown[0, rows] + rnb[0, 0, rows].astype(F32) + rnb[1, 0, rows].astype(F32)
        ).astype(BF16)
        copy(f"y{k}", gy.at[rows], ry.at[rows], pair)
    got("rr1", "sr1", "rl1", "sl1")
    gown[1] = gown[1] + rnb[0, 1].astype(F32) + rnb[1, 1].astype(F32)
    got("y0", "y1")
    gown[1] += ry[...].astype(F32)
    out_fg = pltpu.make_async_copy(gown.at[1], fg_out, loc_sems.at[11])
    out_fg.start()
    sent(*table)
    out_bc.wait()
    out_fg.wait()


def per_device(
    sample, noise, gen_branch, step, teacher_mod, fake_mod, teacher_weight, fake_weight, gen_gate
):
    hbm = pl.BlockSpec(memory_space=pl.ANY)
    vmem = pl.BlockSpec(memory_space=pltpu.VMEM)
    cot, gate_grad, grad = pl.pallas_call(
        kernel,
        out_shape=(
            jax.ShapeDtypeStruct((FB, TOK), BF16),
            jax.ShapeDtypeStruct((1, FB), F32),
            jax.ShapeDtypeStruct((FB, CB), F32),
        ),
        in_specs=[
            hbm, hbm, hbm, pl.BlockSpec(memory_space=pltpu.SMEM), vmem, vmem, hbm, hbm, vmem,
        ],
        out_specs=(hbm, vmem, hbm),
        scratch_shapes=[
            pltpu.VMEM((CLIPS * CB, TOK), BF16),
            pltpu.VMEM((CB, CLIPS * CB), BF16),
            pltpu.VMEM((CB, TOK), F32),
            pltpu.VMEM((FB, TOK), BF16),
            pltpu.VMEM((FB, TOK), BF16),
            pltpu.VMEM((FB, TOK), BF16),
            pltpu.VMEM((FB, TOK), BF16),
            pltpu.VMEM((FB, TOK), F32),
            pltpu.VMEM((8, TOK), F32),
            pltpu.VMEM((8, TOK), F32),
            pltpu.VMEM((1, TOK), F32),
            pltpu.VMEM((2, TOK), F32),
            pltpu.VMEM((CB, 128), F32),
            pltpu.VMEM((CB, 128), F32),
            pltpu.VMEM((FB, 128), F32),
            pltpu.VMEM((FB, 128), F32),
            pltpu.VMEM((2, FB, 128), F32),
            pltpu.VMEM((2, FB, CB), BF16),
            pltpu.VMEM((2, 2, FB, CB), BF16),
            pltpu.VMEM((FB, CB), BF16),
            pltpu.VMEM((2, FB, CB), F32),
            pltpu.VMEM((2, 2, FB // 2, CB), BF16),
            pltpu.VMEM((2, 2, FB, CB), BF16),
            pltpu.VMEM((FB, CB), BF16),
            pltpu.VMEM((4, 8, 128), F32),
            pltpu.VMEM((4, 8, 128), F32),
            pltpu.SemaphoreType.DMA((COPIES,)),
            pltpu.SemaphoreType.DMA((COPIES,)),
            pltpu.SemaphoreType.DMA((12,)),
        ],
        compiler_params=pltpu.CompilerParams(
            collective_id=0, has_side_effects=True, vmem_limit_bytes=62 << 20
        ),
        name="step",
    )(
        sample.T, noise.T, gen_branch.T, step,
        teacher_mod.reshape(2, CLIPS * CB), fake_mod.reshape(2, CLIPS * CB),
        teacher_weight.T, fake_weight.T, gen_gate,
    )
    return cot.T, gate_grad, grad.T


def solution(mesh):
    placed = (
        P("clip", "fsdp"),
        P("clip", "fsdp"),
        P("clip", "fsdp"),
        P("clip"),
        P("clip", None, None),
        P("clip", None, None),
        P("clip", "fsdp"),
        P("clip", "fsdp"),
        P("clip", "fsdp"),
    )
    return jax.shard_map(
        per_device,
        mesh=mesh,
        in_specs=placed,
        out_specs=(P("clip", "fsdp"), P("clip", "fsdp"), P("clip", "fsdp")),
        check_vma=False,
    )
```

```python
import functools
import math

import jax
import jax.numpy as jnp
from jax import lax
from jax.experimental import pallas as pl
from jax.experimental.pallas import tpu as pltpu
from jax.sharding import PartitionSpec as P

EPS = 1e-06
F32 = jnp.float32
BF16 = jnp.bfloat16
NT = (((1,), (1,)), ((), ()))

TOK = 2048
FB = 320
CB = 640
CLIPS = 8
COPIES = 80


def eye(n):
    same = lax.broadcasted_iota(jnp.int32, (n, n), 0) == lax.broadcasted_iota(jnp.int32, (n, n), 1)
    return same.astype(F32)


def kernel(
    sample, noise, gen, step, tmod_in, fmod_in, tw, fw, gate_in,
    bc_out, gg_out, fg_out,
    at, wt, acc, sT, nT, gT, vv, bt, st1, st2, piv, mr, cs, bw, sv, sb, col,
    tmod, fmod, gate, g, gown, rpo, rpn, ryq, rqo, rqn, rpy, gap_s, gap_r,
    send_sems, recv_sems, loc_sems,
):
    clip = lax.axis_index("clip")
    fs = lax.axis_index("fsdp")
    x, l = clip // 2, clip % 2
    p, z, yh = fs % 2, (fs // 2) % 4, fs // 8
    s = 1 - 2 * p
    zu, zd, zo = (z + s + 4) % 4, (z - s + 4) % 4, (z + 2) % 4
    yo = 1 - yh
    xr, xl, xo = (x + 1) % 4, (x + 3) % 4, (x + 2) % 4

    def on_f(y, zz, pp):
        return {"fsdp": (y * 4 + zz) * 2 + pp}

    def on_c(xx, ll):
        return {"clip": xx * 2 + ll}

    up, dn, across, sib = on_f(yh, zu, p), on_f(yh, zd, p), on_f(yo, z, p), on_f(yh, z, 1 - p)
    right, left, pair = on_c(xr, l), on_c(xl, l), on_c(x, 1 - l)
    me, y_me, o, u, d, y_o, y_u, y_d = range(8)

    def slot(block):
        rel = ((block % 4 - z) * s + 8) % 4
        r1, r2 = rel % 2, rel // 2
        yd = (block // 4 + yh) % 2
        return (1 - r1) * (yd + (2 + 2 * yd) * r2) + r1 * (3 + 3 * yd + r2)

    table = {}

    def copy(name, src, dst, to):
        i = len(table)
        assert i < COPIES
        c = pltpu.make_async_remote_copy(
            src_ref=src, dst_ref=dst, send_sem=send_sems.at[i], recv_sem=recv_sems.at[i],
            device_id=to, device_id_type=pl.DeviceIdType.MESH,
        )
        table[name] = [c, False]
        c.start()

    def got(*names):
        for name in names:
            table[name][0].wait_recv()

    def sent(*names):
        for name in names:
            if not table[name][1]:
                table[name][1] = True
                table[name][0].wait_send()

    part = {
        "a": (pl.multiple_of(p * 512, 128), 128),
        "b": (pl.multiple_of(128 + p * 256, 128), 128),
        "c": (pl.multiple_of(256 + p * 64, 64), 64),
        "ab": (pl.multiple_of(p * 384, 128), 256),
        "all": (pl.multiple_of(p * 320, 64), 320),
    }

    def span(block, which):
        first, n = part[which]
        return pl.ds(pl.multiple_of(block * CB + first, 64), n)

    def send(name, here, there, which, to):
        copy(name, at.at[span(here, which), :], at.at[span(there, which), :], to)

    def w_ref(block, half):
        lanes = pl.ds(pl.multiple_of(slot(block) * CB, 128), CB)
        return wt.at[pl.ds(half * FB, FB), lanes]

    def send_w(name, block, half, to):
        copy(name, w_ref(block, half), w_ref(block, half), to)

    loads = {}

    def load(name, src, dst):
        loads[name] = pltpu.make_async_copy(src, dst, loc_sems.at[len(loads)])
        loads[name].start()

    def local(which):
        first, n = part[which]
        return pl.ds(pl.multiple_of(first - p * FB, 64), n)

    for which in ("a", "b", "c"):
        load("s" + which, sample.at[local(which), :], sT.at[local(which), :])
        load("n" + which, noise.at[local(which), :], nT.at[local(which), :])
    load("fw", fw, w_ref(clip, 0))
    load("tw", tw, w_ref(clip, 1))
    load("fmod", fmod_in, fmod)
    load("tmod", tmod_in, tmod)
    load("gen", gen, gT)
    load("gate", gate_in, gate)
    barrier = pltpu.get_barrier_semaphore()
    for to in (up, dn, across, sib, right, left, pair):
        pl.semaphore_signal(barrier, inc=1, device_id=to, device_id_type=pl.DeviceIdType.MESH)

    frac = jnp.full((8, 128), step[0], jnp.int32).astype(F32) / 1000.0
    sigma = (5.0 * frac / (1.0 + 4.0 * frac))[0:1, 0:1]

    def noised(which):
        loads["s" + which].wait()
        loads["n" + which].wait()
        first, n = part[which]
        own = pl.multiple_of(first - p * FB, 64)

        @pl.loop(0, n // 32)
        def _(i):
            rows = pl.ds(pl.multiple_of(own + i * 32, 32), 32)
            mixed = (1.0 - sigma) * sT[rows, :].astype(F32) + sigma * nT[rows, :].astype(F32)
            at[pl.ds(pl.multiple_of(first + i * 32, 32), 32), :] = mixed.astype(BF16)

    noised("a")
    pl.semaphore_wait(barrier, 7)
    send("up_a", me, d, "a", up)
    noised("b")
    send("dn_b", me, u, "b", dn)
    loads["fw"].wait()
    send_w("pair_f", clip, 0, pair)
    send("y_ab", me, y_me, "ab", across)
    send_w("xr_f", clip, 0, right)
    send_w("xl_f", clip, 0, left)
    noised("c")
    send("up_c", me, d, "c", up)
    send("dn_a", me, u, "a", dn)
    send("y_c", me, y_me, "c", across)
    send("s_own", me, me, "all", sib)
    loads["tw"].wait()
    send_w("xr_t", clip, 1, right)
    send_w("xl_t", clip, 1, left)
    send_w("pair_t", clip, 1, pair)

    w_l, w_r, w_o = xl * 2 + l, xr * 2 + l, xo * 2 + l
    v_me, v_l, v_r, v_o = x * 2 + 1 - l, xl * 2 + 1 - l, xr * 2 + 1 - l, xo * 2 + 1 - l
    everyone = (clip, w_l, w_r, w_o, v_me, v_l, v_r, v_o)

    @pl.loop(0, 8)
    def _(i):
        cols = pl.ds(pl.multiple_of(i * 256, 256), 256)
        own = at[pl.ds(*part["all"]), cols].astype(F32)
        piv[:, cols] = jnp.sum(own, axis=0, keepdims=True) * (1.0 / FB)
        st1[:, cols] = jnp.zeros((8, 256), F32)
        st2[:, cols] = jnp.zeros((8, 256), F32)

    cs[...] = jnp.zeros_like(cs)
    bw[...] = jnp.zeros_like(bw)
    sv[...] = jnp.zeros_like(sv)
    sb[...] = jnp.zeros_like(sb)
    col[...] = jnp.zeros_like(col)

    def add_stats(first, n, cols):
        v = at[first : first + n, cols].astype(F32) - piv[:, cols]
        v = v.reshape(n // 8, 8, 256)
        st1[:, cols] += jnp.sum(v, axis=0)
        st2[:, cols] += jnp.sum(v * v, axis=0)

    def stats(block, first, n):
        @pl.loop(0, 8)
        def _(i):
            add_stats(block * CB + first, n, pl.ds(pl.multiple_of(i * 256, 256), 256))

    def scale(block, h, mod):
        lanes = pl.ds(pl.multiple_of(block * CB, 128), CB)
        factor = 1.0 + mod[1:2, lanes]
        shift = mod[0:1, lanes]
        held = pl.ds(pl.multiple_of(slot(block) * CB, 128), CB)

        @pl.loop(0, 5)
        def _(i):
            rows = pl.ds(pl.multiple_of(h * FB + i * 64, 64), 64)
            w = wt[rows, held].astype(F32)
            scaled = (w * factor).astype(BF16)
            wt[rows, held] = scaled
            back, moved = scaled.astype(F32), w * shift
            cs[rows, :] += sum(back[:, k : k + 128] for k in range(0, CB, 128))
            bw[rows, :] += sum(moved[:, k : k + 128] for k in range(0, CB, 128))

    def scale_all(h, mod):
        for block in everyone:
            scale(block, h, mod)
        rows = slice(h * FB, h * FB + FB)
        for ref in (cs, bw):
            ref[rows] = jnp.broadcast_to(jnp.sum(ref[rows], axis=1, keepdims=True), (FB, 128))

    def product(top, spans, cols):
        left_side = [wt[top : top + FB, i : i + n] for i, n in spans]
        right_side = [at[i : i + n, cols] for i, n in spans]
        return jnp.dot(
            jnp.concatenate(left_side, axis=1) if len(spans) > 1 else left_side[0],
            jnp.concatenate(right_side, axis=0) if len(spans) > 1 else right_side[0],
            preferred_element_type=F32,
        )

    def forward(spans, fresh=False, top=0):
        @pl.loop(0, 8)
        def _(i):
            cols = pl.ds(pl.multiple_of(i * 256, 256), 256)
            if fresh:
                acc[top : top + FB, cols] = product(top, spans, cols)
            else:
                acc[top : top + FB, cols] += product(top, spans, cols)

    got("xr_f")
    send_w("xr_of", w_l, 0, right)
    got("pair_f")
    send_w("xr_vf", v_me, 0, right)
    send_w("xl_vf", v_me, 0, left)
    got("up_a")
    send("up_oa", d, o, "a", up)
    got("dn_b")
    send("dn_ob", u, o, "b", dn)
    send("dn_c", me, u, "c", dn)
    got("up_c")
    send("up_oc", d, o, "c", up)
    send("up_b", me, d, "b", up)
    got("s_own")
    stats(me, 0, CB)
    got("xl_vf")
    send_w("xl_vof", v_r, 0, left)
    got("xl_t")
    send_w("xl_ot", w_r, 1, left)
    got("y_ab")
    send("up_yab", y_me, y_d, "ab", up)
    send("dn_yab", y_me, y_u, "ab", dn)
    got("up_oa")
    send("y_oa", o, y_o, "a", across)
    got("dn_ob")
    send("y_ob", o, y_o, "b", across)
    got("up_oc")
    send("y_oc", o, y_o, "c", across)
    send("s_o", o, o, "all", sib)
    got("y_c")
    send("up_yc", y_me, y_d, "c", up)
    send("dn_yc", y_me, y_u, "c", dn)
    send("s_y", y_me, y_me, "all", sib)
    got("pair_t")
    send_w("xr_vt", v_me, 1, right)
    send_w("xl_vt", v_me, 1, left)
    got("xl_f", "xr_of", "xr_vf", "xl_vof")
    sent("xr_f", "xl_f", "pair_f", "xr_of", "xr_vf", "xl_vf", "xl_vof")
    loads["fmod"].wait()
    scale_all(0, fmod)

    @pl.loop(0, 8)
    def _(i):
        cols = pl.ds(pl.multiple_of(i * 256, 256), 256)
        for k in range(0, FB, 64):
            rows = slice(k, k + 64)
            base = jnp.concatenate([bw[rows], bw[rows]], axis=1)
            target = nT[rows, cols].astype(F32) - sT[rows, cols].astype(F32)
            bt[rows, cols] = (base - target) * (1.0 / math.sqrt(CLIPS * TOK))

    got("s_o")
    stats(o, 0, CB)
    got("s_y")
    stats(y_me, 0, CB)
    forward([(0, 3 * CB)], fresh=True)
    got("xr_vt")
    send_w("xr_vot", v_l, 1, right)
    got("dn_a", "dn_c")
    send("s_u", u, d, "all", sib)
    got("up_b")
    send("s_d", d, u, "all", sib)
    got("s_d")
    stats(u, 0, CB)
    got("s_u")
    stats(d, 0, CB)
    forward([(3 * CB, 2 * CB)])
    got("y_oa", "y_ob")
    send("s_yo", y_o, y_o, "ab", sib)
    got("xr_t", "xl_ot", "xl_vt", "xr_vot")
    sent("xr_t", "xl_t", "pair_t", "xl_ot", "xr_vt", "xl_vt", "xr_vot")
    loads["tmod"].wait()
    scale_all(1, tmod)
    forward([(0, 5 * CB)], True, FB)
    got("dn_yab")
    send("s_yu", y_u, y_d, "ab", sib)
    got("up_yab")
    send("s_yd", y_d, y_u, "ab", sib)
    got("s_yo", "s_yd", "s_yu")
    spans = [(b * CB + k, 256) for b in (y_o, y_u, y_d) for k in (0, 384)]
    for first, n in spans:
        stats(0, first, n)
    forward(spans)
    got("dn_yc")
    send("s_yuc", y_u, y_d, "c", sib)
    got("up_yc")
    send("s_ydc", y_d, y_u, "c", sib)
    got("y_oc")
    send("s_yoc", y_o, y_o, "c", sib)
    got("s_yuc", "s_ydc", "s_yoc")

    last = [(b * CB + 256, 128) for b in (y_o, y_u, y_d)]

    @pl.loop(0, 8)
    def _(i):
        cols = pl.ds(pl.multiple_of(i * 256, 256), 256)
        acc[0:FB, cols] += product(0, last, cols)
        for first, n in last:
            add_stats(first, n, cols)
        shift = jnp.sum(st1[:, cols], axis=0, keepdims=True) * (1.0 / (CLIPS * CB))
        power = jnp.sum(st2[:, cols], axis=0, keepdims=True) * (1.0 / (CLIPS * CB))
        mr[0:1, cols] = piv[:, cols] + shift
        mr[1:2, cols] = lax.rsqrt(jnp.maximum(power - shift * shift, 0.0) + EPS)
        m, r = mr[0:1, cols], mr[1:2, cols]
        small = r * (1.0 / math.sqrt(CLIPS * TOK))
        for k in range(0, FB, 64):
            rows = slice(k, k + 64)
            sums = jnp.concatenate([cs[rows], cs[rows]], axis=1)
            err = small * (acc[rows, cols] - sums * m) + bt[rows, cols]
            v = (r * err).astype(BF16)
            vv[rows, cols] = v
            mv = m * v.astype(F32)
            sv[rows, :] += mv[:, :128] + mv[:, 128:]
            sb[rows, :] += err[:, :128] + err[:, 128:]

    sv[...] = jnp.broadcast_to(jnp.sum(sv[...], axis=1, keepdims=True), sv.shape)
    sb[...] = jnp.broadcast_to(jnp.sum(sb[...], axis=1, keepdims=True), sb.shape)

    def grad(block, dst):
        held = slot(block) * CB
        for first, n in ((0, 256), (256, 256), (512, 128)):
            lanes = pl.ds(pl.multiple_of(block * CB + first, 128), n)
            rows = pl.ds(pl.multiple_of(held + first, 128), n)
            part_sum = lax.dot_general(vv[...], at[rows, :], NT, preferred_element_type=F32)
            g = (part_sum - sv[:, 0:1]) * (1.0 + fmod[1:2, lanes]) + sb[:, 0:1] * fmod[0:1, lanes]
            dst[:, first : first + n] = g.astype(dst.dtype)

    P_ROWS, P_A, P_B = slice(0, 192), slice(0, 96), slice(96, 192)
    Q_ROWS, Q_A, Q_B = slice(192, 320), slice(192, 256), slice(256, 320)
    ls = (1 - l, l)

    def add(dst, rows, *terms):
        dst[rows] = sum([t.astype(F32) for t in terms], dst[rows].astype(F32)).astype(dst.dtype)

    def opposite(j):
        grad(xo * 2 + ls[j], g.at[0, j])
        copy(f"or{j}", g.at[0, j, P_A], rpo.at[0, j], right)
        copy(f"ol{j}", g.at[0, j, P_B], rpo.at[1, j], left)

    def next_one(j):
        grad(xr * 2 + ls[j], g.at[1, j])
        copy(f"rr{j}", g.at[1, j, P_B], rpn.at[0, j, P_B], right)
        if j == 0:
            copy("q1", g.at[1, 0, Q_ROWS], ryq.at[1], pair)
        grad(xl * 2 + ls[j], g.at[2, j])
        copy(f"rl{j}", g.at[2, j, P_A], rpn.at[1, j, P_A], left)
        if j == 0:
            copy("q2", g.at[2, 0, Q_ROWS], ryq.at[2], pair)

    def pass_on(j):
        got(f"or{j}")
        add(g.at[1, j], P_A, rpo[0, j])
        copy(f"sr{j}", g.at[1, j, P_A], rpn.at[0, j, P_A], right)
        got(f"ol{j}")
        add(g.at[2, j], P_B, rpo[1, j])
        copy(f"sl{j}", g.at[2, j, P_B], rpn.at[1, j, P_B], left)

    opposite(0)
    copy("q0", g.at[0, 0, Q_ROWS], ryq.at[0], pair)
    opposite(1)
    next_one(0)
    pass_on(0)
    next_one(1)
    got("q0")
    add(g.at[0, 1], Q_ROWS, ryq[0])
    copy("hor", g.at[0, 1, Q_A], rqo.at[0], right)
    copy("hol", g.at[0, 1, Q_B], rqo.at[1], left)
    pass_on(1)
    grad(x * 2 + ls[0], gown.at[0])
    g[3, 0, Q_ROWS] = gown[0, Q_ROWS].astype(BF16)
    copy("q3", g.at[3, 0, Q_ROWS], ryq.at[3], pair)
    grad(x * 2 + ls[1], gown.at[1])

    loads["gen"].wait()
    loads["gate"].wait()

    def teacher(first, last):
        @pl.loop(first, last)
        def _(i):
            cols = pl.ds(pl.multiple_of(i * 256, 256), 256)
            acc[FB:CB, cols] += product(FB, [(5 * CB, 3 * CB)], cols)
            m, r = mr[0:1, cols], mr[1:2, cols]
            for k in range(0, FB, 64):
                rows, more = slice(k, k + 64), slice(FB + k, FB + k + 64)
                own = pl.ds(pl.multiple_of(p * FB + k, 64), 64)

                def twice(ref, where):
                    return jnp.concatenate([ref[where], ref[where]], axis=1)

                fv = r * (acc[rows, cols] - twice(cs, rows) * m) + twice(bw, rows)
                tv = r * (acc[more, cols] - twice(cs, more) * m) + twice(bw, more)
                diff = sigma * (tv - fv)
                acc[more, cols] = diff
                away = jnp.abs(
                    sT[rows, cols].astype(F32) - (at[own, cols].astype(F32) - sigma * tv)
                )
                pushed = diff * gT[rows, cols].astype(F32)
                col[0, rows, :] += away[:, :128] + away[:, 128:]
                col[1, rows, :] += pushed[:, :128] + pushed[:, 128:]

    teacher(0, 4)
    got("q1", "hor")
    add(g.at[1, 1], Q_ROWS, ryq[1])
    add(g.at[1, 1], Q_A, rqo[0])
    copy("hr", g.at[1, 1, Q_ROWS], rqn.at[0], right)
    got("q2", "hol")
    add(g.at[2, 1], Q_ROWS, ryq[2])
    add(g.at[2, 1], Q_B, rqo[1])
    copy("hl", g.at[2, 1, Q_ROWS], rqn.at[1], left)
    teacher(4, 8)

    total = jnp.sum(jnp.sum(col[0], axis=0, keepdims=True), axis=1, keepdims=True)
    gap_s[0] = jnp.broadcast_to(total, (8, 128))
    copy("gap0", gap_s.at[0], gap_r.at[0], sib)
    got("rr0", "sr0", "rl0", "sl0")
    g[3, 0, P_ROWS] = (
        gown[0, P_ROWS] + rpn[0, 0].astype(F32) + rpn[1, 0].astype(F32)
    ).astype(BF16)
    copy("py", g.at[3, 0, P_ROWS], rpy, pair)
    for k, to in enumerate((on_f(yh, z + 1 - 2 * (z % 2), p), on_f(yh, 3 - z, p), across)):
        got(f"gap{k}")
        gap_s[k + 1] = gap_s[k] + gap_r[k]
        copy(f"gap{k + 1}", gap_s.at[k + 1], gap_r.at[k + 1], to)
    got("gap3")
    total = gap_s[3] + gap_r[3]
    weight = 1.0 / (total[0:1, 0:1] * (1.0 / (TOK * CLIPS * CB)) + EPS)

    same = eye(FB)
    gate_col = jnp.sum(same * gate[...], axis=1, keepdims=True) * weight
    col[0] = jnp.broadcast_to(gate_col, (FB, 128))
    gg_col = jnp.sum(col[1], axis=1, keepdims=True) * weight * (1.0 / math.sqrt(TOK))
    gg_out[...] = jnp.sum(same * gg_col, axis=0, keepdims=True)

    @pl.loop(0, 8)
    def _(i):
        rows = pl.ds(pl.multiple_of(i * 256, 256), 256)
        vv[:, rows] = (col[0, :, 0:1] * acc[FB:CB, rows]).astype(BF16)

    out_bc = pltpu.make_async_copy(vv, bc_out, loc_sems.at[13])
    out_bc.start()

    got("rr1", "sr1", "rl1", "sl1")
    add(gown.at[1], P_ROWS, rpn[0, 1], rpn[1, 1])
    got("q3", "hr", "hl")
    add(gown.at[1], Q_ROWS, ryq[3], rqn[0], rqn[1])
    got("py")
    add(gown.at[1], P_ROWS, rpy[...])
    out_fg = pltpu.make_async_copy(gown.at[1], fg_out, loc_sems.at[14])
    out_fg.start()
    sent(*table)
    out_bc.wait()
    out_fg.wait()


def per_device(
    sample, noise, gen_branch, step, teacher_mod, fake_mod, teacher_weight, fake_weight, gen_gate
):
    hbm = pl.BlockSpec(memory_space=pl.ANY)
    vmem = pl.BlockSpec(memory_space=pltpu.VMEM)
    cot, gate_grad, grad = pl.pallas_call(
        kernel,
        out_shape=(
            jax.ShapeDtypeStruct((FB, TOK), BF16),
            jax.ShapeDtypeStruct((1, FB), F32),
            jax.ShapeDtypeStruct((FB, CB), F32),
        ),
        in_specs=[
            hbm, hbm, hbm, pl.BlockSpec(memory_space=pltpu.SMEM), hbm, hbm, hbm, hbm, hbm,
        ],
        out_specs=(hbm, vmem, hbm),
        scratch_shapes=[
            pltpu.VMEM((CLIPS * CB, TOK), BF16),
            pltpu.VMEM((CB, CLIPS * CB), BF16),
            pltpu.VMEM((CB, TOK), F32),
            pltpu.VMEM((FB, TOK), BF16),
            pltpu.VMEM((FB, TOK), BF16),
            pltpu.VMEM((FB, TOK), BF16),
            pltpu.VMEM((FB, TOK), BF16),
            pltpu.VMEM((FB, TOK), F32),
            pltpu.VMEM((8, TOK), F32),
            pltpu.VMEM((8, TOK), F32),
            pltpu.VMEM((1, TOK), F32),
            pltpu.VMEM((2, TOK), F32),
            pltpu.VMEM((CB, 128), F32),
            pltpu.VMEM((CB, 128), F32),
            pltpu.VMEM((FB, 128), F32),
            pltpu.VMEM((FB, 128), F32),
            pltpu.VMEM((2, FB, 128), F32),
            pltpu.VMEM((2, CLIPS * CB), F32),
            pltpu.VMEM((2, CLIPS * CB), F32),
            pltpu.VMEM((1, FB), F32),
            pltpu.VMEM((4, 2, FB, CB), BF16),
            pltpu.VMEM((2, FB, CB), F32),
            pltpu.VMEM((2, 2, 96, CB), BF16),
            pltpu.VMEM((2, 2, 192, CB), BF16),
            pltpu.VMEM((4, 128, CB), BF16),
            pltpu.VMEM((2, 64, CB), BF16),
            pltpu.VMEM((2, 128, CB), BF16),
            pltpu.VMEM((192, CB), BF16),
            pltpu.VMEM((4, 8, 128), F32),
            pltpu.VMEM((4, 8, 128), F32),
            pltpu.SemaphoreType.DMA((COPIES,)),
            pltpu.SemaphoreType.DMA((COPIES,)),
            pltpu.SemaphoreType.DMA((15,)),
        ],
        compiler_params=pltpu.CompilerParams(
            collective_id=0, has_side_effects=True, vmem_limit_bytes=62 << 20
        ),
        name="step",
    )(
        sample.T, noise.T, gen_branch.T, step,
        teacher_mod.reshape(2, CLIPS * CB), fake_mod.reshape(2, CLIPS * CB),
        teacher_weight.T, fake_weight.T, gen_gate,
    )
    return cot.T, gate_grad, grad.T


def solution(mesh):
    placed = (
        P("clip", "fsdp"),
        P("clip", "fsdp"),
        P("clip", "fsdp"),
        P("clip"),
        P("clip", None, None),
        P("clip", None, None),
        P("clip", "fsdp"),
        P("clip", "fsdp"),
        P("clip", "fsdp"),
    )
    return jax.shard_map(
        per_device,
        mesh=mesh,
        in_specs=placed,
        out_specs=(P("clip", "fsdp"), P("clip", "fsdp"), P("clip", "fsdp")),
        check_vma=False,
    )
```

```python
import functools
import math

import jax
import jax.numpy as jnp
from jax import lax
from jax.experimental import pallas as pl
from jax.experimental.pallas import tpu as pltpu
from jax.sharding import PartitionSpec as P

EPS = 1e-06
F32 = jnp.float32
BF16 = jnp.bfloat16
NT = (((1,), (1,)), ((), ()))

TOK = 2048
FB = 320
CB = 640
CLIPS = 8
COPIES = 80


def eye(n):
    same = lax.broadcasted_iota(jnp.int32, (n, n), 0) == lax.broadcasted_iota(jnp.int32, (n, n), 1)
    return same.astype(F32)


def kernel(
    sample, noise, gen, step, tmod_in, fmod_in, tw, fw, gate_in,
    bc_out, gg_out, fg_out,
    at, wt, acc, sT, nT, gT, vv, bt, st1, st2, piv, mr, cs, bw, sv, sb, col,
    tmod, fmod, gate, g, gown, rpo, rpn, ryq, rqo, rqn, rpy, stat_s, stat_r, gap_s, gap_r,
    send_sems, recv_sems, loc_sems,
):
    clip = lax.axis_index("clip")
    fs = lax.axis_index("fsdp")
    x, l = clip // 2, clip % 2
    p, z, yh = fs % 2, (fs // 2) % 4, fs // 8
    s = 1 - 2 * p
    zu, zd, zo = (z + s + 4) % 4, (z - s + 4) % 4, (z + 2) % 4
    yo = 1 - yh
    xr, xl, xo = (x + 1) % 4, (x + 3) % 4, (x + 2) % 4

    def on_f(y, zz, pp):
        return {"fsdp": (y * 4 + zz) * 2 + pp}

    def on_c(xx, ll):
        return {"clip": xx * 2 + ll}

    up, dn, across, sib = on_f(yh, zu, p), on_f(yh, zd, p), on_f(yo, z, p), on_f(yh, z, 1 - p)
    right, left, pair = on_c(xr, l), on_c(xl, l), on_c(x, 1 - l)
    me, y_me, o, u, d, y_o, y_u, y_d = range(8)

    def slot(block):
        rel = ((block % 4 - z) * s + 8) % 4
        r1, r2 = rel % 2, rel // 2
        yd = (block // 4 + yh) % 2
        return (1 - r1) * (yd + (2 + 2 * yd) * r2) + r1 * (3 + 3 * yd + r2)

    table = {}

    def copy(name, src, dst, to):
        i = len(table)
        assert i < COPIES
        c = pltpu.make_async_remote_copy(
            src_ref=src, dst_ref=dst, send_sem=send_sems.at[i], recv_sem=recv_sems.at[i],
            device_id=to, device_id_type=pl.DeviceIdType.MESH,
        )
        table[name] = [c, False]
        c.start()

    def got(*names):
        for name in names:
            table[name][0].wait_recv()

    def sent(*names):
        for name in names:
            if not table[name][1]:
                table[name][1] = True
                table[name][0].wait_send()

    part = {
        "a": (pl.multiple_of(p * 512, 128), 128),
        "b": (pl.multiple_of(128 + p * 256, 128), 128),
        "c": (pl.multiple_of(256 + p * 64, 64), 64),
        "ab": (pl.multiple_of(p * 384, 128), 256),
        "all": (pl.multiple_of(p * 320, 64), 320),
    }

    def span(block, which):
        first, n = part[which]
        return pl.ds(pl.multiple_of(block * CB + first, 64), n)

    def send(name, here, there, which, to):
        copy(name, at.at[span(here, which), :], at.at[span(there, which), :], to)

    def w_ref(block, half):
        lanes = pl.ds(pl.multiple_of(slot(block) * CB, 128), CB)
        return wt.at[pl.ds(half * FB, FB), lanes]

    def send_w(name, block, half, to):
        copy(name, w_ref(block, half), w_ref(block, half), to)

    loads = {}

    def load(name, src, dst):
        loads[name] = pltpu.make_async_copy(src, dst, loc_sems.at[len(loads)])
        loads[name].start()

    def local(which):
        first, n = part[which]
        return pl.ds(pl.multiple_of(first - p * FB, 64), n)

    for which in ("a", "b", "c"):
        load("s" + which, sample.at[local(which), :], sT.at[local(which), :])
        load("n" + which, noise.at[local(which), :], nT.at[local(which), :])
    load("fw", fw, w_ref(clip, 0))
    load("tw", tw, w_ref(clip, 1))
    load("fmod", fmod_in, fmod)
    load("tmod", tmod_in, tmod)
    load("gen", gen, gT)
    load("gate", gate_in, gate)
    barrier = pltpu.get_barrier_semaphore()
    for to in (up, dn, across, sib, right, left, pair):
        pl.semaphore_signal(barrier, inc=1, device_id=to, device_id_type=pl.DeviceIdType.MESH)

    frac = jnp.full((8, 128), step[0], jnp.int32).astype(F32) / 1000.0
    sigma = (5.0 * frac / (1.0 + 4.0 * frac))[0:1, 0:1]

    def noised(which):
        loads["s" + which].wait()
        loads["n" + which].wait()
        first, n = part[which]
        own = pl.multiple_of(first - p * FB, 64)

        @pl.loop(0, n // 32)
        def _(i):
            rows = pl.ds(pl.multiple_of(own + i * 32, 32), 32)
            mixed = (1.0 - sigma) * sT[rows, :].astype(F32) + sigma * nT[rows, :].astype(F32)
            at[pl.ds(pl.multiple_of(first + i * 32, 32), 32), :] = mixed.astype(BF16)

    noised("a")
    pl.semaphore_wait(barrier, 7)
    send("up_a", me, d, "a", up)
    noised("b")
    send("dn_b", me, u, "b", dn)
    loads["fw"].wait()
    send_w("pair_f", clip, 0, pair)
    loads["tw"].wait()
    send_w("pair_t", clip, 1, pair)
    send("y_ab", me, y_me, "ab", across)
    send_w("xr_f", clip, 0, right)
    send_w("xl_f", clip, 0, left)
    noised("c")
    send("up_c", me, d, "c", up)
    send("dn_a", me, u, "a", dn)
    send("y_c", me, y_me, "c", across)
    send("s_own", me, me, "all", sib)
    send_w("xr_t", clip, 1, right)
    send_w("xl_t", clip, 1, left)

    w_l, w_r, w_o = xl * 2 + l, xr * 2 + l, xo * 2 + l
    v_me, v_l, v_r, v_o = x * 2 + 1 - l, xl * 2 + 1 - l, xr * 2 + 1 - l, xo * 2 + 1 - l
    everyone = (clip, w_l, w_r, w_o, v_me, v_l, v_r, v_o)

    @pl.loop(0, 8)
    def _(i):
        cols = pl.ds(pl.multiple_of(i * 256, 256), 256)
        own = at[pl.ds(*part["all"]), cols].astype(F32)
        piv[:, cols] = jnp.sum(own, axis=0, keepdims=True) * (1.0 / FB)
        st1[:, cols] = jnp.zeros((8, 256), F32)
        st2[:, cols] = jnp.zeros((8, 256), F32)

    cs[...] = jnp.zeros_like(cs)
    bw[...] = jnp.zeros_like(bw)
    sv[...] = jnp.zeros_like(sv)
    sb[...] = jnp.zeros_like(sb)
    col[...] = jnp.zeros_like(col)

    def add_stats(first, n, cols):
        v = at[pl.ds(first, n), cols].astype(F32) - piv[:, cols]
        v = v.reshape(n // 8, 8, 256)
        st1[:, cols] += jnp.sum(v, axis=0)
        st2[:, cols] += jnp.sum(v * v, axis=0)

    def stats(block, which):
        first, n = part[which]

        @pl.loop(0, 8)
        def _(i):
            add_stats(pl.multiple_of(block * CB + first, 64), n, pl.ds(pl.multiple_of(i * 256, 256), 256))

    def scale(block, h, mod):
        lanes = pl.ds(pl.multiple_of(block * CB, 128), CB)
        factor = 1.0 + mod[1:2, lanes]
        shift = mod[0:1, lanes]
        held = pl.ds(pl.multiple_of(slot(block) * CB, 128), CB)

        @pl.loop(0, 5)
        def _(i):
            rows = pl.ds(pl.multiple_of(h * FB + i * 64, 64), 64)
            w = wt[rows, held].astype(F32)
            scaled = (w * factor).astype(BF16)
            wt[rows, held] = scaled
            back, moved = scaled.astype(F32), w * shift
            cs[rows, :] += sum(back[:, k : k + 128] for k in range(0, CB, 128))
            bw[rows, :] += sum(moved[:, k : k + 128] for k in range(0, CB, 128))

    def scale_all(h, mod):
        for block in everyone:
            scale(block, h, mod)
        rows = slice(h * FB, h * FB + FB)
        for ref in (cs, bw):
            ref[rows] = jnp.broadcast_to(jnp.sum(ref[rows], axis=1, keepdims=True), (FB, 128))

    def product(top, spans, cols):
        left_side = [wt[top : top + FB, i : i + n] for i, n in spans]
        right_side = [at[i : i + n, cols] for i, n in spans]
        return jnp.dot(
            jnp.concatenate(left_side, axis=1) if len(spans) > 1 else left_side[0],
            jnp.concatenate(right_side, axis=0) if len(spans) > 1 else right_side[0],
            preferred_element_type=F32,
        )

    def forward(spans, fresh=False, top=0):
        @pl.loop(0, 8)
        def _(i):
            cols = pl.ds(pl.multiple_of(i * 256, 256), 256)
            if fresh:
                acc[top : top + FB, cols] = product(top, spans, cols)
            else:
                acc[top : top + FB, cols] += product(top, spans, cols)

    got("xr_f")
    send_w("xr_of", w_l, 0, right)
    got("pair_f")
    send_w("xr_vf", v_me, 0, right)
    send_w("xl_vf", v_me, 0, left)
    got("up_a")
    send("up_oa", d, o, "a", up)
    got("dn_b")
    send("dn_ob", u, o, "b", dn)
    send("dn_c", me, u, "c", dn)
    got("up_c")
    send("up_oc", d, o, "c", up)
    send("up_b", me, d, "b", up)
    stats(me, "all")
    got("xl_vf")
    send_w("xl_vof", v_r, 0, left)
    got("xl_t")
    send_w("xl_ot", w_r, 1, left)
    got("y_ab")
    send("up_yab", y_me, y_d, "ab", up)
    send("dn_yab", y_me, y_u, "ab", dn)
    got("up_oa")
    send("y_oa", o, y_o, "a", across)
    got("dn_ob")
    send("y_ob", o, y_o, "b", across)
    got("up_oc")
    send("y_oc", o, y_o, "c", across)
    send("s_o", o, o, "all", sib)
    got("y_c")
    send("up_yc", y_me, y_d, "c", up)
    send("dn_yc", y_me, y_u, "c", dn)
    send("s_y", y_me, y_me, "all", sib)
    got("pair_t")
    send_w("xr_vt", v_me, 1, right)
    send_w("xl_vt", v_me, 1, left)
    got("xl_f", "xr_of", "xr_vf", "xl_vof")
    sent("xr_f", "xl_f", "pair_f", "xr_of", "xr_vf", "xl_vf", "xl_vof")
    loads["fmod"].wait()
    scale_all(0, fmod)

    @pl.loop(0, 8)
    def _(i):
        cols = pl.ds(pl.multiple_of(i * 256, 256), 256)
        for k in range(0, FB, 64):
            rows = slice(k, k + 64)
            base = jnp.concatenate([bw[rows], bw[rows]], axis=1)
            target = nT[rows, cols].astype(F32) - sT[rows, cols].astype(F32)
            bt[rows, cols] = (base - target) * (1.0 / math.sqrt(CLIPS * TOK))

    stats(o, "all")
    stats(y_me, "all")
    got("s_own", "s_o", "s_y")
    forward([(0, 3 * CB)], fresh=True)
    got("xr_vt")
    send_w("xr_vot", v_l, 1, right)
    got("dn_a", "dn_c")
    send("s_u", u, d, "all", sib)
    got("up_b")
    send("s_d", d, u, "all", sib)
    stats(u, "all")
    stats(d, "all")
    got("s_d", "s_u")
    forward([(3 * CB, 2 * CB)])
    got("xr_t", "xl_ot", "xl_vt", "xr_vot")
    sent("xr_t", "xl_t", "pair_t", "xl_ot", "xr_vt", "xl_vt", "xr_vot")
    loads["tmod"].wait()
    scale_all(1, tmod)
    forward([(0, 5 * CB)], True, FB)
    got("dn_yab")
    send("s_yu", y_u, y_d, "ab", sib)
    got("up_yab")
    send("s_yd", y_d, y_u, "ab", sib)
    stats(y_u, "ab")
    stats(y_d, "ab")
    got("s_yd", "s_yu")
    forward([(b * CB + k, 256) for b in (y_u, y_d) for k in (0, 384)])
    got("y_oa", "y_ob")
    send("s_yo", y_o, y_o, "ab", sib)
    stats(y_o, "ab")

    held = 5 * FB + 3 * 256
    shift = jnp.sum(st1[...], axis=0, keepdims=True)
    stat_s[0:1, :] = piv[...] + shift * (1.0 / held)
    stat_s[1:2, :] = jnp.sum(st2[...], axis=0, keepdims=True) - shift * shift * (1.0 / held)
    copy("stat", stat_s, stat_r, sib)
    got("s_yo")
    forward([(y_o * CB + k, 256) for k in (0, 384)])
    got("stat")
    apart = stat_s[0:1, :] - stat_r[0:1, :]
    piv[...] = 0.5 * (stat_s[0:1, :] + stat_r[0:1, :])
    power_held = stat_s[1:2, :] + stat_r[1:2, :] + apart * apart * (held / 2)
    st1[...] = jnp.zeros_like(st1)
    st2[...] = jnp.broadcast_to(power_held * 0.125, st2.shape)

    got("dn_yc")
    send("s_yuc", y_u, y_d, "c", sib)
    got("up_yc")
    send("s_ydc", y_d, y_u, "c", sib)
    got("y_oc")
    send("s_yoc", y_o, y_o, "c", sib)
    got("s_yuc", "s_ydc", "s_yoc")

    last = [(b * CB + 256, 128) for b in (y_o, y_u, y_d)]

    @pl.loop(0, 8)
    def _(i):
        cols = pl.ds(pl.multiple_of(i * 256, 256), 256)
        acc[0:FB, cols] += product(0, last, cols)
        for first, n in last:
            add_stats(first, n, cols)
        shift = jnp.sum(st1[:, cols], axis=0, keepdims=True) * (1.0 / (CLIPS * CB))
        power = jnp.sum(st2[:, cols], axis=0, keepdims=True) * (1.0 / (CLIPS * CB))
        mr[0:1, cols] = piv[:, cols] + shift
        mr[1:2, cols] = lax.rsqrt(jnp.maximum(power - shift * shift, 0.0) + EPS)
        m, r = mr[0:1, cols], mr[1:2, cols]
        small = r * (1.0 / math.sqrt(CLIPS * TOK))
        for k in range(0, FB, 64):
            rows = slice(k, k + 64)
            sums = jnp.concatenate([cs[rows], cs[rows]], axis=1)
            err = small * (acc[rows, cols] - sums * m) + bt[rows, cols]
            v = (r * err).astype(BF16)
            vv[rows, cols] = v
            mv = m * v.astype(F32)
            sv[rows, :] += mv[:, :128] + mv[:, 128:]
            sb[rows, :] += err[:, :128] + err[:, 128:]

    sv[...] = jnp.broadcast_to(jnp.sum(sv[...], axis=1, keepdims=True), sv.shape)
    sb[...] = jnp.broadcast_to(jnp.sum(sb[...], axis=1, keepdims=True), sb.shape)

    def grad(block, dst):
        held = slot(block) * CB
        for first, n in ((0, 256), (256, 256), (512, 128)):
            lanes = pl.ds(pl.multiple_of(block * CB + first, 128), n)
            rows = pl.ds(pl.multiple_of(held + first, 128), n)
            part_sum = lax.dot_general(vv[...], at[rows, :], NT, preferred_element_type=F32)
            g = (part_sum - sv[:, 0:1]) * (1.0 + fmod[1:2, lanes]) + sb[:, 0:1] * fmod[0:1, lanes]
            dst[:, first : first + n] = g.astype(dst.dtype)

    P_ROWS, P_A, P_B = slice(0, 192), slice(0, 96), slice(96, 192)
    Q_ROWS, Q_A, Q_B = slice(192, 320), slice(192, 256), slice(256, 320)
    ls = (1 - l, l)

    def add(dst, rows, *terms):
        dst[rows] = sum([t.astype(F32) for t in terms], dst[rows].astype(F32)).astype(dst.dtype)

    def opposite(j):
        grad(xo * 2 + ls[j], g.at[0, j])
        copy(f"or{j}", g.at[0, j, P_A], rpo.at[0, j], right)
        copy(f"ol{j}", g.at[0, j, P_B], rpo.at[1, j], left)

    def next_one(j):
        grad(xr * 2 + ls[j], g.at[1, j])
        copy(f"rr{j}", g.at[1, j, P_B], rpn.at[0, j, P_B], right)
        if j == 0:
            copy("q1", g.at[1, 0, Q_ROWS], ryq.at[1], pair)
        grad(xl * 2 + ls[j], g.at[2, j])
        copy(f"rl{j}", g.at[2, j, P_A], rpn.at[1, j, P_A], left)
        if j == 0:
            copy("q2", g.at[2, 0, Q_ROWS], ryq.at[2], pair)

    def pass_on(j):
        got(f"or{j}")
        add(g.at[1, j], P_A, rpo[0, j])
        copy(f"sr{j}", g.at[1, j, P_A], rpn.at[0, j, P_A], right)
        got(f"ol{j}")
        add(g.at[2, j], P_B, rpo[1, j])
        copy(f"sl{j}", g.at[2, j, P_B], rpn.at[1, j, P_B], left)

    opposite(0)
    copy("q0", g.at[0, 0, Q_ROWS], ryq.at[0], pair)
    opposite(1)
    next_one(0)
    pass_on(0)
    next_one(1)
    got("q0")
    add(g.at[0, 1], Q_ROWS, ryq[0])
    copy("hor", g.at[0, 1, Q_A], rqo.at[0], right)
    copy("hol", g.at[0, 1, Q_B], rqo.at[1], left)
    pass_on(1)
    grad(x * 2 + ls[0], gown.at[0])
    g[3, 0, Q_ROWS] = gown[0, Q_ROWS].astype(BF16)
    copy("q3", g.at[3, 0, Q_ROWS], ryq.at[3], pair)

    loads["gen"].wait()
    loads["gate"].wait()

    def teacher(first, last):
        @pl.loop(first, last)
        def _(i):
            cols = pl.ds(pl.multiple_of(i * 256, 256), 256)
            acc[FB:CB, cols] += product(FB, [(5 * CB, 3 * CB)], cols)
            m, r = mr[0:1, cols], mr[1:2, cols]
            for k in range(0, FB, 64):
                rows, more = slice(k, k + 64), slice(FB + k, FB + k + 64)
                own = pl.ds(pl.multiple_of(p * FB + k, 64), 64)

                def twice(ref, where):
                    return jnp.concatenate([ref[where], ref[where]], axis=1)

                fv = r * (acc[rows, cols] - twice(cs, rows) * m) + twice(bw, rows)
                tv = r * (acc[more, cols] - twice(cs, more) * m) + twice(bw, more)
                diff = sigma * (tv - fv)
                acc[more, cols] = diff
                away = jnp.abs(
                    sT[rows, cols].astype(F32) - (at[own, cols].astype(F32) - sigma * tv)
                )
                pushed = diff * gT[rows, cols].astype(F32)
                col[0, rows, :] += away[:, :128] + away[:, 128:]
                col[1, rows, :] += pushed[:, :128] + pushed[:, 128:]

    teacher(0, 8)
    total = jnp.sum(jnp.sum(col[0], axis=0, keepdims=True), axis=1, keepdims=True)
    gap_s[0] = jnp.broadcast_to(total, (8, 128))
    gap_to = (sib, on_f(yh, z + 1 - 2 * (z % 2), p), on_f(yh, 3 - z, p), across)

    def gap_step(k):
        if k:
            got(f"gap{k - 1}")
            gap_s[k] = gap_s[k - 1] + gap_r[k - 1]
        copy(f"gap{k}", gap_s.at[k], gap_r.at[k], gap_to[k])

    gap_step(0)
    got("q1", "hor")
    add(g.at[1, 1], Q_ROWS, ryq[1])
    add(g.at[1, 1], Q_A, rqo[0])
    copy("hr", g.at[1, 1, Q_ROWS], rqn.at[0], right)
    gap_step(1)
    got("q2", "hol")
    add(g.at[2, 1], Q_ROWS, ryq[2])
    add(g.at[2, 1], Q_B, rqo[1])
    copy("hl", g.at[2, 1, Q_ROWS], rqn.at[1], left)
    gap_step(2)
    got("rr0", "sr0", "rl0", "sl0")
    g[3, 0, P_ROWS] = (
        gown[0, P_ROWS] + rpn[0, 0].astype(F32) + rpn[1, 0].astype(F32)
    ).astype(BF16)
    copy("py", g.at[3, 0, P_ROWS], rpy, pair)
    gap_step(3)
    grad(x * 2 + ls[1], gown.at[1])
    got("gap3")
    total = gap_s[3] + gap_r[3]
    weight = 1.0 / (total[0:1, 0:1] * (1.0 / (TOK * CLIPS * CB)) + EPS)

    same = eye(FB)
    gate_col = jnp.sum(same * gate[...], axis=1, keepdims=True) * weight
    col[0] = jnp.broadcast_to(gate_col, (FB, 128))
    gg_col = jnp.sum(col[1], axis=1, keepdims=True) * weight * (1.0 / math.sqrt(TOK))
    gg_out[...] = jnp.sum(same * gg_col, axis=0, keepdims=True)

    @pl.loop(0, 8)
    def _(i):
        rows = pl.ds(pl.multiple_of(i * 256, 256), 256)
        vv[:, rows] = (col[0, :, 0:1] * acc[FB:CB, rows]).astype(BF16)

    out_bc = pltpu.make_async_copy(vv, bc_out, loc_sems.at[13])
    out_bc.start()

    got("rr1", "sr1", "rl1", "sl1")
    add(gown.at[1], P_ROWS, rpn[0, 1], rpn[1, 1])
    got("q3", "hr", "hl")
    add(gown.at[1], Q_ROWS, ryq[3], rqn[0], rqn[1])
    got("py")
    add(gown.at[1], P_ROWS, rpy[...])
    out_fg = pltpu.make_async_copy(gown.at[1], fg_out, loc_sems.at[14])
    out_fg.start()
    sent(*table)
    out_bc.wait()
    out_fg.wait()


def per_device(
    sample, noise, gen_branch, step, teacher_mod, fake_mod, teacher_weight, fake_weight, gen_gate
):
    hbm = pl.BlockSpec(memory_space=pl.ANY)
    vmem = pl.BlockSpec(memory_space=pltpu.VMEM)
    cot, gate_grad, grad = pl.pallas_call(
        kernel,
        out_shape=(
            jax.ShapeDtypeStruct((FB, TOK), BF16),
            jax.ShapeDtypeStruct((1, FB), F32),
            jax.ShapeDtypeStruct((FB, CB), F32),
        ),
        in_specs=[
            hbm, hbm, hbm, pl.BlockSpec(memory_space=pltpu.SMEM), hbm, hbm, hbm, hbm, hbm,
        ],
        out_specs=(hbm, vmem, hbm),
        scratch_shapes=[
            pltpu.VMEM((CLIPS * CB, TOK), BF16),
            pltpu.VMEM((CB, CLIPS * CB), BF16),
            pltpu.VMEM((CB, TOK), F32),
            pltpu.VMEM((FB, TOK), BF16),
            pltpu.VMEM((FB, TOK), BF16),
            pltpu.VMEM((FB, TOK), BF16),
            pltpu.VMEM((FB, TOK), BF16),
            pltpu.VMEM((FB, TOK), F32),
            pltpu.VMEM((8, TOK), F32),
            pltpu.VMEM((8, TOK), F32),
            pltpu.VMEM((1, TOK), F32),
            pltpu.VMEM((2, TOK), F32),
            pltpu.VMEM((CB, 128), F32),
            pltpu.VMEM((CB, 128), F32),
            pltpu.VMEM((FB, 128), F32),
            pltpu.VMEM((FB, 128), F32),
            pltpu.VMEM((2, FB, 128), F32),
            pltpu.VMEM((2, CLIPS * CB), F32),
            pltpu.VMEM((2, CLIPS * CB), F32),
            pltpu.VMEM((1, FB), F32),
            pltpu.VMEM((4, 2, FB, CB), BF16),
            pltpu.VMEM((2, FB, CB), F32),
            pltpu.VMEM((2, 2, 96, CB), BF16),
            pltpu.VMEM((2, 2, 192, CB), BF16),
            pltpu.VMEM((4, 128, CB), BF16),
            pltpu.VMEM((2, 64, CB), BF16),
            pltpu.VMEM((2, 128, CB), BF16),
            pltpu.VMEM((192, CB), BF16),
            pltpu.VMEM((2, TOK), F32),
            pltpu.VMEM((2, TOK), F32),
            pltpu.VMEM((4, 8, 128), F32),
            pltpu.VMEM((4, 8, 128), F32),
            pltpu.SemaphoreType.DMA((COPIES,)),
            pltpu.SemaphoreType.DMA((COPIES,)),
            pltpu.SemaphoreType.DMA((15,)),
        ],
        compiler_params=pltpu.CompilerParams(
            collective_id=0, has_side_effects=True, vmem_limit_bytes=62 << 20
        ),
        name="step",
    )(
        sample.T, noise.T, gen_branch.T, step,
        teacher_mod.reshape(2, CLIPS * CB), fake_mod.reshape(2, CLIPS * CB),
        teacher_weight.T, fake_weight.T, gen_gate,
    )
    return cot.T, gate_grad, grad.T


def solution(mesh):
    placed = (
        P("clip", "fsdp"),
        P("clip", "fsdp"),
        P("clip", "fsdp"),
        P("clip"),
        P("clip", None, None),
        P("clip", None, None),
        P("clip", "fsdp"),
        P("clip", "fsdp"),
        P("clip", "fsdp"),
    )
    return jax.shard_map(
        per_device,
        mesh=mesh,
        in_specs=placed,
        out_specs=(P("clip", "fsdp"), P("clip", "fsdp"), P("clip", "fsdp")),
        check_vma=False,
    )
```

```python
import functools
import math

import jax
import jax.numpy as jnp
from jax import lax
from jax.experimental import pallas as pl
from jax.experimental.pallas import tpu as pltpu
from jax.sharding import PartitionSpec as P

EPS = 1e-06
F32 = jnp.float32
BF16 = jnp.bfloat16
NT = (((1,), (1,)), ((), ()))

TOK = 2048
FB = 320
CB = 640
CLIPS = 8
COPIES = 80


def eye(n):
    same = lax.broadcasted_iota(jnp.int32, (n, n), 0) == lax.broadcasted_iota(jnp.int32, (n, n), 1)
    return same.astype(F32)


def kernel(
    sample, noise, gen, step, tmod_in, fmod_in, tw, fw, gate_in,
    bc_out, gg_out, fg_out,
    at, wt, acc, sT, nT, gT, vv, bt, st1, st2, piv, mr, cs, bw, sv, sb, col,
    tmod, fmod, gate, g, gown, rpo, rpn, ryq, rqo, rqn, rpy, stat_s, stat_r, gap_s, gap_r,
    send_sems, recv_sems, loc_sems,
):
    clip = lax.axis_index("clip")
    fs = lax.axis_index("fsdp")
    x, l = clip // 2, clip % 2
    p, z, yh = fs % 2, (fs // 2) % 4, fs // 8
    s = 1 - 2 * p
    zu, zd, zo = (z + s + 4) % 4, (z - s + 4) % 4, (z + 2) % 4
    yo = 1 - yh
    xr, xl, xo = (x + 1) % 4, (x + 3) % 4, (x + 2) % 4

    def on_f(y, zz, pp):
        return {"fsdp": (y * 4 + zz) * 2 + pp}

    def on_c(xx, ll):
        return {"clip": xx * 2 + ll}

    up, dn, across, sib = on_f(yh, zu, p), on_f(yh, zd, p), on_f(yo, z, p), on_f(yh, z, 1 - p)
    right, left, pair = on_c(xr, l), on_c(xl, l), on_c(x, 1 - l)
    me, o, u, d, y_me, y_o, y_u, y_d = range(8)

    def slot(block):
        rel = ((block % 4 - z) * s + 8) % 4
        yd = (block // 4 + yh) % 2
        return yd * 4 + (rel % 2) * 2 + rel // 2

    table = {}

    def copy(name, src, dst, to):
        i = len(table)
        assert i < COPIES
        c = pltpu.make_async_remote_copy(
            src_ref=src, dst_ref=dst, send_sem=send_sems.at[i], recv_sem=recv_sems.at[i],
            device_id=to, device_id_type=pl.DeviceIdType.MESH,
        )
        table[name] = [c, False]
        c.start()

    def got(*names):
        for name in names:
            table[name][0].wait_recv()

    def sent(*names):
        for name in names:
            if not table[name][1]:
                table[name][1] = True
                table[name][0].wait_send()

    part = {
        "a": (pl.multiple_of(p * 512, 128), 128),
        "b": (pl.multiple_of(128 + p * 256, 128), 128),
        "c": (pl.multiple_of(256 + p * 64, 64), 64),
        "ab": (pl.multiple_of(p * 384, 128), 256),
        "all": (pl.multiple_of(p * 320, 64), 320),
    }

    def span(block, which):
        first, n = part[which]
        return pl.ds(pl.multiple_of(block * CB + first, 64), n)

    def send(name, here, there, which, to):
        copy(name, at.at[span(here, which), :], at.at[span(there, which), :], to)

    def w_ref(block, half):
        lanes = pl.ds(pl.multiple_of(slot(block) * CB, 128), CB)
        return wt.at[pl.ds(half * FB, FB), lanes]

    def send_w(name, block, half, to):
        copy(name, w_ref(block, half), w_ref(block, half), to)

    loads = {}

    def load(name, src, dst):
        loads[name] = pltpu.make_async_copy(src, dst, loc_sems.at[len(loads)])
        loads[name].start()

    def local(which):
        first, n = part[which]
        return pl.ds(pl.multiple_of(first - p * FB, 64), n)

    for which in ("a", "b", "c"):
        load("s" + which, sample.at[local(which), :], sT.at[local(which), :])
        load("n" + which, noise.at[local(which), :], nT.at[local(which), :])
    load("fw", fw, w_ref(clip, 0))
    load("tw", tw, w_ref(clip, 1))
    load("fmod", fmod_in, fmod)
    load("tmod", tmod_in, tmod)
    load("gen", gen, gT)
    load("gate", gate_in, gate)
    barrier = pltpu.get_barrier_semaphore()
    for to in (up, dn, across, sib, right, left, pair):
        pl.semaphore_signal(barrier, inc=1, device_id=to, device_id_type=pl.DeviceIdType.MESH)

    frac = jnp.full((8, 128), step[0], jnp.int32).astype(F32) / 1000.0
    sigma = (5.0 * frac / (1.0 + 4.0 * frac))[0:1, 0:1]

    def noised(which):
        loads["s" + which].wait()
        loads["n" + which].wait()
        first, n = part[which]
        own = pl.multiple_of(first - p * FB, 64)

        @pl.loop(0, n // 32)
        def _(i):
            rows = pl.ds(pl.multiple_of(own + i * 32, 32), 32)
            mixed = (1.0 - sigma) * sT[rows, :].astype(F32) + sigma * nT[rows, :].astype(F32)
            at[pl.ds(pl.multiple_of(first + i * 32, 32), 32), :] = mixed.astype(BF16)

    noised("a")
    pl.semaphore_wait(barrier, 7)
    send("up_a", me, d, "a", up)
    noised("b")
    send("dn_b", me, u, "b", dn)
    loads["fw"].wait()
    send_w("pair_f", clip, 0, pair)
    loads["tw"].wait()
    send_w("pair_t", clip, 1, pair)
    send("y_ab", me, y_me, "ab", across)
    send_w("xr_f", clip, 0, right)
    send_w("xl_f", clip, 0, left)
    noised("c")
    send("up_c", me, d, "c", up)
    send("dn_a", me, u, "a", dn)
    send("y_c", me, y_me, "c", across)
    send("s_own", me, me, "all", sib)
    send_w("xr_t", clip, 1, right)
    send_w("xl_t", clip, 1, left)

    w_l, w_r, w_o = xl * 2 + l, xr * 2 + l, xo * 2 + l
    v_me, v_l, v_r, v_o = x * 2 + 1 - l, xl * 2 + 1 - l, xr * 2 + 1 - l, xo * 2 + 1 - l
    everyone = (clip, w_l, w_r, w_o, v_me, v_l, v_r, v_o)

    @pl.loop(0, 8)
    def _(i):
        cols = pl.ds(pl.multiple_of(i * 256, 256), 256)
        own = at[pl.ds(*part["all"]), cols].astype(F32)
        piv[:, cols] = jnp.sum(own, axis=0, keepdims=True) * (1.0 / FB)
        st1[:, cols] = jnp.zeros((8, 256), F32)
        st2[:, cols] = jnp.zeros((8, 256), F32)

    cs[...] = jnp.zeros_like(cs)
    bw[...] = jnp.zeros_like(bw)
    sv[...] = jnp.zeros_like(sv)
    sb[...] = jnp.zeros_like(sb)
    col[...] = jnp.zeros_like(col)

    def add_stats(first, n, cols):
        v = at[pl.ds(first, n), cols].astype(F32) - piv[:, cols]
        v = v.reshape(n // 8, 8, 256)
        st1[:, cols] += jnp.sum(v, axis=0)
        st2[:, cols] += jnp.sum(v * v, axis=0)

    def stats(block, which):
        first, n = part[which]

        @pl.loop(0, 8)
        def _(i):
            add_stats(pl.multiple_of(block * CB + first, 64), n, pl.ds(pl.multiple_of(i * 256, 256), 256))

    def scale(block, h, mod):
        lanes = pl.ds(pl.multiple_of(block * CB, 128), CB)
        factor = 1.0 + mod[1:2, lanes]
        shift = mod[0:1, lanes]
        held = pl.ds(pl.multiple_of(slot(block) * CB, 128), CB)

        @pl.loop(0, 5)
        def _(i):
            rows = pl.ds(pl.multiple_of(h * FB + i * 64, 64), 64)
            w = wt[rows, held].astype(F32)
            scaled = (w * factor).astype(BF16)
            wt[rows, held] = scaled
            back, moved = scaled.astype(F32), w * shift
            cs[rows, :] += sum(back[:, k : k + 128] for k in range(0, CB, 128))
            bw[rows, :] += sum(moved[:, k : k + 128] for k in range(0, CB, 128))

    def scale_all(h, mod):
        for block in everyone:
            scale(block, h, mod)
        rows = slice(h * FB, h * FB + FB)
        for ref in (cs, bw):
            ref[rows] = jnp.broadcast_to(jnp.sum(ref[rows], axis=1, keepdims=True), (FB, 128))

    def product(top, spans, cols):
        left_side = [wt[top : top + FB, i : i + n] for i, n in spans]
        right_side = [at[i : i + n, cols] for i, n in spans]
        return jnp.dot(
            jnp.concatenate(left_side, axis=1) if len(spans) > 1 else left_side[0],
            jnp.concatenate(right_side, axis=0) if len(spans) > 1 else right_side[0],
            preferred_element_type=F32,
        )

    def forward(spans, fresh=False, top=0):
        @pl.loop(0, 8)
        def _(i):
            cols = pl.ds(pl.multiple_of(i * 256, 256), 256)
            if fresh:
                acc[top : top + FB, cols] = product(top, spans, cols)
            else:
                acc[top : top + FB, cols] += product(top, spans, cols)

    got("xr_f")
    send_w("xr_of", w_l, 0, right)
    got("up_a")
    send("up_oa", d, o, "a", up)
    got("dn_b")
    send("dn_ob", u, o, "b", dn)
    send("dn_c", me, u, "c", dn)
    got("pair_f")
    send_w("xr_vf", v_me, 0, right)
    send_w("xl_vf", v_me, 0, left)
    got("up_c")
    send("up_oc", d, o, "c", up)
    send("up_b", me, d, "b", up)
    got("pair_t")
    send_w("xr_vt", v_me, 1, right)
    stats(me, "all")
    got("xl_vf")
    send_w("xl_vof", v_r, 0, left)
    send_w("xl_vt", v_me, 1, left)
    got("xl_t")
    send_w("xl_ot", w_r, 1, left)
    got("up_oa")
    send("y_oa", o, y_o, "a", across)
    got("dn_ob")
    send("y_ob", o, y_o, "b", across)
    got("up_oc")
    send("y_oc", o, y_o, "c", across)
    send("s_o", o, o, "all", sib)
    got("xl_f", "xr_of", "xr_vf", "xl_vof")
    sent("xr_f", "xl_f", "pair_f", "xr_of", "xr_vf", "xl_vf", "xl_vof")
    loads["fmod"].wait()
    scale_all(0, fmod)
    got("y_ab")
    send("up_yab", y_me, y_d, "ab", up)
    send("dn_yab", y_me, y_u, "ab", dn)

    @pl.loop(0, 8)
    def _(i):
        cols = pl.ds(pl.multiple_of(i * 256, 256), 256)
        for k in range(0, FB, 64):
            rows = slice(k, k + 64)
            base = jnp.concatenate([bw[rows], bw[rows]], axis=1)
            target = nT[rows, cols].astype(F32) - sT[rows, cols].astype(F32)
            bt[rows, cols] = (base - target) * (1.0 / math.sqrt(CLIPS * TOK))

    got("s_own", "s_o")
    forward([(0, 2 * CB)], fresh=True)
    got("xr_vt")
    send_w("xr_vot", v_l, 1, right)
    got("dn_a", "dn_c")
    send("s_u", u, d, "all", sib)
    stats(o, "all")
    got("up_b")
    send("s_d", d, u, "all", sib)
    got("y_c")
    send("up_yc", y_me, y_d, "c", up)
    send("dn_yc", y_me, y_u, "c", dn)
    send("s_y", y_me, y_me, "all", sib)
    stats(u, "all")
    stats(d, "all")
    got("s_d", "s_u", "s_y")
    forward([(2 * CB, 3 * CB)])
    stats(y_me, "all")
    got("xr_t", "xl_ot", "xl_vt", "xr_vot")
    sent("xr_t", "xl_t", "pair_t", "xl_ot", "xr_vt", "xl_vt", "xr_vot")
    loads["tmod"].wait()
    scale_all(1, tmod)
    forward([(0, 5 * CB)], True, FB)
    got("dn_yab")
    send("s_yu", y_u, y_d, "ab", sib)
    got("up_yab")
    send("s_yd", y_d, y_u, "ab", sib)
    stats(y_u, "ab")
    stats(y_d, "ab")
    got("s_yd", "s_yu")
    forward([(b * CB + k, 256) for b in (y_u, y_d) for k in (0, 384)])
    got("y_oa", "y_ob")
    send("s_yo", y_o, y_o, "ab", sib)
    stats(y_o, "ab")

    held = 5 * FB + 3 * 256
    shift = jnp.sum(st1[...], axis=0, keepdims=True)
    stat_s[0:1, :] = piv[...] + shift * (1.0 / held)
    stat_s[1:2, :] = jnp.sum(st2[...], axis=0, keepdims=True) - shift * shift * (1.0 / held)
    copy("stat", stat_s, stat_r, sib)
    got("s_yo")
    forward([(y_o * CB + k, 256) for k in (0, 384)])
    got("stat")
    apart = stat_s[0:1, :] - stat_r[0:1, :]
    piv[...] = 0.5 * (stat_s[0:1, :] + stat_r[0:1, :])
    power_held = stat_s[1:2, :] + stat_r[1:2, :] + apart * apart * (held / 2)
    st1[...] = jnp.zeros_like(st1)
    st2[...] = jnp.broadcast_to(power_held * 0.125, st2.shape)

    got("dn_yc")
    send("s_yuc", y_u, y_d, "c", sib)
    got("up_yc")
    send("s_ydc", y_d, y_u, "c", sib)
    got("y_oc")
    send("s_yoc", y_o, y_o, "c", sib)
    got("s_yuc", "s_ydc", "s_yoc")

    last = [(b * CB + 256, 128) for b in (y_o, y_u, y_d)]

    @pl.loop(0, 8)
    def _(i):
        cols = pl.ds(pl.multiple_of(i * 256, 256), 256)
        acc[0:FB, cols] += product(0, last, cols)
        for first, n in last:
            add_stats(first, n, cols)
        shift = jnp.sum(st1[:, cols], axis=0, keepdims=True) * (1.0 / (CLIPS * CB))
        power = jnp.sum(st2[:, cols], axis=0, keepdims=True) * (1.0 / (CLIPS * CB))
        mr[0:1, cols] = piv[:, cols] + shift
        mr[1:2, cols] = lax.rsqrt(jnp.maximum(power - shift * shift, 0.0) + EPS)
        m, r = mr[0:1, cols], mr[1:2, cols]
        small = r * (1.0 / math.sqrt(CLIPS * TOK))
        for k in range(0, FB, 64):
            rows = slice(k, k + 64)
            sums = jnp.concatenate([cs[rows], cs[rows]], axis=1)
            err = small * (acc[rows, cols] - sums * m) + bt[rows, cols]
            v = (r * err).astype(BF16)
            vv[rows, cols] = v
            mv = m * v.astype(F32)
            sv[rows, :] += mv[:, :128] + mv[:, 128:]
            sb[rows, :] += err[:, :128] + err[:, 128:]

    sv[...] = jnp.broadcast_to(jnp.sum(sv[...], axis=1, keepdims=True), sv.shape)
    sb[...] = jnp.broadcast_to(jnp.sum(sb[...], axis=1, keepdims=True), sb.shape)

    def grad(block, dst):
        held = slot(block) * CB
        for first, n in ((0, 256), (256, 256), (512, 128)):
            lanes = pl.ds(pl.multiple_of(block * CB + first, 128), n)
            rows = pl.ds(pl.multiple_of(held + first, 128), n)
            part_sum = lax.dot_general(vv[...], at[rows, :], NT, preferred_element_type=F32)
            g = (part_sum - sv[:, 0:1]) * (1.0 + fmod[1:2, lanes]) + sb[:, 0:1] * fmod[0:1, lanes]
            dst[:, first : first + n] = g.astype(dst.dtype)

    P_ROWS, P_A, P_B = slice(0, 192), slice(0, 96), slice(96, 192)
    Q_ROWS, Q_A, Q_B = slice(192, 320), slice(192, 256), slice(256, 320)
    ls = (1 - l, l)

    def add(dst, rows, *terms):
        dst[rows] = sum([t.astype(F32) for t in terms], dst[rows].astype(F32)).astype(dst.dtype)

    def opposite(j):
        grad(xo * 2 + ls[j], g.at[0, j])
        copy(f"or{j}", g.at[0, j, P_A], rpo.at[0, j], right)
        copy(f"ol{j}", g.at[0, j, P_B], rpo.at[1, j], left)

    def next_one(j):
        grad(xr * 2 + ls[j], g.at[1, j])
        copy(f"rr{j}", g.at[1, j, P_B], rpn.at[0, j, P_B], right)
        if j == 0:
            copy("q1", g.at[1, 0, Q_ROWS], ryq.at[1], pair)
        grad(xl * 2 + ls[j], g.at[2, j])
        copy(f"rl{j}", g.at[2, j, P_A], rpn.at[1, j, P_A], left)
        if j == 0:
            copy("q2", g.at[2, 0, Q_ROWS], ryq.at[2], pair)

    def pass_on(j):
        got(f"or{j}")
        add(g.at[1, j], P_A, rpo[0, j])
        copy(f"sr{j}", g.at[1, j, P_A], rpn.at[0, j, P_A], right)
        got(f"ol{j}")
        add(g.at[2, j], P_B, rpo[1, j])
        copy(f"sl{j}", g.at[2, j, P_B], rpn.at[1, j, P_B], left)

    opposite(0)
    copy("q0", g.at[0, 0, Q_ROWS], ryq.at[0], pair)
    opposite(1)
    next_one(0)
    pass_on(0)
    next_one(1)
    got("q0")
    add(g.at[0, 1], Q_ROWS, ryq[0])
    copy("hor", g.at[0, 1, Q_A], rqo.at[0], right)
    copy("hol", g.at[0, 1, Q_B], rqo.at[1], left)
    pass_on(1)

    loads["gen"].wait()
    loads["gate"].wait()

    def teacher(first, last):
        @pl.loop(first, last)
        def _(i):
            cols = pl.ds(pl.multiple_of(i * 256, 256), 256)
            acc[FB:CB, cols] += product(FB, [(5 * CB, 3 * CB)], cols)
            m, r = mr[0:1, cols], mr[1:2, cols]
            for k in range(0, FB, 64):
                rows, more = slice(k, k + 64), slice(FB + k, FB + k + 64)
                own = pl.ds(pl.multiple_of(p * FB + k, 64), 64)

                def twice(ref, where):
                    return jnp.concatenate([ref[where], ref[where]], axis=1)

                fv = r * (acc[rows, cols] - twice(cs, rows) * m) + twice(bw, rows)
                tv = r * (acc[more, cols] - twice(cs, more) * m) + twice(bw, more)
                diff = sigma * (tv - fv)
                acc[more, cols] = diff
                away = jnp.abs(
                    sT[rows, cols].astype(F32) - (at[own, cols].astype(F32) - sigma * tv)
                )
                pushed = diff * gT[rows, cols].astype(F32)
                col[0, rows, :] += away[:, :128] + away[:, 128:]
                col[1, rows, :] += pushed[:, :128] + pushed[:, 128:]

    teacher(0, 8)
    total = jnp.sum(jnp.sum(col[0], axis=0, keepdims=True), axis=1, keepdims=True)
    gap_s[0] = jnp.broadcast_to(total, (8, 128))
    gap_to = (across, on_f(yh, z + 1 - 2 * (z % 2), p), on_f(yh, 3 - z, p), sib)

    def gap_step(k):
        if k:
            got(f"gap{k - 1}")
            gap_s[k] = gap_s[k - 1] + gap_r[k - 1]
        copy(f"gap{k}", gap_s.at[k], gap_r.at[k], gap_to[k])

    gap_step(0)
    grad(x * 2 + ls[0], gown.at[0])
    g[3, 0, Q_ROWS] = gown[0, Q_ROWS].astype(BF16)
    copy("q3", g.at[3, 0, Q_ROWS], ryq.at[3], pair)
    got("q1", "hor")
    add(g.at[1, 1], Q_ROWS, ryq[1])
    add(g.at[1, 1], Q_A, rqo[0])
    copy("hr", g.at[1, 1, Q_ROWS], rqn.at[0], right)
    gap_step(1)
    got("q2", "hol")
    add(g.at[2, 1], Q_ROWS, ryq[2])
    add(g.at[2, 1], Q_B, rqo[1])
    copy("hl", g.at[2, 1, Q_ROWS], rqn.at[1], left)
    gap_step(2)
    got("rr0", "sr0", "rl0", "sl0")
    g[3, 0, P_ROWS] = (
        gown[0, P_ROWS] + rpn[0, 0].astype(F32) + rpn[1, 0].astype(F32)
    ).astype(BF16)
    copy("py", g.at[3, 0, P_ROWS], rpy, pair)
    gap_step(3)
    grad(x * 2 + ls[1], gown.at[1])
    got("gap3")
    total = gap_s[3] + gap_r[3]
    weight = 1.0 / (total[0:1, 0:1] * (1.0 / (TOK * CLIPS * CB)) + EPS)

    same = eye(FB)
    gate_col = jnp.sum(same * gate[...], axis=1, keepdims=True) * weight
    col[0] = jnp.broadcast_to(gate_col, (FB, 128))
    gg_col = jnp.sum(col[1], axis=1, keepdims=True) * weight * (1.0 / math.sqrt(TOK))
    gg_out[...] = jnp.sum(same * gg_col, axis=0, keepdims=True)

    @pl.loop(0, 8)
    def _(i):
        rows = pl.ds(pl.multiple_of(i * 256, 256), 256)
        vv[:, rows] = (col[0, :, 0:1] * acc[FB:CB, rows]).astype(BF16)

    out_bc = pltpu.make_async_copy(vv, bc_out, loc_sems.at[13])
    out_bc.start()

    got("rr1", "sr1", "rl1", "sl1")
    add(gown.at[1], P_ROWS, rpn[0, 1], rpn[1, 1])
    got("q3", "hr", "hl")
    add(gown.at[1], Q_ROWS, ryq[3], rqn[0], rqn[1])
    got("py")
    add(gown.at[1], P_ROWS, rpy[...])
    out_fg = pltpu.make_async_copy(gown.at[1], fg_out, loc_sems.at[14])
    out_fg.start()
    sent(*table)
    out_bc.wait()
    out_fg.wait()


def per_device(
    sample, noise, gen_branch, step, teacher_mod, fake_mod, teacher_weight, fake_weight, gen_gate
):
    hbm = pl.BlockSpec(memory_space=pl.ANY)
    vmem = pl.BlockSpec(memory_space=pltpu.VMEM)
    cot, gate_grad, grad = pl.pallas_call(
        kernel,
        out_shape=(
            jax.ShapeDtypeStruct((FB, TOK), BF16),
            jax.ShapeDtypeStruct((1, FB), F32),
            jax.ShapeDtypeStruct((FB, CB), F32),
        ),
        in_specs=[
            hbm, hbm, hbm, pl.BlockSpec(memory_space=pltpu.SMEM), hbm, hbm, hbm, hbm, hbm,
        ],
        out_specs=(hbm, vmem, hbm),
        scratch_shapes=[
            pltpu.VMEM((CLIPS * CB, TOK), BF16),
            pltpu.VMEM((CB, CLIPS * CB), BF16),
            pltpu.VMEM((CB, TOK), F32),
            pltpu.VMEM((FB, TOK), BF16),
            pltpu.VMEM((FB, TOK), BF16),
            pltpu.VMEM((FB, TOK), BF16),
            pltpu.VMEM((FB, TOK), BF16),
            pltpu.VMEM((FB, TOK), F32),
            pltpu.VMEM((8, TOK), F32),
            pltpu.VMEM((8, TOK), F32),
            pltpu.VMEM((1, TOK), F32),
            pltpu.VMEM((2, TOK), F32),
            pltpu.VMEM((CB, 128), F32),
            pltpu.VMEM((CB, 128), F32),
            pltpu.VMEM((FB, 128), F32),
            pltpu.VMEM((FB, 128), F32),
            pltpu.VMEM((2, FB, 128), F32),
            pltpu.VMEM((2, CLIPS * CB), F32),
            pltpu.VMEM((2, CLIPS * CB), F32),
            pltpu.VMEM((1, FB), F32),
            pltpu.VMEM((4, 2, FB, CB), BF16),
            pltpu.VMEM((2, FB, CB), F32),
            pltpu.VMEM((2, 2, 96, CB), BF16),
            pltpu.VMEM((2, 2, 192, CB), BF16),
            pltpu.VMEM((4, 128, CB), BF16),
            pltpu.VMEM((2, 64, CB), BF16),
            pltpu.VMEM((2, 128, CB), BF16),
            pltpu.VMEM((192, CB), BF16),
            pltpu.VMEM((2, TOK), F32),
            pltpu.VMEM((2, TOK), F32),
            pltpu.VMEM((4, 8, 128), F32),
            pltpu.VMEM((4, 8, 128), F32),
            pltpu.SemaphoreType.DMA((COPIES,)),
            pltpu.SemaphoreType.DMA((COPIES,)),
            pltpu.SemaphoreType.DMA((15,)),
        ],
        compiler_params=pltpu.CompilerParams(
            collective_id=0, has_side_effects=True, vmem_limit_bytes=62 << 20
        ),
        name="step",
    )(
        sample.T, noise.T, gen_branch.T, step,
        teacher_mod.reshape(2, CLIPS * CB), fake_mod.reshape(2, CLIPS * CB),
        teacher_weight.T, fake_weight.T, gen_gate,
    )
    return cot.T, gate_grad, grad.T


def solution(mesh):
    placed = (
        P("clip", "fsdp"),
        P("clip", "fsdp"),
        P("clip", "fsdp"),
        P("clip"),
        P("clip", None, None),
        P("clip", None, None),
        P("clip", "fsdp"),
        P("clip", "fsdp"),
        P("clip", "fsdp"),
    )
    return jax.shard_map(
        per_device,
        mesh=mesh,
        in_specs=placed,
        out_specs=(P("clip", "fsdp"), P("clip", "fsdp"), P("clip", "fsdp")),
        check_vma=False,
    )
```

```python
import functools
import math

import jax
import jax.numpy as jnp
from jax import lax
from jax.experimental import pallas as pl
from jax.experimental.pallas import tpu as pltpu
from jax.sharding import PartitionSpec as P

EPS = 1e-06
F32 = jnp.float32
BF16 = jnp.bfloat16
NT = (((1,), (1,)), ((), ()))

TOK = 2048
FB = 320
CB = 640
CLIPS = 8
COPIES = 80


def eye(n):
    same = lax.broadcasted_iota(jnp.int32, (n, n), 0) == lax.broadcasted_iota(jnp.int32, (n, n), 1)
    return same.astype(F32)


def kernel(
    sample, noise, gen, step, tmod_in, fmod_in, tw, fw, gate_in,
    bc_out, gg_out, fg_out,
    at, wt, acc, sT, nT, gT, vv, bt, st1, st2, piv, mr, cs, bw, sv, sb, col,
    tmod, fmod, gate, g, gown, rpo, rpn, ryq, rqo, rqn, rpy, stat_s, stat_r, gap_s, gap_r,
    send_sems, recv_sems, loc_sems,
):
    clip = lax.axis_index("clip")
    fs = lax.axis_index("fsdp")
    x, l = clip // 2, clip % 2
    p, z, yh = fs % 2, (fs // 2) % 4, fs // 8
    s = 1 - 2 * p
    zu, zd, zo = (z + s + 4) % 4, (z - s + 4) % 4, (z + 2) % 4
    yo = 1 - yh
    xr, xl, xo = (x + 1) % 4, (x + 3) % 4, (x + 2) % 4

    def on_f(y, zz, pp):
        return {"fsdp": (y * 4 + zz) * 2 + pp}

    def on_c(xx, ll):
        return {"clip": xx * 2 + ll}

    up, dn, across, sib = on_f(yh, zu, p), on_f(yh, zd, p), on_f(yo, z, p), on_f(yh, z, 1 - p)
    right, left, pair = on_c(xr, l), on_c(xl, l), on_c(x, 1 - l)
    me, o, u, d, y_me, y_o, y_u, y_d = range(8)

    def slot(block):
        rel = ((block % 4 - z) * s + 8) % 4
        yd = (block // 4 + yh) % 2
        return yd * 4 + (rel % 2) * 2 + rel // 2

    table = {}

    def copy(name, src, dst, to):
        i = len(table)
        assert i < COPIES
        c = pltpu.make_async_remote_copy(
            src_ref=src, dst_ref=dst, send_sem=send_sems.at[i], recv_sem=recv_sems.at[i],
            device_id=to, device_id_type=pl.DeviceIdType.MESH,
        )
        table[name] = [c, False]
        c.start()

    def got(*names):
        for name in names:
            table[name][0].wait_recv()

    def sent(*names):
        for name in names:
            if not table[name][1]:
                table[name][1] = True
                table[name][0].wait_send()

    part = {
        "a": (pl.multiple_of(p * 512, 128), 128),
        "b": (pl.multiple_of(128 + p * 256, 128), 128),
        "c": (pl.multiple_of(256 + p * 64, 64), 64),
        "ab": (pl.multiple_of(p * 384, 128), 256),
        "all": (pl.multiple_of(p * 320, 64), 320),
    }

    def span(block, which):
        first, n = part[which]
        return pl.ds(pl.multiple_of(block * CB + first, 64), n)

    def send(name, here, there, which, to):
        copy(name, at.at[span(here, which), :], at.at[span(there, which), :], to)

    def w_ref(block, half):
        lanes = pl.ds(pl.multiple_of(slot(block) * CB, 128), CB)
        return wt.at[pl.ds(half * FB, FB), lanes]

    def send_w(name, block, half, to):
        copy(name, w_ref(block, half), w_ref(block, half), to)

    loads = {}

    def load(name, src, dst):
        loads[name] = pltpu.make_async_copy(src, dst, loc_sems.at[len(loads)])
        loads[name].start()

    def local(which):
        first, n = part[which]
        return pl.ds(pl.multiple_of(first - p * FB, 64), n)

    def load_part(which):
        load("s" + which, sample.at[local(which), :], sT.at[local(which), :])
        load("n" + which, noise.at[local(which), :], nT.at[local(which), :])

    load_part("a")
    barrier = pltpu.get_barrier_semaphore()
    for to in (up, dn, across, sib, right, left, pair):
        pl.semaphore_signal(barrier, inc=1, device_id=to, device_id_type=pl.DeviceIdType.MESH)
    load_part("b")
    load("fw", fw, w_ref(clip, 0))
    load("tw", tw, w_ref(clip, 1))
    load_part("c")

    frac = jnp.full((8, 128), step[0], jnp.int32).astype(F32) / 1000.0
    sigma = (5.0 * frac / (1.0 + 4.0 * frac))[0:1, 0:1]

    def noised(which):
        loads["s" + which].wait()
        loads["n" + which].wait()
        first, n = part[which]
        own = pl.multiple_of(first - p * FB, 64)

        @pl.loop(0, n // 32)
        def _(i):
            rows = pl.ds(pl.multiple_of(own + i * 32, 32), 32)
            mixed = (1.0 - sigma) * sT[rows, :].astype(F32) + sigma * nT[rows, :].astype(F32)
            at[pl.ds(pl.multiple_of(first + i * 32, 32), 32), :] = mixed.astype(BF16)

    noised("a")
    pl.semaphore_wait(barrier, 7)
    send("up_a", me, d, "a", up)
    noised("b")
    send("dn_b", me, u, "b", dn)
    loads["fw"].wait()
    send_w("pair_f", clip, 0, pair)
    loads["tw"].wait()
    send_w("pair_t", clip, 1, pair)
    send("y_ab", me, y_me, "ab", across)
    send_w("xr_f", clip, 0, right)
    send_w("xl_f", clip, 0, left)
    noised("c")
    send("up_c", me, d, "c", up)
    send("dn_a", me, u, "a", dn)
    send("y_c", me, y_me, "c", across)
    send("s_own", me, me, "all", sib)
    send_w("xr_t", clip, 1, right)
    send_w("xl_t", clip, 1, left)

    w_l, w_r, w_o = xl * 2 + l, xr * 2 + l, xo * 2 + l
    v_me, v_l, v_r, v_o = x * 2 + 1 - l, xl * 2 + 1 - l, xr * 2 + 1 - l, xo * 2 + 1 - l
    everyone = (clip, w_l, w_r, w_o, v_me, v_l, v_r, v_o)

    load("fmod", fmod_in, fmod)
    load("tmod", tmod_in, tmod)
    load("gen", gen, gT)
    load("gate", gate_in, gate)

    @pl.loop(0, 8)
    def _(i):
        cols = pl.ds(pl.multiple_of(i * 256, 256), 256)
        own = at[pl.ds(*part["all"]), cols].astype(F32)
        piv[:, cols] = jnp.sum(own, axis=0, keepdims=True) * (1.0 / FB)
        st1[:, cols] = jnp.zeros((8, 256), F32)
        st2[:, cols] = jnp.zeros((8, 256), F32)

    cs[...] = jnp.zeros_like(cs)
    bw[...] = jnp.zeros_like(bw)
    sv[...] = jnp.zeros_like(sv)
    sb[...] = jnp.zeros_like(sb)
    col[...] = jnp.zeros_like(col)

    def add_stats(first, n, cols):
        v = at[pl.ds(first, n), cols].astype(F32) - piv[:, cols]
        v = v.reshape(n // 8, 8, 256)
        st1[:, cols] += jnp.sum(v, axis=0)
        st2[:, cols] += jnp.sum(v * v, axis=0)

    def stats(block, which):
        first, n = part[which]

        @pl.loop(0, 8)
        def _(i):
            add_stats(pl.multiple_of(block * CB + first, 64), n, pl.ds(pl.multiple_of(i * 256, 256), 256))

    def scale(block, h, mod):
        lanes = pl.ds(pl.multiple_of(block * CB, 128), CB)
        factor = 1.0 + mod[1:2, lanes]
        shift = mod[0:1, lanes]
        held = pl.ds(pl.multiple_of(slot(block) * CB, 128), CB)

        @pl.loop(0, 5)
        def _(i):
            rows = pl.ds(pl.multiple_of(h * FB + i * 64, 64), 64)
            w = wt[rows, held].astype(F32)
            scaled = (w * factor).astype(BF16)
            wt[rows, held] = scaled
            back, moved = scaled.astype(F32), w * shift
            cs[rows, :] += sum(back[:, k : k + 128] for k in range(0, CB, 128))
            bw[rows, :] += sum(moved[:, k : k + 128] for k in range(0, CB, 128))

    def scale_all(h, mod):
        for block in everyone:
            scale(block, h, mod)
        rows = slice(h * FB, h * FB + FB)
        for ref in (cs, bw):
            ref[rows] = jnp.broadcast_to(jnp.sum(ref[rows], axis=1, keepdims=True), (FB, 128))

    def product(top, spans, cols):
        left_side = [wt[top : top + FB, i : i + n] for i, n in spans]
        right_side = [at[i : i + n, cols] for i, n in spans]
        return jnp.dot(
            jnp.concatenate(left_side, axis=1) if len(spans) > 1 else left_side[0],
            jnp.concatenate(right_side, axis=0) if len(spans) > 1 else right_side[0],
            preferred_element_type=F32,
        )

    def forward(spans, fresh=False, top=0):
        @pl.loop(0, 2)
        def _(i):
            cols = pl.ds(pl.multiple_of(i * 1024, 1024), 1024)
            if fresh:
                acc[top : top + FB, cols] = product(top, spans, cols)
            else:
                acc[top : top + FB, cols] += product(top, spans, cols)

    got("xr_f")
    send_w("xr_of", w_l, 0, right)
    got("up_a")
    send("up_oa", d, o, "a", up)
    got("dn_b")
    send("dn_ob", u, o, "b", dn)
    send("dn_c", me, u, "c", dn)
    got("pair_f")
    send_w("xr_vf", v_me, 0, right)
    send_w("xl_vf", v_me, 0, left)
    got("up_c")
    send("up_oc", d, o, "c", up)
    send("up_b", me, d, "b", up)
    got("pair_t")
    send_w("xr_vt", v_me, 1, right)
    stats(me, "all")
    got("xl_vf")
    send_w("xl_vof", v_r, 0, left)
    send_w("xl_vt", v_me, 1, left)
    got("xl_t")
    send_w("xl_ot", w_r, 1, left)
    got("up_oa")
    send("y_oa", o, y_o, "a", across)
    got("dn_ob")
    send("y_ob", o, y_o, "b", across)
    got("up_oc")
    send("y_oc", o, y_o, "c", across)
    send("s_o", o, o, "all", sib)
    got("xl_f", "xr_of", "xr_vf", "xl_vof")
    sent("xr_f", "xl_f", "pair_f", "xr_of", "xr_vf", "xl_vf", "xl_vof")
    loads["fmod"].wait()
    scale_all(0, fmod)
    got("y_ab")
    send("up_yab", y_me, y_d, "ab", up)
    send("dn_yab", y_me, y_u, "ab", dn)

    @pl.loop(0, 8)
    def _(i):
        cols = pl.ds(pl.multiple_of(i * 256, 256), 256)
        for k in range(0, FB, 64):
            rows = slice(k, k + 64)
            base = jnp.concatenate([bw[rows], bw[rows]], axis=1)
            target = nT[rows, cols].astype(F32) - sT[rows, cols].astype(F32)
            bt[rows, cols] = (base - target) * (1.0 / math.sqrt(CLIPS * TOK))

    got("s_own", "s_o")
    forward([(0, 2 * CB)], fresh=True)
    got("xr_vt")
    send_w("xr_vot", v_l, 1, right)
    got("dn_a", "dn_c")
    send("s_u", u, d, "all", sib)
    stats(o, "all")
    got("up_b")
    send("s_d", d, u, "all", sib)
    got("y_c")
    send("up_yc", y_me, y_d, "c", up)
    send("dn_yc", y_me, y_u, "c", dn)
    send("s_y", y_me, y_me, "all", sib)
    stats(u, "all")
    stats(d, "all")
    got("s_d", "s_u", "s_y")
    forward([(2 * CB, 3 * CB)])
    stats(y_me, "all")
    got("xr_t", "xl_ot", "xl_vt", "xr_vot")
    sent("xr_t", "xl_t", "pair_t", "xl_ot", "xr_vt", "xl_vt", "xr_vot")
    loads["tmod"].wait()
    scale_all(1, tmod)
    forward([(0, 5 * CB)], True, FB)
    got("dn_yab")
    send("s_yu", y_u, y_d, "ab", sib)
    got("up_yab")
    send("s_yd", y_d, y_u, "ab", sib)
    stats(y_u, "ab")
    stats(y_d, "ab")
    got("s_yd", "s_yu")
    forward([(b * CB + k, 256) for b in (y_u, y_d) for k in (0, 384)])
    got("y_oa", "y_ob")
    send("s_yo", y_o, y_o, "ab", sib)
    stats(y_o, "ab")

    held = 5 * FB + 3 * 256
    shift = jnp.sum(st1[...], axis=0, keepdims=True)
    stat_s[0:1, :] = piv[...] + shift * (1.0 / held)
    stat_s[1:2, :] = jnp.sum(st2[...], axis=0, keepdims=True) - shift * shift * (1.0 / held)
    copy("stat", stat_s, stat_r, sib)
    got("s_yo")
    forward([(y_o * CB + k, 256) for k in (0, 384)])
    got("stat")
    apart = stat_s[0:1, :] - stat_r[0:1, :]
    piv[...] = 0.5 * (stat_s[0:1, :] + stat_r[0:1, :])
    power_held = stat_s[1:2, :] + stat_r[1:2, :] + apart * apart * (held / 2)
    st1[...] = jnp.zeros_like(st1)
    st2[...] = jnp.broadcast_to(power_held * 0.125, st2.shape)

    got("dn_yc")
    send("s_yuc", y_u, y_d, "c", sib)
    got("up_yc")
    send("s_ydc", y_d, y_u, "c", sib)
    got("y_oc")
    send("s_yoc", y_o, y_o, "c", sib)
    got("s_yuc", "s_ydc", "s_yoc")

    last = [(b * CB + 256, 128) for b in (y_o, y_u, y_d)]

    @pl.loop(0, 8)
    def _(i):
        cols = pl.ds(pl.multiple_of(i * 256, 256), 256)
        acc[0:FB, cols] += product(0, last, cols)
        for first, n in last:
            add_stats(first, n, cols)
        shift = jnp.sum(st1[:, cols], axis=0, keepdims=True) * (1.0 / (CLIPS * CB))
        power = jnp.sum(st2[:, cols], axis=0, keepdims=True) * (1.0 / (CLIPS * CB))
        mr[0:1, cols] = piv[:, cols] + shift
        mr[1:2, cols] = lax.rsqrt(jnp.maximum(power - shift * shift, 0.0) + EPS)
        m, r = mr[0:1, cols], mr[1:2, cols]
        small = r * (1.0 / math.sqrt(CLIPS * TOK))
        for k in range(0, FB, 64):
            rows = slice(k, k + 64)
            sums = jnp.concatenate([cs[rows], cs[rows]], axis=1)
            err = small * (acc[rows, cols] - sums * m) + bt[rows, cols]
            v = (r * err).astype(BF16)
            vv[rows, cols] = v
            mv = m * v.astype(F32)
            sv[rows, :] += mv[:, :128] + mv[:, 128:]
            sb[rows, :] += err[:, :128] + err[:, 128:]

    sv[...] = jnp.broadcast_to(jnp.sum(sv[...], axis=1, keepdims=True), sv.shape)
    sb[...] = jnp.broadcast_to(jnp.sum(sb[...], axis=1, keepdims=True), sb.shape)

    def grad(block, dst):
        held = slot(block) * CB
        for first, n in ((0, 256), (256, 256), (512, 128)):
            lanes = pl.ds(pl.multiple_of(block * CB + first, 128), n)
            rows = pl.ds(pl.multiple_of(held + first, 128), n)
            part_sum = lax.dot_general(vv[...], at[rows, :], NT, preferred_element_type=F32)
            g = (part_sum - sv[:, 0:1]) * (1.0 + fmod[1:2, lanes]) + sb[:, 0:1] * fmod[0:1, lanes]
            dst[:, first : first + n] = g.astype(dst.dtype)

    P_ROWS, P_A, P_B = slice(0, 176), slice(0, 96), slice(96, 176)
    Q_ROWS, Q_A, Q_B = slice(176, 320), slice(176, 240), slice(240, 320)
    ls = (1 - l, l)

    def add(dst, rows, *terms):
        dst[rows] = sum([t.astype(F32) for t in terms], dst[rows].astype(F32)).astype(dst.dtype)

    def opposite(j):
        grad(xo * 2 + ls[j], g.at[0, j])
        copy(f"or{j}", g.at[0, j, P_A], rpo.at[0, j], right)
        copy(f"ol{j}", g.at[0, j, P_B], rpo.at[1, j, 0:80], left)

    def next_one(j):
        grad(xr * 2 + ls[j], g.at[1, j])
        copy(f"rr{j}", g.at[1, j, P_B], rpn.at[0, j, P_B], right)
        if j == 0:
            copy("q1", g.at[1, 0, Q_ROWS], ryq.at[1], pair)
        grad(xl * 2 + ls[j], g.at[2, j])
        copy(f"rl{j}", g.at[2, j, P_A], rpn.at[1, j, P_A], left)
        if j == 0:
            copy("q2", g.at[2, 0, Q_ROWS], ryq.at[2], pair)

    def pass_on(j):
        got(f"or{j}")
        add(g.at[1, j], P_A, rpo[0, j])
        copy(f"sr{j}", g.at[1, j, P_A], rpn.at[0, j, P_A], right)
        got(f"ol{j}")
        add(g.at[2, j], P_B, rpo[1, j, 0:80])
        copy(f"sl{j}", g.at[2, j, P_B], rpn.at[1, j, P_B], left)

    opposite(0)
    copy("q0", g.at[0, 0, Q_ROWS], ryq.at[0], pair)
    opposite(1)
    next_one(0)
    pass_on(0)
    next_one(1)
    got("q0")
    add(g.at[0, 1], Q_ROWS, ryq[0])
    copy("hor", g.at[0, 1, Q_A], rqo.at[0, 0:64], right)
    copy("hol", g.at[0, 1, Q_B], rqo.at[1], left)
    pass_on(1)

    loads["gen"].wait()
    loads["gate"].wait()

    def teacher():
        forward([(5 * CB, 3 * CB)], False, FB)

        @pl.loop(0, 8)
        def _(i):
            cols = pl.ds(pl.multiple_of(i * 256, 256), 256)
            m, r = mr[0:1, cols], mr[1:2, cols]
            for k in range(0, FB, 64):
                rows, more = slice(k, k + 64), slice(FB + k, FB + k + 64)
                own = pl.ds(pl.multiple_of(p * FB + k, 64), 64)

                def twice(ref, where):
                    return jnp.concatenate([ref[where], ref[where]], axis=1)

                fv = r * (acc[rows, cols] - twice(cs, rows) * m) + twice(bw, rows)
                tv = r * (acc[more, cols] - twice(cs, more) * m) + twice(bw, more)
                diff = sigma * (tv - fv)
                acc[more, cols] = diff
                away = jnp.abs(
                    sT[rows, cols].astype(F32) - (at[own, cols].astype(F32) - sigma * tv)
                )
                pushed = diff * gT[rows, cols].astype(F32)
                col[0, rows, :] += away[:, :128] + away[:, 128:]
                col[1, rows, :] += pushed[:, :128] + pushed[:, 128:]

    teacher()
    total = jnp.sum(jnp.sum(col[0], axis=0, keepdims=True), axis=1, keepdims=True)
    gap_s[0] = jnp.broadcast_to(total, (8, 128))
    gap_to = (across, on_f(yh, z + 1 - 2 * (z % 2), p), on_f(yh, 3 - z, p), sib)

    def gap_step(k):
        if k:
            got(f"gap{k - 1}")
            gap_s[k] = gap_s[k - 1] + gap_r[k - 1]
        copy(f"gap{k}", gap_s.at[k], gap_r.at[k], gap_to[k])

    gap_step(0)
    grad(x * 2 + ls[0], gown.at[0])
    g[3, 0, Q_ROWS] = gown[0, Q_ROWS].astype(BF16)
    copy("q3", g.at[3, 0, Q_ROWS], ryq.at[3], pair)
    got("q1", "hor")
    add(g.at[1, 1], Q_ROWS, ryq[1])
    add(g.at[1, 1], Q_A, rqo[0, 0:64])
    copy("hr", g.at[1, 1, Q_ROWS], rqn.at[0], right)
    gap_step(1)
    got("q2", "hol")
    add(g.at[2, 1], Q_ROWS, ryq[2])
    add(g.at[2, 1], Q_B, rqo[1])
    copy("hl", g.at[2, 1, Q_ROWS], rqn.at[1], left)
    gap_step(2)
    got("rr0", "sr0", "rl0", "sl0")
    g[3, 0, P_ROWS] = (
        gown[0, P_ROWS] + rpn[0, 0].astype(F32) + rpn[1, 0].astype(F32)
    ).astype(BF16)
    copy("py", g.at[3, 0, P_ROWS], rpy, pair)
    gap_step(3)
    grad(x * 2 + ls[1], gown.at[1])
    got("gap3")
    total = gap_s[3] + gap_r[3]
    weight = 1.0 / (total[0:1, 0:1] * (1.0 / (TOK * CLIPS * CB)) + EPS)

    same = eye(FB)
    gate_col = jnp.sum(same * gate[...], axis=1, keepdims=True) * weight
    col[0] = jnp.broadcast_to(gate_col, (FB, 128))
    gg_col = jnp.sum(col[1], axis=1, keepdims=True) * weight * (1.0 / math.sqrt(TOK))
    gg_out[...] = jnp.sum(same * gg_col, axis=0, keepdims=True)

    @pl.loop(0, 8)
    def _(i):
        rows = pl.ds(pl.multiple_of(i * 256, 256), 256)
        vv[:, rows] = (col[0, :, 0:1] * acc[FB:CB, rows]).astype(BF16)

    out_bc = pltpu.make_async_copy(vv, bc_out, loc_sems.at[13])
    out_bc.start()

    got("rr1", "sr1", "rl1", "sl1")
    add(gown.at[1], P_ROWS, rpn[0, 1], rpn[1, 1])
    got("q3", "hr", "hl")
    add(gown.at[1], Q_ROWS, ryq[3], rqn[0], rqn[1])
    got("py")
    add(gown.at[1], P_ROWS, rpy[...])
    out_fg = pltpu.make_async_copy(gown.at[1], fg_out, loc_sems.at[14])
    out_fg.start()
    sent(*table)
    out_bc.wait()
    out_fg.wait()


def hand_over(cot, gate_grad, grad, cot_out, gate_grad_out, grad_out, a, b, c, in_sems, out_sems):
    pieces = [(gate_grad, b, gate_grad_out)]
    for k in range(0, FB, 160):
        rows = pl.ds(k, 160)
        pieces.append((cot.at[rows], a.at[rows], cot_out.at[rows]))
        pieces.append((grad.at[rows], c.at[rows], grad_out.at[rows]))
    first = [pltpu.make_async_copy(x, y, in_sems.at[i]) for i, (x, y, _) in enumerate(pieces)]
    second = [pltpu.make_async_copy(y, z, out_sems.at[i]) for i, (_, y, z) in enumerate(pieces)]
    for one in first:
        one.start()
    for one, two in zip(first, second):
        one.wait()
        two.start()
    for two in second:
        two.wait()


def per_device(
    sample, noise, gen_branch, step, teacher_mod, fake_mod, teacher_weight, fake_weight, gen_gate
):
    hbm = pl.BlockSpec(memory_space=pl.ANY)
    vmem = pl.BlockSpec(memory_space=pltpu.VMEM)
    cot, gate_grad, grad = pl.pallas_call(
        kernel,
        out_shape=(
            jax.ShapeDtypeStruct((FB, TOK), BF16),
            jax.ShapeDtypeStruct((1, FB), F32),
            jax.ShapeDtypeStruct((FB, CB), F32),
        ),
        in_specs=[
            hbm, hbm, hbm, pl.BlockSpec(memory_space=pltpu.SMEM), hbm, hbm, hbm, hbm, hbm,
        ],
        out_specs=(hbm, vmem, hbm),
        scratch_shapes=[
            pltpu.VMEM((CLIPS * CB, TOK), BF16),
            pltpu.VMEM((CB, CLIPS * CB), BF16),
            pltpu.VMEM((CB, TOK), F32),
            pltpu.VMEM((FB, TOK), BF16),
            pltpu.VMEM((FB, TOK), BF16),
            pltpu.VMEM((FB, TOK), BF16),
            pltpu.VMEM((FB, TOK), BF16),
            pltpu.VMEM((FB, TOK), F32),
            pltpu.VMEM((8, TOK), F32),
            pltpu.VMEM((8, TOK), F32),
            pltpu.VMEM((1, TOK), F32),
            pltpu.VMEM((2, TOK), F32),
            pltpu.VMEM((CB, 128), F32),
            pltpu.VMEM((CB, 128), F32),
            pltpu.VMEM((FB, 128), F32),
            pltpu.VMEM((FB, 128), F32),
            pltpu.VMEM((2, FB, 128), F32),
            pltpu.VMEM((2, CLIPS * CB), F32),
            pltpu.VMEM((2, CLIPS * CB), F32),
            pltpu.VMEM((1, FB), F32),
            pltpu.VMEM((4, 2, FB, CB), BF16),
            pltpu.VMEM((2, FB, CB), F32),
            pltpu.VMEM((2, 2, 96, CB), BF16),
            pltpu.VMEM((2, 2, 176, CB), BF16),
            pltpu.VMEM((4, 144, CB), BF16),
            pltpu.VMEM((2, 80, CB), BF16),
            pltpu.VMEM((2, 144, CB), BF16),
            pltpu.VMEM((176, CB), BF16),
            pltpu.VMEM((2, TOK), F32),
            pltpu.VMEM((2, TOK), F32),
            pltpu.VMEM((4, 8, 128), F32),
            pltpu.VMEM((4, 8, 128), F32),
            pltpu.SemaphoreType.DMA((COPIES,)),
            pltpu.SemaphoreType.DMA((COPIES,)),
            pltpu.SemaphoreType.DMA((15,)),
        ],
        compiler_params=pltpu.CompilerParams(
            collective_id=0, has_side_effects=True, vmem_limit_bytes=62 << 20
        ),
        name="step",
    )(
        sample.T, noise.T, gen_branch.T, step,
        teacher_mod.reshape(2, CLIPS * CB), fake_mod.reshape(2, CLIPS * CB),
        teacher_weight.T, fake_weight.T, gen_gate,
    )
    cot, gate_grad, grad = pl.pallas_call(
        hand_over,
        out_shape=(
            jax.ShapeDtypeStruct((FB, TOK), BF16),
            jax.ShapeDtypeStruct((1, FB), F32),
            jax.ShapeDtypeStruct((FB, CB), F32),
        ),
        in_specs=[hbm] * 3,
        out_specs=(hbm,) * 3,
        scratch_shapes=[
            pltpu.VMEM((FB, TOK), BF16),
            pltpu.VMEM((1, FB), F32),
            pltpu.VMEM((FB, CB), F32),
            pltpu.SemaphoreType.DMA((5,)),
            pltpu.SemaphoreType.DMA((5,)),
        ],
        compiler_params=pltpu.CompilerParams(vmem_limit_bytes=60 << 20),
        name="hand_over",
    )(cot, gate_grad, grad)
    return cot.T, gate_grad, grad.T


def solution(mesh):
    placed = (
        P("clip", "fsdp"),
        P("clip", "fsdp"),
        P("clip", "fsdp"),
        P("clip"),
        P("clip", None, None),
        P("clip", None, None),
        P("clip", "fsdp"),
        P("clip", "fsdp"),
        P("clip", "fsdp"),
    )
    return jax.shard_map(
        per_device,
        mesh=mesh,
        in_specs=placed,
        out_specs=(P("clip", "fsdp"), P("clip", "fsdp"), P("clip", "fsdp")),
        check_vma=False,
    )
```

```python
import functools
import math

import jax
import jax.numpy as jnp
from jax import lax
from jax.experimental import pallas as pl
from jax.experimental.pallas import tpu as pltpu
from jax.sharding import PartitionSpec as P

EPS = 1e-06
F32 = jnp.float32
BF16 = jnp.bfloat16
NT = (((1,), (1,)), ((), ()))

TOK = 2048
FB = 320
CB = 640
CLIPS = 8
COPIES = 80


def eye(n):
    same = lax.broadcasted_iota(jnp.int32, (n, n), 0) == lax.broadcasted_iota(jnp.int32, (n, n), 1)
    return same.astype(F32)


def kernel(
    sample, noise, gen, step, tmod_in, fmod_in, tw, fw, gate_in,
    bc_out, gc_out, gg_out, fg_out,
    at, wt, acc, sT, nT, gT, vv, bt, st1, st2, piv, mr, cs, bw, sv, sb, col,
    tmod, fmod, gate, g, gown, rpo, rpn, ryq, rqo, rqn, rpy, stat_s, stat_r, gap_s, gap_r,
    send_sems, recv_sems, loc_sems,
):
    clip = lax.axis_index("clip")
    fs = lax.axis_index("fsdp")
    x, l = clip // 2, clip % 2
    p, z, yh = fs % 2, (fs // 2) % 4, fs // 8
    s = 1 - 2 * p
    zu, zd, zo = (z + s + 4) % 4, (z - s + 4) % 4, (z + 2) % 4
    yo = 1 - yh
    xr, xl, xo = (x + 1) % 4, (x + 3) % 4, (x + 2) % 4

    def on_f(y, zz, pp):
        return {"fsdp": (y * 4 + zz) * 2 + pp}

    def on_c(xx, ll):
        return {"clip": xx * 2 + ll}

    up, dn, across, sib = on_f(yh, zu, p), on_f(yh, zd, p), on_f(yo, z, p), on_f(yh, z, 1 - p)
    right, left, pair = on_c(xr, l), on_c(xl, l), on_c(x, 1 - l)
    me, o, u, d, y_me, y_o, y_u, y_d = range(8)

    def slot(block):
        rel = ((block % 4 - z) * s + 8) % 4
        yd = (block // 4 + yh) % 2
        return yd * 4 + (rel % 2) * 2 + rel // 2

    table = {}

    def copy(name, src, dst, to):
        i = len(table)
        assert i < COPIES
        c = pltpu.make_async_remote_copy(
            src_ref=src, dst_ref=dst, send_sem=send_sems.at[i], recv_sem=recv_sems.at[i],
            device_id=to, device_id_type=pl.DeviceIdType.MESH,
        )
        table[name] = [c, False]
        c.start()

    def got(*names):
        for name in names:
            table[name][0].wait_recv()

    def sent(*names):
        for name in names:
            if not table[name][1]:
                table[name][1] = True
                table[name][0].wait_send()

    part = {
        "a": (pl.multiple_of(p * 512, 128), 128),
        "b": (pl.multiple_of(128 + p * 256, 128), 128),
        "c": (pl.multiple_of(256 + p * 64, 64), 64),
        "ab": (pl.multiple_of(p * 384, 128), 256),
        "all": (pl.multiple_of(p * 320, 64), 320),
    }

    def span(block, which):
        first, n = part[which]
        return pl.ds(pl.multiple_of(block * CB + first, 64), n)

    def send(name, here, there, which, to):
        copy(name, at.at[span(here, which), :], at.at[span(there, which), :], to)

    def w_ref(block, half):
        lanes = pl.ds(pl.multiple_of(slot(block) * CB, 128), CB)
        return wt.at[pl.ds(half * FB, FB), lanes]

    def send_w(name, block, half, to):
        copy(name, w_ref(block, half), w_ref(block, half), to)

    loads = {}

    def load(name, src, dst):
        loads[name] = pltpu.make_async_copy(src, dst, loc_sems.at[len(loads)])
        loads[name].start()

    def local(which):
        first, n = part[which]
        return pl.ds(pl.multiple_of(first - p * FB, 64), n)

    def load_part(which):
        load("s" + which, sample.at[local(which), :], sT.at[local(which), :])
        load("n" + which, noise.at[local(which), :], nT.at[local(which), :])

    load_part("a")
    barrier = pltpu.get_barrier_semaphore()
    for to in (up, dn, across, sib, right, left, pair):
        pl.semaphore_signal(barrier, inc=1, device_id=to, device_id_type=pl.DeviceIdType.MESH)
    load_part("b")
    load("fw", fw, w_ref(clip, 0))
    load("tw", tw, w_ref(clip, 1))
    load_part("c")

    frac = jnp.full((8, 128), step[0], jnp.int32).astype(F32) / 1000.0
    sigma = (5.0 * frac / (1.0 + 4.0 * frac))[0:1, 0:1]

    def noised(which):
        loads["s" + which].wait()
        loads["n" + which].wait()
        first, n = part[which]
        own = pl.multiple_of(first - p * FB, 64)

        @pl.loop(0, n // 32)
        def _(i):
            rows = pl.ds(pl.multiple_of(own + i * 32, 32), 32)
            mixed = (1.0 - sigma) * sT[rows, :].astype(F32) + sigma * nT[rows, :].astype(F32)
            at[pl.ds(pl.multiple_of(first + i * 32, 32), 32), :] = mixed.astype(BF16)

    noised("a")
    pl.semaphore_wait(barrier, 7)
    send("up_a", me, d, "a", up)
    noised("b")
    send("dn_b", me, u, "b", dn)
    loads["fw"].wait()
    send_w("pair_f", clip, 0, pair)
    loads["tw"].wait()
    send_w("pair_t", clip, 1, pair)
    send("y_ab", me, y_me, "ab", across)
    send_w("xr_f", clip, 0, right)
    send_w("xl_f", clip, 0, left)
    noised("c")
    send("up_c", me, d, "c", up)
    send("dn_a", me, u, "a", dn)
    send("y_c", me, y_me, "c", across)
    send("s_own", me, me, "all", sib)
    send_w("xr_t", clip, 1, right)
    send_w("xl_t", clip, 1, left)

    w_l, w_r, w_o = xl * 2 + l, xr * 2 + l, xo * 2 + l
    v_me, v_l, v_r, v_o = x * 2 + 1 - l, xl * 2 + 1 - l, xr * 2 + 1 - l, xo * 2 + 1 - l
    everyone = (clip, w_l, w_r, w_o, v_me, v_l, v_r, v_o)

    load("fmod", fmod_in, fmod)
    load("tmod", tmod_in, tmod)
    load("gen", gen, gT)
    load("gate", gate_in, gate)

    @pl.loop(0, 8)
    def _(i):
        cols = pl.ds(pl.multiple_of(i * 256, 256), 256)
        own = at[pl.ds(*part["all"]), cols].astype(F32)
        piv[:, cols] = jnp.sum(own, axis=0, keepdims=True) * (1.0 / FB)
        st1[:, cols] = jnp.zeros((8, 256), F32)
        st2[:, cols] = jnp.zeros((8, 256), F32)

    cs[...] = jnp.zeros_like(cs)
    bw[...] = jnp.zeros_like(bw)
    sv[...] = jnp.zeros_like(sv)
    sb[...] = jnp.zeros_like(sb)
    col[...] = jnp.zeros_like(col)

    def add_stats(first, n, cols):
        v = at[pl.ds(first, n), cols].astype(F32) - piv[:, cols]
        v = v.reshape(n // 8, 8, 256)
        st1[:, cols] += jnp.sum(v, axis=0)
        st2[:, cols] += jnp.sum(v * v, axis=0)

    def stats(block, which):
        first, n = part[which]

        @pl.loop(0, 8)
        def _(i):
            add_stats(pl.multiple_of(block * CB + first, 64), n, pl.ds(pl.multiple_of(i * 256, 256), 256))

    def scale(block, h, mod):
        lanes = pl.ds(pl.multiple_of(block * CB, 128), CB)
        factor = 1.0 + mod[1:2, lanes]
        shift = mod[0:1, lanes]
        held = pl.ds(pl.multiple_of(slot(block) * CB, 128), CB)

        @pl.loop(0, 5)
        def _(i):
            rows = pl.ds(pl.multiple_of(h * FB + i * 64, 64), 64)
            w = wt[rows, held].astype(F32)
            scaled = (w * factor).astype(BF16)
            wt[rows, held] = scaled
            back, moved = scaled.astype(F32), w * shift
            cs[rows, :] += sum(back[:, k : k + 128] for k in range(0, CB, 128))
            bw[rows, :] += sum(moved[:, k : k + 128] for k in range(0, CB, 128))

    def scale_all(h, mod):
        for block in everyone:
            scale(block, h, mod)
        rows = slice(h * FB, h * FB + FB)
        for ref in (cs, bw):
            ref[rows] = jnp.broadcast_to(jnp.sum(ref[rows], axis=1, keepdims=True), (FB, 128))

    def product(top, spans, cols):
        left_side = [wt[top : top + FB, i : i + n] for i, n in spans]
        right_side = [at[i : i + n, cols] for i, n in spans]
        return jnp.dot(
            jnp.concatenate(left_side, axis=1) if len(spans) > 1 else left_side[0],
            jnp.concatenate(right_side, axis=0) if len(spans) > 1 else right_side[0],
            preferred_element_type=F32,
        )

    def forward(spans, fresh=False, top=0):
        @pl.loop(0, 2)
        def _(i):
            cols = pl.ds(pl.multiple_of(i * 1024, 1024), 1024)
            if fresh:
                acc[top : top + FB, cols] = product(top, spans, cols)
            else:
                acc[top : top + FB, cols] += product(top, spans, cols)

    got("xr_f")
    send_w("xr_of", w_l, 0, right)
    got("up_a")
    send("up_oa", d, o, "a", up)
    got("dn_b")
    send("dn_ob", u, o, "b", dn)
    send("dn_c", me, u, "c", dn)
    got("pair_f")
    send_w("xr_vf", v_me, 0, right)
    send_w("xl_vf", v_me, 0, left)
    got("up_c")
    send("up_oc", d, o, "c", up)
    send("up_b", me, d, "b", up)
    got("pair_t")
    send_w("xr_vt", v_me, 1, right)
    stats(me, "all")
    got("xl_vf")
    send_w("xl_vof", v_r, 0, left)
    send_w("xl_vt", v_me, 1, left)
    got("xl_t")
    send_w("xl_ot", w_r, 1, left)
    got("up_oa")
    send("y_oa", o, y_o, "a", across)
    got("dn_ob")
    send("y_ob", o, y_o, "b", across)
    got("up_oc")
    send("y_oc", o, y_o, "c", across)
    send("s_o", o, o, "all", sib)
    got("xl_f", "xr_of", "xr_vf", "xl_vof")
    sent("xr_f", "xl_f", "pair_f", "xr_of", "xr_vf", "xl_vf", "xl_vof")
    loads["fmod"].wait()
    scale_all(0, fmod)
    got("y_ab")
    send("up_yab", y_me, y_d, "ab", up)
    send("dn_yab", y_me, y_u, "ab", dn)

    @pl.loop(0, 8)
    def _(i):
        cols = pl.ds(pl.multiple_of(i * 256, 256), 256)
        for k in range(0, FB, 64):
            rows = slice(k, k + 64)
            base = jnp.concatenate([bw[rows], bw[rows]], axis=1)
            target = nT[rows, cols].astype(F32) - sT[rows, cols].astype(F32)
            bt[rows, cols] = (base - target) * (1.0 / math.sqrt(CLIPS * TOK))

    got("s_own", "s_o")
    forward([(0, 2 * CB)], fresh=True)
    got("xr_vt")
    send_w("xr_vot", v_l, 1, right)
    got("dn_a", "dn_c")
    send("s_u", u, d, "all", sib)
    stats(o, "all")
    got("up_b")
    send("s_d", d, u, "all", sib)
    got("y_c")
    send("up_yc", y_me, y_d, "c", up)
    send("dn_yc", y_me, y_u, "c", dn)
    send("s_y", y_me, y_me, "all", sib)
    stats(u, "all")
    stats(d, "all")
    got("s_d", "s_u", "s_y")
    forward([(2 * CB, 3 * CB)])
    stats(y_me, "all")
    got("xr_t", "xl_ot", "xl_vt", "xr_vot")
    sent("xr_t", "xl_t", "pair_t", "xl_ot", "xr_vt", "xl_vt", "xr_vot")
    loads["tmod"].wait()
    scale_all(1, tmod)
    forward([(0, 5 * CB)], True, FB)
    got("dn_yab")
    send("s_yu", y_u, y_d, "ab", sib)
    got("up_yab")
    send("s_yd", y_d, y_u, "ab", sib)
    stats(y_u, "ab")
    stats(y_d, "ab")
    got("s_yd", "s_yu")
    forward([(b * CB + k, 256) for b in (y_u, y_d) for k in (0, 384)])
    got("y_oa", "y_ob")
    send("s_yo", y_o, y_o, "ab", sib)
    stats(y_o, "ab")

    held = 5 * FB + 3 * 256
    shift = jnp.sum(st1[...], axis=0, keepdims=True)
    stat_s[0:1, :] = piv[...] + shift * (1.0 / held)
    stat_s[1:2, :] = jnp.sum(st2[...], axis=0, keepdims=True) - shift * shift * (1.0 / held)
    copy("stat", stat_s, stat_r, sib)
    got("s_yo")
    forward([(y_o * CB + k, 256) for k in (0, 384)])
    got("stat")
    apart = stat_s[0:1, :] - stat_r[0:1, :]
    piv[...] = 0.5 * (stat_s[0:1, :] + stat_r[0:1, :])
    power_held = stat_s[1:2, :] + stat_r[1:2, :] + apart * apart * (held / 2)
    st1[...] = jnp.zeros_like(st1)
    st2[...] = jnp.broadcast_to(power_held * 0.125, st2.shape)

    got("dn_yc")
    send("s_yuc", y_u, y_d, "c", sib)
    got("up_yc")
    send("s_ydc", y_d, y_u, "c", sib)
    got("y_oc")
    send("s_yoc", y_o, y_o, "c", sib)
    got("s_yuc", "s_ydc", "s_yoc")

    last = [(b * CB + 256, 128) for b in (y_o, y_u, y_d)]

    @pl.loop(0, 8)
    def _(i):
        cols = pl.ds(pl.multiple_of(i * 256, 256), 256)
        acc[0:FB, cols] += product(0, last, cols)
        for first, n in last:
            add_stats(first, n, cols)
        shift = jnp.sum(st1[:, cols], axis=0, keepdims=True) * (1.0 / (CLIPS * CB))
        power = jnp.sum(st2[:, cols], axis=0, keepdims=True) * (1.0 / (CLIPS * CB))
        mr[0:1, cols] = piv[:, cols] + shift
        mr[1:2, cols] = lax.rsqrt(jnp.maximum(power - shift * shift, 0.0) + EPS)
        m, r = mr[0:1, cols], mr[1:2, cols]
        small = r * (1.0 / math.sqrt(CLIPS * TOK))
        for k in range(0, FB, 64):
            rows = slice(k, k + 64)
            sums = jnp.concatenate([cs[rows], cs[rows]], axis=1)
            err = small * (acc[rows, cols] - sums * m) + bt[rows, cols]
            v = (r * err).astype(BF16)
            vv[rows, cols] = v
            mv = m * v.astype(F32)
            sv[rows, :] += mv[:, :128] + mv[:, 128:]
            sb[rows, :] += err[:, :128] + err[:, 128:]

    sv[...] = jnp.broadcast_to(jnp.sum(sv[...], axis=1, keepdims=True), sv.shape)
    sb[...] = jnp.broadcast_to(jnp.sum(sb[...], axis=1, keepdims=True), sb.shape)

    def grad(block, dst):
        held = slot(block) * CB
        for first, n in ((0, 256), (256, 256), (512, 128)):
            lanes = pl.ds(pl.multiple_of(block * CB + first, 128), n)
            rows = pl.ds(pl.multiple_of(held + first, 128), n)
            part_sum = lax.dot_general(vv[...], at[rows, :], NT, preferred_element_type=F32)
            g = (part_sum - sv[:, 0:1]) * (1.0 + fmod[1:2, lanes]) + sb[:, 0:1] * fmod[0:1, lanes]
            dst[:, first : first + n] = g.astype(dst.dtype)

    P_ROWS, P_A, P_B = slice(0, 176), slice(0, 96), slice(96, 176)
    Q_ROWS, Q_A, Q_B = slice(176, 320), slice(176, 240), slice(240, 320)
    ls = (1 - l, l)

    def add(dst, rows, *terms):
        dst[rows] = sum([t.astype(F32) for t in terms], dst[rows].astype(F32)).astype(dst.dtype)

    def opposite(j):
        grad(xo * 2 + ls[j], g.at[0, j])
        copy(f"or{j}", g.at[0, j, P_A], rpo.at[0, j], right)
        copy(f"ol{j}", g.at[0, j, P_B], rpo.at[1, j, 0:80], left)

    def next_one(j):
        grad(xr * 2 + ls[j], g.at[1, j])
        copy(f"rr{j}", g.at[1, j, P_B], rpn.at[0, j, P_B], right)
        if j == 0:
            copy("q1", g.at[1, 0, Q_ROWS], ryq.at[1], pair)
        grad(xl * 2 + ls[j], g.at[2, j])
        copy(f"rl{j}", g.at[2, j, P_A], rpn.at[1, j, P_A], left)
        if j == 0:
            copy("q2", g.at[2, 0, Q_ROWS], ryq.at[2], pair)

    def pass_on(j):
        got(f"or{j}")
        add(g.at[1, j], P_A, rpo[0, j])
        copy(f"sr{j}", g.at[1, j, P_A], rpn.at[0, j, P_A], right)
        got(f"ol{j}")
        add(g.at[2, j], P_B, rpo[1, j, 0:80])
        copy(f"sl{j}", g.at[2, j, P_B], rpn.at[1, j, P_B], left)

    opposite(0)
    copy("q0", g.at[0, 0, Q_ROWS], ryq.at[0], pair)
    opposite(1)
    next_one(0)
    pass_on(0)
    next_one(1)
    got("q0")
    add(g.at[0, 1], Q_ROWS, ryq[0])
    copy("hor", g.at[0, 1, Q_A], rqo.at[0, 0:64], right)
    copy("hol", g.at[0, 1, Q_B], rqo.at[1], left)
    pass_on(1)

    loads["gen"].wait()
    loads["gate"].wait()

    def teacher():
        forward([(5 * CB, 3 * CB)], False, FB)

        @pl.loop(0, 8)
        def _(i):
            cols = pl.ds(pl.multiple_of(i * 256, 256), 256)
            m, r = mr[0:1, cols], mr[1:2, cols]
            for k in range(0, FB, 64):
                rows, more = slice(k, k + 64), slice(FB + k, FB + k + 64)
                own = pl.ds(pl.multiple_of(p * FB + k, 64), 64)

                def twice(ref, where):
                    return jnp.concatenate([ref[where], ref[where]], axis=1)

                fv = r * (acc[rows, cols] - twice(cs, rows) * m) + twice(bw, rows)
                tv = r * (acc[more, cols] - twice(cs, more) * m) + twice(bw, more)
                diff = sigma * (tv - fv)
                acc[more, cols] = diff
                away = jnp.abs(
                    sT[rows, cols].astype(F32) - (at[own, cols].astype(F32) - sigma * tv)
                )
                pushed = diff * gT[rows, cols].astype(F32)
                col[0, rows, :] += away[:, :128] + away[:, 128:]
                col[1, rows, :] += pushed[:, :128] + pushed[:, 128:]

    teacher()
    out_bc = pltpu.make_async_copy(acc.at[FB:CB], bc_out, loc_sems.at[13])
    out_bc.start()
    total = jnp.sum(jnp.sum(col[0], axis=0, keepdims=True), axis=1, keepdims=True)
    gap_s[0] = jnp.broadcast_to(total, (8, 128))
    gap_to = (across, on_f(yh, z + 1 - 2 * (z % 2), p), on_f(yh, 3 - z, p), sib)

    def gap_step(k):
        if k:
            got(f"gap{k - 1}")
            gap_s[k] = gap_s[k - 1] + gap_r[k - 1]
        copy(f"gap{k}", gap_s.at[k], gap_r.at[k], gap_to[k])

    gap_step(0)
    grad(x * 2 + ls[0], gown.at[0])
    g[3, 0, Q_ROWS] = gown[0, Q_ROWS].astype(BF16)
    copy("q3", g.at[3, 0, Q_ROWS], ryq.at[3], pair)
    got("q1", "hor")
    add(g.at[1, 1], Q_ROWS, ryq[1])
    add(g.at[1, 1], Q_A, rqo[0, 0:64])
    copy("hr", g.at[1, 1, Q_ROWS], rqn.at[0], right)
    gap_step(1)
    got("q2", "hol")
    add(g.at[2, 1], Q_ROWS, ryq[2])
    add(g.at[2, 1], Q_B, rqo[1])
    copy("hl", g.at[2, 1, Q_ROWS], rqn.at[1], left)
    gap_step(2)
    got("rr0", "sr0", "rl0", "sl0")
    g[3, 0, P_ROWS] = (
        gown[0, P_ROWS] + rpn[0, 0].astype(F32) + rpn[1, 0].astype(F32)
    ).astype(BF16)
    copy("py", g.at[3, 0, P_ROWS], rpy, pair)
    gap_step(3)
    grad(x * 2 + ls[1], gown.at[1])
    got("gap3")
    total = gap_s[3] + gap_r[3]
    weight = 1.0 / (total[0:1, 0:1] * (1.0 / (TOK * CLIPS * CB)) + EPS)

    same = eye(FB)
    gate_col = jnp.sum(same * gate[...], axis=1, keepdims=True) * weight
    col[0] = jnp.broadcast_to(gate_col, (FB, 128))
    gg_col = jnp.sum(col[1], axis=1, keepdims=True) * weight * (1.0 / math.sqrt(TOK))
    gg_out[...] = jnp.sum(same * gg_col, axis=0, keepdims=True)

    out_gc = pltpu.make_async_copy(col.at[0], gc_out, loc_sems.at[12])
    out_gc.start()

    got("rr1", "sr1", "rl1", "sl1")
    add(gown.at[1], P_ROWS, rpn[0, 1], rpn[1, 1])
    got("q3", "hr", "hl")
    add(gown.at[1], Q_ROWS, ryq[3], rqn[0], rqn[1])
    got("py")
    add(gown.at[1], P_ROWS, rpy[...])
    out_fg = pltpu.make_async_copy(gown.at[1], fg_out, loc_sems.at[14])
    out_fg.start()
    sent(*table)
    out_bc.wait()
    out_gc.wait()
    out_fg.wait()


def hand_over(
    diff, gate, gate_grad, grad, cot_out, gate_grad_out, grad_out, a, g, b, c, d, in_sems, out_sems
):
    pieces = [(gate, g, None), (gate_grad, b, gate_grad_out)]
    for k in range(0, FB, 80):
        rows = pl.ds(k, 80)
        pieces.append((diff.at[rows], a.at[rows], (d.at[rows], cot_out.at[rows], k)))
    pieces.append((grad, c, grad_out))
    first = [pltpu.make_async_copy(x, y, in_sems.at[i]) for i, (x, y, _) in enumerate(pieces)]
    for one in first:
        one.start()
    second = []
    for i, (_, y, z) in enumerate(pieces):
        first[i].wait()
        if z is None:
            continue
        if isinstance(z, tuple):
            y, z, k = z
            for r in range(k, k + 80, 16):
                d[r : r + 16, :] = (g[r : r + 16, 0:1] * a[r : r + 16, :]).astype(BF16)
        second.append(pltpu.make_async_copy(y, z, out_sems.at[i]))
        second[-1].start()
    for two in second:
        two.wait()


def per_device(
    sample, noise, gen_branch, step, teacher_mod, fake_mod, teacher_weight, fake_weight, gen_gate
):
    hbm = pl.BlockSpec(memory_space=pl.ANY)
    vmem = pl.BlockSpec(memory_space=pltpu.VMEM)
    diff, gate, gate_grad, grad = pl.pallas_call(
        kernel,
        out_shape=(
            jax.ShapeDtypeStruct((FB, TOK), F32),
            jax.ShapeDtypeStruct((FB, 128), F32),
            jax.ShapeDtypeStruct((1, FB), F32),
            jax.ShapeDtypeStruct((FB, CB), F32),
        ),
        in_specs=[
            hbm, hbm, hbm, pl.BlockSpec(memory_space=pltpu.SMEM), hbm, hbm, hbm, hbm, hbm,
        ],
        out_specs=(hbm, hbm, vmem, hbm),
        scratch_shapes=[
            pltpu.VMEM((CLIPS * CB, TOK), BF16),
            pltpu.VMEM((CB, CLIPS * CB), BF16),
            pltpu.VMEM((CB, TOK), F32),
            pltpu.VMEM((FB, TOK), BF16),
            pltpu.VMEM((FB, TOK), BF16),
            pltpu.VMEM((FB, TOK), BF16),
            pltpu.VMEM((FB, TOK), BF16),
            pltpu.VMEM((FB, TOK), F32),
            pltpu.VMEM((8, TOK), F32),
            pltpu.VMEM((8, TOK), F32),
            pltpu.VMEM((1, TOK), F32),
            pltpu.VMEM((2, TOK), F32),
            pltpu.VMEM((CB, 128), F32),
            pltpu.VMEM((CB, 128), F32),
            pltpu.VMEM((FB, 128), F32),
            pltpu.VMEM((FB, 128), F32),
            pltpu.VMEM((2, FB, 128), F32),
            pltpu.VMEM((2, CLIPS * CB), F32),
            pltpu.VMEM((2, CLIPS * CB), F32),
            pltpu.VMEM((1, FB), F32),
            pltpu.VMEM((4, 2, FB, CB), BF16),
            pltpu.VMEM((2, FB, CB), F32),
            pltpu.VMEM((2, 2, 96, CB), BF16),
            pltpu.VMEM((2, 2, 176, CB), BF16),
            pltpu.VMEM((4, 144, CB), BF16),
            pltpu.VMEM((2, 80, CB), BF16),
            pltpu.VMEM((2, 144, CB), BF16),
            pltpu.VMEM((176, CB), BF16),
            pltpu.VMEM((2, TOK), F32),
            pltpu.VMEM((2, TOK), F32),
            pltpu.VMEM((4, 8, 128), F32),
            pltpu.VMEM((4, 8, 128), F32),
            pltpu.SemaphoreType.DMA((COPIES,)),
            pltpu.SemaphoreType.DMA((COPIES,)),
            pltpu.SemaphoreType.DMA((15,)),
        ],
        compiler_params=pltpu.CompilerParams(
            collective_id=0, has_side_effects=True, vmem_limit_bytes=62 << 20
        ),
        name="step",
    )(
        sample.T, noise.T, gen_branch.T, step,
        teacher_mod.reshape(2, CLIPS * CB), fake_mod.reshape(2, CLIPS * CB),
        teacher_weight.T, fake_weight.T, gen_gate,
    )
    cot, gate_grad, grad = pl.pallas_call(
        hand_over,
        out_shape=(
            jax.ShapeDtypeStruct((FB, TOK), BF16),
            jax.ShapeDtypeStruct((1, FB), F32),
            jax.ShapeDtypeStruct((FB, CB), F32),
        ),
        in_specs=[hbm] * 4,
        out_specs=(hbm,) * 3,
        scratch_shapes=[
            pltpu.VMEM((FB, TOK), F32),
            pltpu.VMEM((FB, 128), F32),
            pltpu.VMEM((1, FB), F32),
            pltpu.VMEM((FB, CB), F32),
            pltpu.VMEM((FB, TOK), BF16),
            pltpu.SemaphoreType.DMA((7,)),
            pltpu.SemaphoreType.DMA((7,)),
        ],
        compiler_params=pltpu.CompilerParams(vmem_limit_bytes=60 << 20),
        name="hand_over",
    )(diff, gate, gate_grad, grad)
    return cot.T, gate_grad, grad.T


def solution(mesh):
    placed = (
        P("clip", "fsdp"),
        P("clip", "fsdp"),
        P("clip", "fsdp"),
        P("clip"),
        P("clip", None, None),
        P("clip", None, None),
        P("clip", "fsdp"),
        P("clip", "fsdp"),
        P("clip", "fsdp"),
    )
    return jax.shard_map(
        per_device,
        mesh=mesh,
        in_specs=placed,
        out_specs=(P("clip", "fsdp"), P("clip", "fsdp"), P("clip", "fsdp")),
        check_vma=False,
    )
```

```python
import functools
import math

import jax
import jax.numpy as jnp
from jax import lax
from jax.experimental import pallas as pl
from jax.experimental.pallas import tpu as pltpu
from jax.sharding import PartitionSpec as P

EPS = 1e-06
F32 = jnp.float32
BF16 = jnp.bfloat16
NT = (((1,), (1,)), ((), ()))

TOK = 2048
FB = 320
CB = 640
CLIPS = 8
COPIES = 80


def eye(n):
    same = lax.broadcasted_iota(jnp.int32, (n, n), 0) == lax.broadcasted_iota(jnp.int32, (n, n), 1)
    return same.astype(F32)


def kernel(
    sample, noise, gen, step, tmod_in, fmod_in, tw, fw, gate_in,
    bc_out, gc_out, gg_out, fg_out,
    at, wt, acc, sT, nT, gT, vv, bt, st1, st2, piv, mr, cs, bw, sv, sb, col,
    tmod, fmod, gate, g, gown, rpo, rpn, ryq, rqo, rqn, rpy, stat_s, stat_r, gap_s, gap_r,
    send_sems, recv_sems, loc_sems,
):
    clip = lax.axis_index("clip")
    fs = lax.axis_index("fsdp")
    x, l = clip // 2, clip % 2
    p, z, yh = fs % 2, (fs // 2) % 4, fs // 8
    s = 1 - 2 * p
    zu, zd, zo = (z + s + 4) % 4, (z - s + 4) % 4, (z + 2) % 4
    yo = 1 - yh
    xr, xl, xo = (x + 1) % 4, (x + 3) % 4, (x + 2) % 4

    def on_f(y, zz, pp):
        return {"fsdp": (y * 4 + zz) * 2 + pp}

    def on_c(xx, ll):
        return {"clip": xx * 2 + ll}

    up, dn, across, sib = on_f(yh, zu, p), on_f(yh, zd, p), on_f(yo, z, p), on_f(yh, z, 1 - p)
    right, left, pair = on_c(xr, l), on_c(xl, l), on_c(x, 1 - l)
    me, o, u, d, y_me, y_o, y_u, y_d = range(8)

    def slot(block):
        rel = ((block % 4 - z) * s + 8) % 4
        yd = (block // 4 + yh) % 2
        return yd * 4 + (rel % 2) * 2 + rel // 2

    table = {}

    def copy(name, src, dst, to):
        i = len(table)
        assert i < COPIES
        c = pltpu.make_async_remote_copy(
            src_ref=src, dst_ref=dst, send_sem=send_sems.at[i], recv_sem=recv_sems.at[i],
            device_id=to, device_id_type=pl.DeviceIdType.MESH,
        )
        table[name] = [c, False]
        c.start()

    def got(*names):
        for name in names:
            table[name][0].wait_recv()

    def sent(*names):
        for name in names:
            if not table[name][1]:
                table[name][1] = True
                table[name][0].wait_send()

    part = {
        "a": (pl.multiple_of(p * 512, 128), 128),
        "b": (pl.multiple_of(128 + p * 256, 128), 128),
        "c": (pl.multiple_of(256 + p * 64, 64), 64),
        "ab": (pl.multiple_of(p * 384, 128), 256),
        "all": (pl.multiple_of(p * 320, 64), 320),
    }

    def span(block, which):
        first, n = part[which]
        return pl.ds(pl.multiple_of(block * CB + first, 64), n)

    def send(name, here, there, which, to):
        copy(name, at.at[span(here, which), :], at.at[span(there, which), :], to)

    def w_ref(block, half):
        lanes = pl.ds(pl.multiple_of(slot(block) * CB, 128), CB)
        return wt.at[pl.ds(half * FB, FB), lanes]

    def send_w(name, block, half, to):
        copy(name, w_ref(block, half), w_ref(block, half), to)

    loads = {}

    def load(name, src, dst):
        loads[name] = pltpu.make_async_copy(src, dst, loc_sems.at[len(loads)])
        loads[name].start()

    def local(which):
        first, n = part[which]
        return pl.ds(pl.multiple_of(first - p * FB, 64), n)

    def load_part(which):
        load("s" + which, sample.at[local(which), :], sT.at[local(which), :])
        load("n" + which, noise.at[local(which), :], nT.at[local(which), :])

    load_part("a")
    barrier = pltpu.get_barrier_semaphore()
    for to in (up, dn, across, sib, right, left, pair):
        pl.semaphore_signal(barrier, inc=1, device_id=to, device_id_type=pl.DeviceIdType.MESH)
    load_part("b")
    load("fw", fw, w_ref(clip, 0))
    load("tw", tw, w_ref(clip, 1))
    load_part("c")

    frac = jnp.full((8, 128), step[0], jnp.int32).astype(F32) / 1000.0
    sigma = (5.0 * frac / (1.0 + 4.0 * frac))[0:1, 0:1]

    def noised(which):
        loads["s" + which].wait()
        loads["n" + which].wait()
        first, n = part[which]
        own = pl.multiple_of(first - p * FB, 64)

        @pl.loop(0, n // 32)
        def _(i):
            rows = pl.ds(pl.multiple_of(own + i * 32, 32), 32)
            mixed = (1.0 - sigma) * sT[rows, :].astype(F32) + sigma * nT[rows, :].astype(F32)
            at[pl.ds(pl.multiple_of(first + i * 32, 32), 32), :] = mixed.astype(BF16)

    noised("a")
    pl.semaphore_wait(barrier, 7)
    send("up_a", me, d, "a", up)
    noised("b")
    send("dn_b", me, u, "b", dn)
    loads["fw"].wait()
    send_w("pair_f", clip, 0, pair)
    loads["tw"].wait()
    send_w("pair_t", clip, 1, pair)
    send("y_ab", me, y_me, "ab", across)
    send_w("xr_f", clip, 0, right)
    send_w("xl_f", clip, 0, left)
    noised("c")
    send("up_c", me, d, "c", up)
    send("dn_a", me, u, "a", dn)
    send("y_c", me, y_me, "c", across)
    send("s_own", me, me, "all", sib)
    send_w("xr_t", clip, 1, right)
    send_w("xl_t", clip, 1, left)

    w_l, w_r, w_o = xl * 2 + l, xr * 2 + l, xo * 2 + l
    v_me, v_l, v_r, v_o = x * 2 + 1 - l, xl * 2 + 1 - l, xr * 2 + 1 - l, xo * 2 + 1 - l
    everyone = (clip, w_l, w_r, w_o, v_me, v_l, v_r, v_o)

    load("fmod", fmod_in, fmod)
    load("tmod", tmod_in, tmod)
    load("gen", gen, gT)
    load("gate", gate_in, gate)

    @pl.loop(0, 8)
    def _(i):
        cols = pl.ds(pl.multiple_of(i * 256, 256), 256)
        own = at[pl.ds(*part["all"]), cols].astype(F32)
        piv[:, cols] = jnp.sum(own, axis=0, keepdims=True) * (1.0 / FB)
        st1[:, cols] = jnp.zeros((8, 256), F32)
        st2[:, cols] = jnp.zeros((8, 256), F32)

    cs[...] = jnp.zeros_like(cs)
    bw[...] = jnp.zeros_like(bw)
    sv[...] = jnp.zeros_like(sv)
    sb[...] = jnp.zeros_like(sb)
    col[...] = jnp.zeros_like(col)

    def add_stats(first, n, cols):
        v = at[pl.ds(first, n), cols].astype(F32) - piv[:, cols]
        v = v.reshape(n // 8, 8, 256)
        st1[:, cols] += jnp.sum(v, axis=0)
        st2[:, cols] += jnp.sum(v * v, axis=0)

    def stats(block, which):
        first, n = part[which]

        @pl.loop(0, 8)
        def _(i):
            add_stats(pl.multiple_of(block * CB + first, 64), n, pl.ds(pl.multiple_of(i * 256, 256), 256))

    def scale(block, h, mod):
        lanes = pl.ds(pl.multiple_of(block * CB, 128), CB)
        factor = 1.0 + mod[1:2, lanes]
        shift = mod[0:1, lanes]
        held = pl.ds(pl.multiple_of(slot(block) * CB, 128), CB)

        @pl.loop(0, 5)
        def _(i):
            rows = pl.ds(pl.multiple_of(h * FB + i * 64, 64), 64)
            w = wt[rows, held].astype(F32)
            scaled = (w * factor).astype(BF16)
            wt[rows, held] = scaled
            back, moved = scaled.astype(F32), w * shift
            cs[rows, :] += sum(back[:, k : k + 128] for k in range(0, CB, 128))
            bw[rows, :] += sum(moved[:, k : k + 128] for k in range(0, CB, 128))

    def scale_all(h, mod):
        for block in everyone:
            scale(block, h, mod)
        rows = slice(h * FB, h * FB + FB)
        for ref in (cs, bw):
            ref[rows] = jnp.broadcast_to(jnp.sum(ref[rows], axis=1, keepdims=True), (FB, 128))

    def product(top, spans, cols):
        left_side = [wt[top : top + FB, i : i + n] for i, n in spans]
        right_side = [at[i : i + n, cols] for i, n in spans]
        return jnp.dot(
            jnp.concatenate(left_side, axis=1) if len(spans) > 1 else left_side[0],
            jnp.concatenate(right_side, axis=0) if len(spans) > 1 else right_side[0],
            preferred_element_type=F32,
        )

    def forward(spans, fresh=False, top=0):
        @pl.loop(0, 2)
        def _(i):
            cols = pl.ds(pl.multiple_of(i * 1024, 1024), 1024)
            if fresh:
                acc[top : top + FB, cols] = product(top, spans, cols)
            else:
                acc[top : top + FB, cols] += product(top, spans, cols)

    got("xr_f")
    send_w("xr_of", w_l, 0, right)
    got("up_a")
    send("up_oa", d, o, "a", up)
    got("dn_b")
    send("dn_ob", u, o, "b", dn)
    send("dn_c", me, u, "c", dn)
    got("pair_f")
    send_w("xr_vf", v_me, 0, right)
    send_w("xl_vf", v_me, 0, left)
    got("up_c")
    send("up_oc", d, o, "c", up)
    send("up_b", me, d, "b", up)
    got("pair_t")
    send_w("xr_vt", v_me, 1, right)
    stats(me, "all")
    got("xl_vf")
    send_w("xl_vof", v_r, 0, left)
    send_w("xl_vt", v_me, 1, left)
    got("xl_t")
    send_w("xl_ot", w_r, 1, left)
    got("up_oa")
    send("y_oa", o, y_o, "a", across)
    got("dn_ob")
    send("y_ob", o, y_o, "b", across)
    got("up_oc")
    send("y_oc", o, y_o, "c", across)
    send("s_o", o, o, "all", sib)
    got("xl_f", "xr_of", "xr_vf", "xl_vof")
    sent("xr_f", "xl_f", "pair_f", "xr_of", "xr_vf", "xl_vf", "xl_vof")
    loads["fmod"].wait()
    scale_all(0, fmod)
    got("y_ab")
    send("up_yab", y_me, y_d, "ab", up)
    send("dn_yab", y_me, y_u, "ab", dn)

    @pl.loop(0, 8)
    def _(i):
        cols = pl.ds(pl.multiple_of(i * 256, 256), 256)
        for k in range(0, FB, 64):
            rows = slice(k, k + 64)
            base = jnp.concatenate([bw[rows], bw[rows]], axis=1)
            target = nT[rows, cols].astype(F32) - sT[rows, cols].astype(F32)
            bt[rows, cols] = (base - target) * (1.0 / math.sqrt(CLIPS * TOK))

    got("s_own", "s_o")
    forward([(0, 2 * CB)], fresh=True)
    got("xr_vt")
    send_w("xr_vot", v_l, 1, right)
    got("dn_a", "dn_c")
    send("s_u", u, d, "all", sib)
    stats(o, "all")
    got("up_b")
    send("s_d", d, u, "all", sib)
    got("y_c")
    send("up_yc", y_me, y_d, "c", up)
    send("dn_yc", y_me, y_u, "c", dn)
    send("s_y", y_me, y_me, "all", sib)
    stats(u, "all")
    stats(d, "all")
    got("s_d", "s_u", "s_y")
    forward([(2 * CB, 3 * CB)])
    stats(y_me, "all")
    got("xr_t", "xl_ot", "xl_vt", "xr_vot")
    sent("xr_t", "xl_t", "pair_t", "xl_ot", "xr_vt", "xl_vt", "xr_vot")
    loads["tmod"].wait()
    scale_all(1, tmod)
    forward([(0, 5 * CB)], True, FB)
    got("dn_yab")
    send("s_yu", y_u, y_d, "ab", sib)
    got("up_yab")
    send("s_yd", y_d, y_u, "ab", sib)
    stats(y_u, "ab")
    stats(y_d, "ab")
    got("s_yd", "s_yu")
    forward([(b * CB + k, 256) for b in (y_u, y_d) for k in (0, 384)])
    got("y_oa", "y_ob")
    send("s_yo", y_o, y_o, "ab", sib)
    stats(y_o, "ab")

    held = 5 * FB + 3 * 256
    shift = jnp.sum(st1[...], axis=0, keepdims=True)
    stat_s[0:1, :] = piv[...] + shift * (1.0 / held)
    stat_s[1:2, :] = jnp.sum(st2[...], axis=0, keepdims=True) - shift * shift * (1.0 / held)
    copy("stat", stat_s, stat_r, sib)
    got("s_yo")
    forward([(y_o * CB + k, 256) for k in (0, 384)])
    got("stat")
    apart = stat_s[0:1, :] - stat_r[0:1, :]
    piv[...] = 0.5 * (stat_s[0:1, :] + stat_r[0:1, :])
    power_held = stat_s[1:2, :] + stat_r[1:2, :] + apart * apart * (held / 2)
    st1[...] = jnp.zeros_like(st1)
    st2[...] = jnp.broadcast_to(power_held * 0.125, st2.shape)

    got("dn_yc")
    send("s_yuc", y_u, y_d, "c", sib)
    got("up_yc")
    send("s_ydc", y_d, y_u, "c", sib)
    got("y_oc")
    send("s_yoc", y_o, y_o, "c", sib)
    got("s_yuc", "s_ydc", "s_yoc")

    last = [(b * CB + 256, 128) for b in (y_o, y_u, y_d)]

    @pl.loop(0, 8)
    def _(i):
        cols = pl.ds(pl.multiple_of(i * 256, 256), 256)
        acc[0:FB, cols] += product(0, last, cols)
        for first, n in last:
            add_stats(first, n, cols)
        shift = jnp.sum(st1[:, cols], axis=0, keepdims=True) * (1.0 / (CLIPS * CB))
        power = jnp.sum(st2[:, cols], axis=0, keepdims=True) * (1.0 / (CLIPS * CB))
        mr[0:1, cols] = piv[:, cols] + shift
        mr[1:2, cols] = lax.rsqrt(jnp.maximum(power - shift * shift, 0.0) + EPS)
        m, r = mr[0:1, cols], mr[1:2, cols]
        small = r * (1.0 / math.sqrt(CLIPS * TOK))
        for k in range(0, FB, 64):
            rows = slice(k, k + 64)
            sums = jnp.concatenate([cs[rows], cs[rows]], axis=1)
            err = small * (acc[rows, cols] - sums * m) + bt[rows, cols]
            v = (r * err).astype(BF16)
            vv[rows, cols] = v
            mv = m * v.astype(F32)
            sv[rows, :] += mv[:, :128] + mv[:, 128:]
            sb[rows, :] += err[:, :128] + err[:, 128:]

    sv[...] = jnp.broadcast_to(jnp.sum(sv[...], axis=1, keepdims=True), sv.shape)
    sb[...] = jnp.broadcast_to(jnp.sum(sb[...], axis=1, keepdims=True), sb.shape)

    def grad(block, dst, pieces=((0, 256), (256, 256), (512, 128))):
        held = slot(block) * CB
        for first, n in pieces:
            lanes = pl.ds(pl.multiple_of(block * CB + first, 128), n)
            rows = pl.ds(pl.multiple_of(held + first, 128), n)
            part_sum = lax.dot_general(vv[...], at[rows, :], NT, preferred_element_type=F32)
            g = (part_sum - sv[:, 0:1]) * (1.0 + fmod[1:2, lanes]) + sb[:, 0:1] * fmod[0:1, lanes]
            dst[:, first : first + n] = g.astype(dst.dtype)

    P_ROWS, P_A, P_B = slice(0, 176), slice(0, 96), slice(96, 176)
    Q_ROWS, Q_A, Q_B = slice(176, 320), slice(176, 240), slice(240, 320)
    ls = (1 - l, l)

    def add(dst, rows, *terms):
        dst[rows] = sum([t.astype(F32) for t in terms], dst[rows].astype(F32)).astype(dst.dtype)

    def opposite(j):
        grad(xo * 2 + ls[j], g.at[0, j])
        copy(f"or{j}", g.at[0, j, P_A], rpo.at[0, j], right)
        copy(f"ol{j}", g.at[0, j, P_B], rpo.at[1, j, 0:80], left)

    def next_one(j):
        grad(xr * 2 + ls[j], g.at[1, j])
        copy(f"rr{j}", g.at[1, j, P_B], rpn.at[0, j, P_B], right)
        if j == 0:
            copy("q1", g.at[1, 0, Q_ROWS], ryq.at[1], pair)
        grad(xl * 2 + ls[j], g.at[2, j])
        copy(f"rl{j}", g.at[2, j, P_A], rpn.at[1, j, P_A], left)
        if j == 0:
            copy("q2", g.at[2, 0, Q_ROWS], ryq.at[2], pair)

    def pass_on(j):
        got(*(("or00", "or01") if j == 0 else ("or1",)))
        add(g.at[1, j], P_A, rpo[0, j])
        copy(f"sr{j}", g.at[1, j, P_A], rpn.at[0, j, P_A], right)
        got(*(("ol00", "ol01") if j == 0 else ("ol1",)))
        add(g.at[2, j], P_B, rpo[1, j, 0:80])
        copy(f"sl{j}", g.at[2, j, P_B], rpn.at[1, j, P_B], left)

    for k, pieces in enumerate((((0, 256),), ((256, 256), (512, 128)))):
        grad(xo * 2 + ls[0], g.at[0, 0], pieces)
        lanes = slice(k * 256, CB if k else 256)
        copy(f"or0{k}", g.at[0, 0, P_A, lanes], rpo.at[0, 0, :, lanes], right)
        copy(f"ol0{k}", g.at[0, 0, P_B, lanes], rpo.at[1, 0, 0:80, lanes], left)
    copy("q0", g.at[0, 0, Q_ROWS], ryq.at[0], pair)
    opposite(1)
    next_one(0)
    pass_on(0)
    next_one(1)
    got("q0")
    add(g.at[0, 1], Q_ROWS, ryq[0])
    copy("hor", g.at[0, 1, Q_A], rqo.at[0, 0:64], right)
    copy("hol", g.at[0, 1, Q_B], rqo.at[1], left)
    pass_on(1)

    loads["gen"].wait()
    loads["gate"].wait()

    def teacher():
        forward([(5 * CB, 3 * CB)], False, FB)

        @pl.loop(0, 8)
        def _(i):
            cols = pl.ds(pl.multiple_of(i * 256, 256), 256)
            m, r = mr[0:1, cols], mr[1:2, cols]
            for k in range(0, FB, 64):
                rows, more = slice(k, k + 64), slice(FB + k, FB + k + 64)
                own = pl.ds(pl.multiple_of(p * FB + k, 64), 64)

                def twice(ref, where):
                    return jnp.concatenate([ref[where], ref[where]], axis=1)

                fv = r * (acc[rows, cols] - twice(cs, rows) * m) + twice(bw, rows)
                tv = r * (acc[more, cols] - twice(cs, more) * m) + twice(bw, more)
                diff = sigma * (tv - fv)
                acc[more, cols] = diff
                away = jnp.abs(
                    sT[rows, cols].astype(F32) - (at[own, cols].astype(F32) - sigma * tv)
                )
                pushed = diff * gT[rows, cols].astype(F32)
                col[0, rows, :] += away[:, :128] + away[:, 128:]
                col[1, rows, :] += pushed[:, :128] + pushed[:, 128:]

    teacher()
    out_bc = pltpu.make_async_copy(acc.at[FB:CB], bc_out, loc_sems.at[13])
    out_bc.start()
    total = jnp.sum(jnp.sum(col[0], axis=0, keepdims=True), axis=1, keepdims=True)
    gap_s[0] = jnp.broadcast_to(total, (8, 128))
    gap_to = (across, on_f(yh, z + 1 - 2 * (z % 2), p), on_f(yh, 3 - z, p), sib)

    def gap_step(k):
        if k:
            got(f"gap{k - 1}")
            gap_s[k] = gap_s[k - 1] + gap_r[k - 1]
        copy(f"gap{k}", gap_s.at[k], gap_r.at[k], gap_to[k])

    gap_step(0)
    grad(x * 2 + ls[0], gown.at[0])
    g[3, 0, Q_ROWS] = gown[0, Q_ROWS].astype(BF16)
    copy("q3", g.at[3, 0, Q_ROWS], ryq.at[3], pair)
    got("q1", "hor")
    add(g.at[1, 1], Q_ROWS, ryq[1])
    add(g.at[1, 1], Q_A, rqo[0, 0:64])
    copy("hr", g.at[1, 1, Q_ROWS], rqn.at[0], right)
    gap_step(1)
    got("q2", "hol")
    add(g.at[2, 1], Q_ROWS, ryq[2])
    add(g.at[2, 1], Q_B, rqo[1])
    copy("hl", g.at[2, 1, Q_ROWS], rqn.at[1], left)
    gap_step(2)
    got("rr0", "sr0", "rl0", "sl0")
    g[3, 0, P_ROWS] = (
        gown[0, P_ROWS] + rpn[0, 0].astype(F32) + rpn[1, 0].astype(F32)
    ).astype(BF16)
    copy("py", g.at[3, 0, P_ROWS], rpy, pair)
    gap_step(3)
    grad(x * 2 + ls[1], gown.at[1])
    got("gap3")
    total = gap_s[3] + gap_r[3]
    weight = 1.0 / (total[0:1, 0:1] * (1.0 / (TOK * CLIPS * CB)) + EPS)

    same = eye(FB)
    gate_col = jnp.sum(same * gate[...], axis=1, keepdims=True) * weight
    col[0] = jnp.broadcast_to(gate_col, (FB, 128))
    gg_col = jnp.sum(col[1], axis=1, keepdims=True) * weight * (1.0 / math.sqrt(TOK))
    gg_out[...] = jnp.sum(same * gg_col, axis=0, keepdims=True)

    out_gc = pltpu.make_async_copy(col.at[0], gc_out, loc_sems.at[12])
    out_gc.start()

    got("rr1", "sr1", "rl1", "sl1")
    add(gown.at[1], P_ROWS, rpn[0, 1], rpn[1, 1])
    got("q3", "hr", "hl")
    add(gown.at[1], Q_ROWS, ryq[3], rqn[0], rqn[1])
    got("py")
    add(gown.at[1], P_ROWS, rpy[...])
    out_fg = pltpu.make_async_copy(gown.at[1], fg_out, loc_sems.at[14])
    out_fg.start()
    sent(*table)
    out_bc.wait()
    out_gc.wait()
    out_fg.wait()


def hand_over(
    diff, gate, gate_grad, grad, cot_out, gate_grad_out, grad_out, a, g, b, c, d, in_sems, out_sems
):
    pieces = [(gate, g, None), (gate_grad, b, gate_grad_out)]
    for k in range(0, FB, 80):
        rows = pl.ds(k, 80)
        pieces.append((diff.at[rows], a.at[rows], (d.at[rows], cot_out.at[rows], k)))
    pieces.append((grad, c, grad_out))
    first = [pltpu.make_async_copy(x, y, in_sems.at[i]) for i, (x, y, _) in enumerate(pieces)]
    for one in first:
        one.start()
    second = []
    for i, (_, y, z) in enumerate(pieces):
        first[i].wait()
        if z is None:
            continue
        if isinstance(z, tuple):
            y, z, k = z
            for r in range(k, k + 80, 16):
                d[r : r + 16, :] = (g[r : r + 16, 0:1] * a[r : r + 16, :]).astype(BF16)
        second.append(pltpu.make_async_copy(y, z, out_sems.at[i]))
        second[-1].start()
    for two in second:
        two.wait()


def per_device(
    sample, noise, gen_branch, step, teacher_mod, fake_mod, teacher_weight, fake_weight, gen_gate
):
    hbm = pl.BlockSpec(memory_space=pl.ANY)
    vmem = pl.BlockSpec(memory_space=pltpu.VMEM)
    diff, gate, gate_grad, grad = pl.pallas_call(
        kernel,
        out_shape=(
            jax.ShapeDtypeStruct((FB, TOK), F32),
            jax.ShapeDtypeStruct((FB, 128), F32),
            jax.ShapeDtypeStruct((1, FB), F32),
            jax.ShapeDtypeStruct((FB, CB), F32),
        ),
        in_specs=[
            hbm, hbm, hbm, pl.BlockSpec(memory_space=pltpu.SMEM), hbm, hbm, hbm, hbm, hbm,
        ],
        out_specs=(hbm, hbm, vmem, hbm),
        scratch_shapes=[
            pltpu.VMEM((CLIPS * CB, TOK), BF16),
            pltpu.VMEM((CB, CLIPS * CB), BF16),
            pltpu.VMEM((CB, TOK), F32),
            pltpu.VMEM((FB, TOK), BF16),
            pltpu.VMEM((FB, TOK), BF16),
            pltpu.VMEM((FB, TOK), BF16),
            pltpu.VMEM((FB, TOK), BF16),
            pltpu.VMEM((FB, TOK), F32),
            pltpu.VMEM((8, TOK), F32),
            pltpu.VMEM((8, TOK), F32),
            pltpu.VMEM((1, TOK), F32),
            pltpu.VMEM((2, TOK), F32),
            pltpu.VMEM((CB, 128), F32),
            pltpu.VMEM((CB, 128), F32),
            pltpu.VMEM((FB, 128), F32),
            pltpu.VMEM((FB, 128), F32),
            pltpu.VMEM((2, FB, 128), F32),
            pltpu.VMEM((2, CLIPS * CB), F32),
            pltpu.VMEM((2, CLIPS * CB), F32),
            pltpu.VMEM((1, FB), F32),
            pltpu.VMEM((4, 2, FB, CB), BF16),
            pltpu.VMEM((2, FB, CB), F32),
            pltpu.VMEM((2, 2, 96, CB), BF16),
            pltpu.VMEM((2, 2, 176, CB), BF16),
            pltpu.VMEM((4, 144, CB), BF16),
            pltpu.VMEM((2, 80, CB), BF16),
            pltpu.VMEM((2, 144, CB), BF16),
            pltpu.VMEM((176, CB), BF16),
            pltpu.VMEM((2, TOK), F32),
            pltpu.VMEM((2, TOK), F32),
            pltpu.VMEM((4, 8, 128), F32),
            pltpu.VMEM((4, 8, 128), F32),
            pltpu.SemaphoreType.DMA((COPIES,)),
            pltpu.SemaphoreType.DMA((COPIES,)),
            pltpu.SemaphoreType.DMA((15,)),
        ],
        compiler_params=pltpu.CompilerParams(
            collective_id=0, has_side_effects=True, vmem_limit_bytes=62 << 20
        ),
        name="step",
    )(
        sample.T, noise.T, gen_branch.T, step,
        teacher_mod.reshape(2, CLIPS * CB), fake_mod.reshape(2, CLIPS * CB),
        teacher_weight.T, fake_weight.T, gen_gate,
    )
    cot, gate_grad, grad = pl.pallas_call(
        hand_over,
        out_shape=(
            jax.ShapeDtypeStruct((FB, TOK), BF16),
            jax.ShapeDtypeStruct((1, FB), F32),
            jax.ShapeDtypeStruct((FB, CB), F32),
        ),
        in_specs=[hbm] * 4,
        out_specs=(hbm,) * 3,
        scratch_shapes=[
            pltpu.VMEM((FB, TOK), F32),
            pltpu.VMEM((FB, 128), F32),
            pltpu.VMEM((1, FB), F32),
            pltpu.VMEM((FB, CB), F32),
            pltpu.VMEM((FB, TOK), BF16),
            pltpu.SemaphoreType.DMA((7,)),
            pltpu.SemaphoreType.DMA((7,)),
        ],
        compiler_params=pltpu.CompilerParams(vmem_limit_bytes=60 << 20),
        name="hand_over",
    )(diff, gate, gate_grad, grad)
    return cot.T, gate_grad, grad.T


def solution(mesh):
    placed = (
        P("clip", "fsdp"),
        P("clip", "fsdp"),
        P("clip", "fsdp"),
        P("clip"),
        P("clip", None, None),
        P("clip", None, None),
        P("clip", "fsdp"),
        P("clip", "fsdp"),
        P("clip", "fsdp"),
    )
    return jax.shard_map(
        per_device,
        mesh=mesh,
        in_specs=placed,
        out_specs=(P("clip", "fsdp"), P("clip", "fsdp"), P("clip", "fsdp")),
        check_vma=False,
    )
```
